32 devices in a mesh: dp: 4 (over z), fsdp: 8 (over y, x, core).
Axes of the slice: x: 2, y: 2, z: 4, core: 2. Of those that a mesh axis runs over, the one named last changes fastest.
Arguments:
- visual: bfloat16 [8, 288, 12, 768], P('dp', 'fsdp'), may hold values from -6 to 6
- query_slots: bfloat16 [8, 128, 768], P('dp', 'fsdp'), may hold values from -6 to 6
- lengths: int32 [8], P('dp'), may hold values from 1 to 128, as said below
- slot_order: int32 [8, 8], P('dp'), may hold values from 0 to 7, each once within a row
- norm_window: bfloat16 [768], P(('dp', 'fsdp')), may hold values from 0.099609375 to 1.8984375
- window_qkv: bfloat16 [768, 2304], P(('dp', 'fsdp')), may hold values from -0.21875 to 0.21875
- window_out: bfloat16 [768, 768], P(('dp', 'fsdp')), may hold values from -1.5 to 1.5
- norm_slots: bfloat16 [768], P(('dp', 'fsdp')), may hold values from 0.099609375 to 1.8984375
- slots_qkv: bfloat16 [768, 2304], P(('dp', 'fsdp')), may hold values from -0.21875 to 0.21875
- slots_out: bfloat16 [768, 768], P(('dp', 'fsdp')), may hold values from -0.875 to 0.875
- norm_reader: bfloat16 [768], P(('dp', 'fsdp')), may hold values from 0.099609375 to 1.8984375
- norm_page: bfloat16 [768], P(('dp', 'fsdp')), may hold values from 0.099609375 to 1.8984375
- reader_qkv: bfloat16 [768, 2304], P(('dp', 'fsdp')), may hold values from -0.21875 to 0.21875
- reader_out: bfloat16 [768, 768], P(('dp', 'fsdp')), may hold values from -6 to 6
- writer_qkv: bfloat16 [768, 2304], P(('dp', 'fsdp')), may hold values from -0.21875 to 0.21875
- writer_out: bfloat16 [768, 768], P(('dp', 'fsdp')), may hold values from -0.875 to 0.875
- norm_visual_mlp: bfloat16 [768], P(('dp', 'fsdp')), may hold values from 0.099609375 to 1.8984375
- visual_up: bfloat16 [768, 3072], P(('dp', 'fsdp')), may hold values from -0.21875 to 0.21875
- visual_down: bfloat16 [3072, 768], P(('dp', 'fsdp')), may hold values from -0.109375 to 0.109375
- norm_query_mlp: bfloat16 [768], P(('dp', 'fsdp')), may hold values from 0.099609375 to 1.8984375
- query_up: bfloat16 [768, 3072], P(('dp', 'fsdp')), may hold values from -0.21875 to 0.21875
- query_down: bfloat16 [3072, 768], P(('dp', 'fsdp')), may hold values from -0.109375 to 0.109375
- visual_cot: bfloat16 [8, 288, 12, 768], P('dp', 'fsdp'), may hold values from -6 to 6
- query_cot: bfloat16 [8, 128, 768], P('dp', 'fsdp'), may hold values from -6 to 6
Outputs:
- visual_out: bfloat16 [8, 288, 12, 768], P('dp', 'fsdp')
- query_out: bfloat16 [8, 128, 768], P('dp', 'fsdp')
- visual_grad: bfloat16 [8, 288, 12, 768], P('dp', 'fsdp')
- query_grad: bfloat16 [8, 128, 768], P('dp', 'fsdp')
- grad_norm_window: float32 [768], P(('dp', 'fsdp'))
- grad_window_qkv: float32 [768, 2304], P(('dp', 'fsdp'))
- grad_window_out: float32 [768, 768], P(('dp', 'fsdp'))
- grad_norm_slots: float32 [768], P(('dp', 'fsdp'))
- grad_slots_qkv: float32 [768, 2304], P(('dp', 'fsdp'))
- grad_slots_out: float32 [768, 768], P(('dp', 'fsdp'))
- grad_norm_reader: float32 [768], P(('dp', 'fsdp'))
- grad_norm_page: float32 [768], P(('dp', 'fsdp'))
- grad_reader_qkv: float32 [768, 2304], P(('dp', 'fsdp'))
- grad_reader_out: float32 [768, 768], P(('dp', 'fsdp'))
- grad_writer_qkv: float32 [768, 2304], P(('dp', 'fsdp'))
- grad_writer_out: float32 [768, 768], P(('dp', 'fsdp'))
- grad_norm_visual_mlp: float32 [768], P(('dp', 'fsdp'))
- grad_visual_up: float32 [768, 3072], P(('dp', 'fsdp'))
- grad_visual_down: float32 [3072, 768], P(('dp', 'fsdp'))
- grad_norm_query_mlp: float32 [768], P(('dp', 'fsdp'))
- grad_query_up: float32 [768, 3072], P(('dp', 'fsdp'))
- grad_query_down: float32 [3072, 768], P(('dp', 'fsdp'))
The draws below stay inside these ranges and needn't reach their ends.
Inputs may be any that keep to these rules, and one draw needn't show every extreme that they name: `lengths`: in each group of 2 consecutive pages one page has length 128; the others follow a heavy-tailed law.
All inputs are finite; a program needn't handle non-finite values.
Results may differ from the reference program's by a relative error of at most 0.025.
Values may be sent and summed in bfloat16 or wider, within the bound.
No kernel may reach another device: no remote copies, remote signals or barrier semaphores. Data moves between devices by JAX's collectives and lax.ppermute only.
A program may use at most 384 MiB of HBM per device.

```python
import jax
import jax.numpy as jnp
from jax import lax

D = 768
HEADS = 12
HEAD = 64
FF = 3072
WIN = 12
WCOLS = 8
Q_DEV = 16
MICRO = 2
PAGES = 8
BLOCKS = 8
ROWS = 36
COLS = 96
SLOTS = 128


def draw_lengths(key, part):
    key = jax.random.fold_in(key, 11)
    key_len, key_full = jax.random.split(key)
    drawn = jax.random.randint(key_len, (PAGES,), 0, SLOTS)
    tailed = 1 + drawn * drawn // SLOTS * drawn // SLOTS
    chosen = jax.random.randint(key_full, (PAGES // MICRO,), 0, MICRO)
    pages_all = jnp.arange(PAGES, dtype=jnp.int32)
    is_full = pages_all % MICRO == jnp.repeat(chosen, MICRO)
    return jnp.where(is_full, SLOTS, tailed).astype(jnp.int32)


def block_levels(rng, extent, cuts, least, high):
    factor_of, own = 1.0, jax.random.fold_in(rng, 6)
    for position, shards_of in cuts:
        draws = jnp.exp(jax.random.uniform(jax.random.fold_in(own, position), (shards_of,), jnp.float32, least / len(cuts), high / len(cuts)))
        factor_of = factor_of * jnp.repeat(draws, extent[position] // shards_of).reshape([-1 if axis == position else 1 for axis in range(len(extent))])
    return factor_of


def noise(rng, dims, deviation, most, pieces=(), kind=jnp.bfloat16):
    values = jax.random.normal(rng, dims, jnp.float32) * deviation
    if len(pieces) > 0:
        values = block_levels(rng, dims, pieces, -0.22, 0.18) * values
    return jnp.clip(values, min=-most, max=most).astype(kind)


def setup_inputs(seed: int = 0) -> dict:
    key_list = jax.random.split(jax.random.key(seed), 25)
    visual = noise(key_list[0], (PAGES, WCOLS * ROWS, WIN, D), 1.0, 6.0, ((0, 4), (1, 8)))
    query_slots = noise(key_list[1], (PAGES, SLOTS, D), 1.0, 6.0, ((0, 4), (1, 8)))
    lengths = draw_lengths(jax.random.fold_in(key_list[24], 71), 0)
    slot_order = jax.vmap(lambda own: jax.random.permutation(own, BLOCKS))(jax.random.split(key_list[3], PAGES)).reshape((PAGES, BLOCKS)).astype(jnp.int32)
    norm_window = jnp.clip(1.0 + 0.18 * jax.random.normal(key_list[4], (D,), jnp.float32), 0.099609375, 1.8984375).astype(jnp.bfloat16)
    window_qkv = noise(key_list[5], (D, 3 * D), D ** -0.5, 0.21875, ((0, 32),))
    window_out = noise(key_list[6], (D, D), (D // 48) ** -0.5, 1.5, ((0, 32),))
    norm_slots = jnp.clip(1.0 + 0.18 * jax.random.normal(key_list[7], (D,), jnp.float32), 0.099609375, 1.8984375).astype(jnp.bfloat16)
    slots_qkv = noise(key_list[8], (D, 3 * D), D ** -0.5, 0.21875, ((0, 32),))
    slots_out = noise(key_list[9], (D, D), (D // 16) ** -0.5, 0.875, ((0, 32),))
    norm_reader = jnp.clip(1.0 + 0.18 * jax.random.normal(key_list[10], (D,), jnp.float32), 0.099609375, 1.8984375).astype(jnp.bfloat16)
    norm_page = jnp.clip(1.0 + 0.18 * jax.random.normal(key_list[11], (D,), jnp.float32), 0.099609375, 1.8984375).astype(jnp.bfloat16)
    reader_qkv = noise(key_list[12], (D, 3 * D), D ** -0.5, 0.21875, ((0, 32),))
    reader_out = noise(key_list[13], (D, D), 1 ** -0.5, 6.0, ((0, 32),))
    writer_qkv = noise(key_list[14], (D, 3 * D), D ** -0.5, 0.21875, ((0, 32),))
    writer_out = noise(key_list[15], (D, D), (D // 16) ** -0.5, 0.875, ((0, 32),))
    norm_visual_mlp = jnp.clip(1.0 + 0.18 * jax.random.normal(key_list[16], (D,), jnp.float32), 0.099609375, 1.8984375).astype(jnp.bfloat16)
    visual_up = noise(key_list[17], (D, FF), D ** -0.5, 0.21875, ((0, 32),))
    visual_down = noise(key_list[18], (FF, D), FF ** -0.5, 0.109375, ((0, 32),))
    norm_query_mlp = jnp.clip(1.0 + 0.18 * jax.random.normal(key_list[19], (D,), jnp.float32), 0.099609375, 1.8984375).astype(jnp.bfloat16)
    query_up = noise(key_list[20], (D, FF), D ** -0.5, 0.21875, ((0, 32),))
    query_down = noise(key_list[21], (FF, D), FF ** -0.5, 0.109375, ((0, 32),))
    visual_cot = noise(key_list[22], (PAGES, WCOLS * ROWS, WIN, D), 1.0, 6.0, ((0, 4), (1, 8)))
    query_cot = noise(key_list[23], (PAGES, SLOTS, D), 1.0, 6.0, ((0, 4), (1, 8)))
    return dict(visual=visual, query_slots=query_slots, lengths=lengths, slot_order=slot_order, norm_window=norm_window, window_qkv=window_qkv, window_out=window_out, norm_slots=norm_slots, slots_qkv=slots_qkv, slots_out=slots_out, norm_reader=norm_reader, norm_page=norm_page, reader_qkv=reader_qkv, reader_out=reader_out, writer_qkv=writer_qkv, writer_out=writer_out, norm_visual_mlp=norm_visual_mlp, visual_up=visual_up, visual_down=visual_down, norm_query_mlp=norm_query_mlp, query_up=query_up, query_down=query_down, visual_cot=visual_cot, query_cot=query_cot)


@jax.custom_vjp
def low(v):
    return lax.optimization_barrier(v.astype(jnp.bfloat16)).astype(jnp.float32)

@jax.custom_vjp
def low_back(v):
    return v

def low_keep(v):
    return (low(v), None)

def low_pass(kept, grad):
    return (grad,)

def back_keep(v):
    return (v, None)

def back_low(kept, grad):
    return (low(grad),)
low.defvjp(low_keep, low_pass)
low_back.defvjp(back_keep, back_low)
precise = lax.Precision.HIGHEST

def rounded(tensor):
    return low(low_back(tensor))

def project(tensor, weight):
    return jnp.dot(tensor, weight, precision=precise)

def layer_norm(tensor, norm_gain):
    average = lax.optimization_barrier(jnp.mean(tensor, axis=-1, keepdims=True))
    centred = tensor - average
    spread = lax.optimization_barrier(jnp.mean(centred * centred, axis=-1, keepdims=True))
    return centred * lax.rsqrt(spread + 1e-05) * norm_gain

def attend(queries, key_rows, values, allowed):
    q_heads = queries.reshape(queries.shape[:-1] + (HEADS, HEAD))
    k_heads = key_rows.reshape(key_rows.shape[:-1] + (HEADS, HEAD))
    v_heads = values.reshape(values.shape[:-1] + (HEADS, HEAD))
    scores = low_back(jnp.einsum('...rhe,...khe->...hrk', q_heads, k_heads, precision=precise) * HEAD ** (-0.5))
    if allowed is not None:
        scores = jnp.where(allowed, scores, -1e+30)
    maximum = lax.optimization_barrier(jnp.max(scores, axis=-1, keepdims=True))
    powers = jnp.exp(scores - maximum)
    totals = lax.optimization_barrier(jnp.sum(powers, axis=-1))
    summed = jnp.einsum('...hrk,...khe->...rhe', low(powers), v_heads, precision=precise)
    result = summed / jnp.swapaxes(totals, -1, -2)[..., None]
    return result.reshape(queries.shape)

def partition(layout, height, across):
    tiles = layout.reshape((height // WIN, WIN, across // WIN, WIN) + layout.shape[2:])
    tiles = jnp.swapaxes(tiles, 1, 2)
    return tiles.reshape((height // WIN * (across // WIN), WIN * WIN) + layout.shape[2:])

def departition(tiles, height, across):
    layout = tiles.reshape((height // WIN, across // WIN, WIN, WIN) + tiles.shape[2:])
    layout = jnp.swapaxes(layout, 1, 2)
    return layout.reshape((height, across) + tiles.shape[2:])

def to_grid(bands):
    return jnp.swapaxes(bands.reshape(WCOLS, ROWS, WIN, D), 0, 1).reshape(ROWS, COLS, D)

def from_grid(layout):
    return jnp.swapaxes(layout.reshape(ROWS, WCOLS, WIN, D), 0, 1).reshape(WCOLS * ROWS, WIN, D)

def region_mask(rows_all, total_rows, total_cols):
    offset = WIN // 2
    cols_all = jnp.arange(total_cols, dtype=jnp.int32)
    row_band = (rows_all >= total_rows - WIN).astype(jnp.int32) + (rows_all >= total_rows - offset).astype(jnp.int32)
    col_band = (cols_all >= total_cols - WIN).astype(jnp.int32) + (cols_all >= total_cols - offset).astype(jnp.int32)
    labels = row_band[:, None] * 3 + col_band[None, :]
    tile_labels = partition(labels, rows_all.shape[0], total_cols)
    return (tile_labels[:, :, None] == tile_labels[:, None, :])[:, None]

def feed_forward(stream, norm_gain, up_weight, down_weight):
    normed = low(layer_norm(stream, norm_gain))
    upper = low_back(project(normed, up_weight))
    active = low(jax.nn.gelu(upper))
    return stream + low_back(project(active, down_weight))

def page_forward(visual_bands, slots, length, ordering, params):
    norm_window, window_qkv, window_out, norm_slots, slots_qkv, slots_out, norm_reader, norm_page, reader_qkv, reader_out, writer_qkv, writer_out, norm_visual_mlp, visual_up, visual_down, norm_query_mlp, query_up, query_down = params
    offset = WIN // 2
    visual = to_grid(visual_bands)
    normed = rounded(layer_norm(visual, norm_window))
    rolled = jnp.roll(normed, (-offset, -offset), axis=(0, 1))
    windows = partition(rolled, ROWS, COLS)
    mixture = rounded(project(windows, window_qkv))
    allowed = region_mask(jnp.arange(ROWS, dtype=jnp.int32), ROWS, COLS)
    attended = rounded(attend(mixture[..., :D], mixture[..., D:2 * D], mixture[..., 2 * D:], allowed))
    unrolled = jnp.roll(departition(attended, ROWS, COLS), (offset, offset), axis=(0, 1))
    visual_one = visual + low_back(project(unrolled, window_out))
    positions = (ordering[:, None] * Q_DEV + jnp.arange(Q_DEV, dtype=jnp.int32)[None, :]).reshape(SLOTS)
    live_keys = positions < length
    slot_norm = low(layer_norm(slots, norm_slots))
    slot_mix = rounded(project(slot_norm, slots_qkv))
    slot_heard = rounded(attend(slot_mix[:, :D], slot_mix[:, D:2 * D], slot_mix[:, 2 * D:], live_keys[None, None, :]))
    slots_one = slots + low_back(project(slot_heard, slots_out))
    reader_norm = low(layer_norm(slots_one, norm_reader))
    flat_one = visual_one.reshape(ROWS * COLS, D)
    page_norm = low(layer_norm(flat_one, norm_page))
    read_q = rounded(project(reader_norm, reader_qkv[:, :D]))
    read_kv = rounded(project(page_norm, reader_qkv[:, D:]))
    write_q = rounded(project(page_norm, writer_qkv[:, :D]))
    write_kv = rounded(project(reader_norm, writer_qkv[:, D:]))
    reading = attend(read_q, read_kv[:, :D], read_kv[:, D:], None)
    writing = rounded(attend(write_q, write_kv[:, :D], write_kv[:, D:], live_keys[None, None, :]))
    slots_two = slots_one + low_back(project(rounded(reading), reader_out))
    visual_two = flat_one + low_back(project(writing, writer_out))
    visual_three = feed_forward(visual_two, norm_visual_mlp, visual_up, visual_down)
    slots_three = feed_forward(slots_two, norm_query_mlp, query_up, query_down)
    return (from_grid(visual_three.reshape(ROWS, COLS, D)), slots_three)

def reference(visual, query_slots, lengths, slot_order, norm_window, window_qkv, window_out, norm_slots, slots_qkv, slots_out, norm_reader, norm_page, reader_qkv, reader_out, writer_qkv, writer_out, norm_visual_mlp, visual_up, visual_down, norm_query_mlp, query_up, query_down, visual_cot, query_cot):
    params = tuple((weight.astype(jnp.float32) for weight in (norm_window, window_qkv, window_out, norm_slots, slots_qkv, slots_out, norm_reader, norm_page, reader_qkv, reader_out, writer_qkv, writer_out, norm_visual_mlp, visual_up, visual_down, norm_query_mlp, query_up, query_down)))

    def forward(visual_all, slots_all, *weights):

        def one_page(page_items):
            return page_forward(page_items[0], page_items[1], page_items[2], page_items[3], weights)
        return lax.map(jax.checkpoint(one_page), (visual_all, slots_all, lengths, slot_order))
    outputs, pullback = jax.vjp(forward, visual.astype(jnp.float32), query_slots.astype(jnp.float32), *params)
    gradients = pullback((visual_cot.astype(jnp.float32), query_cot.astype(jnp.float32)))
    return (outputs[0].astype(jnp.bfloat16), outputs[1].astype(jnp.bfloat16), gradients[0].astype(jnp.bfloat16), gradients[1].astype(jnp.bfloat16), gradients[2], gradients[3], gradients[4], gradients[5], gradients[6], gradients[7], gradients[8], gradients[9], gradients[10], gradients[11], gradients[12], gradients[13], gradients[14], gradients[15], gradients[16], gradients[17], gradients[18], gradients[19])
```

```python
from functools import partial

import jax
import jax.numpy as jnp
from jax import lax
from jax.experimental import pallas as pl
from jax.experimental.pallas import tpu as pltpu
from jax.sharding import PartitionSpec as P

D = 768
HEADS = 12
HEAD = 64
WIN = 12
WCOLS = 8
Q_DEV = 16
MICRO = 2
PATCH = WIN * WIN
PAIRS = HEADS // 2
GROUPS = 4
GHEADS = HEADS // GROUPS
GCOLS = GHEADS * HEAD
SCALE = HEAD ** (-0.5)

bf = jnp.bfloat16
f32 = jnp.float32


def dot(a, b):
    return lax.dot_general(a, b, (((1,), (0,)), ((), ())), preferred_element_type=f32)


def dot_t(a, b):
    return lax.dot_general(a, b, (((1,), (1,)), ((), ())), preferred_element_type=f32)


def t_dot(a, b):
    return lax.dot_general(a, b, (((0,), (0,)), ((), ())), preferred_element_type=f32)


def normalise(x):
    centred = x - jnp.mean(x, axis=-1, keepdims=True)
    inv = lax.rsqrt(jnp.mean(centred * centred, axis=-1, keepdims=True) + 1e-05)
    return centred * inv, inv


def norm_back(grad, hat, inv, gain):
    scaled = grad * gain
    mean_one = jnp.mean(scaled, axis=-1, keepdims=True)
    mean_two = jnp.mean(scaled * hat, axis=-1, keepdims=True)
    return inv * (scaled - mean_one - hat * mean_two), jnp.sum(grad * hat, axis=0, keepdims=True)


def gelu_both(u):
    k = 0.7978845608028654
    t = jnp.tanh(k * (u + 0.044715 * u * u * u))
    slope = 0.5 * (1.0 + t) + 0.5 * u * (1.0 - t * t) * k * (1.0 + 3 * 0.044715 * u * u)
    return 0.5 * u * (1.0 + t), slope


def low_lanes(rows):
    return lax.broadcasted_iota(jnp.int32, (rows, 2 * HEAD), 1) < HEAD


def twofold(pair, mask):
    zero = jnp.zeros_like(pair)
    return jnp.concatenate([jnp.where(mask, pair, zero), jnp.where(mask, zero, pair)], axis=0)


def onefold(stacked, mask):
    rows = stacked.shape[0] // 2
    return jnp.where(mask, stacked[:rows], stacked[rows:])


def pair_forward(q2, k2, v2, bias):
    mask = low_lanes(q2.shape[0])
    s = dot_t(twofold(q2, mask), k2) * SCALE
    if bias is not None:
        s = s + bias
    m = jnp.max(s, axis=-1, keepdims=True)
    e = jnp.exp(s - m)
    l = jnp.sum(e, axis=-1, keepdims=True)
    out = dot(e.astype(bf), v2) / l
    return onefold(out, mask), m, l


def pair_backward(q2, k2, v2, d2, a2, bias, lse=None):
    mask = low_lanes(q2.shape[0])
    qs = twofold(q2, mask)
    ds = twofold(d2, mask)
    s = dot_t(qs, k2) * SCALE
    if bias is not None:
        s = s + bias
    if lse is None:
        e = jnp.exp(s - jnp.max(s, axis=-1, keepdims=True))
        p = e * (1.0 / jnp.sum(e, axis=-1, keepdims=True))
    else:
        p = jnp.exp(s - lse)
    corr = jnp.sum(ds.astype(f32) * twofold(a2, mask).astype(f32), axis=-1, keepdims=True)
    dp = dot_t(ds, v2)
    dsc = (p * (dp - corr)).astype(bf)
    dq = onefold(dot(dsc, k2), mask) * SCALE
    dk = t_dot(dsc, qs) * SCALE
    dv = t_dot(p.astype(bf), ds)
    return dq, dk, dv


def call(body, name, out_shape, in_specs, out_specs, grid, args, scratch=(), flops=0):
    return pl.pallas_call(
        body,
        name=name,
        out_shape=out_shape,
        grid=grid,
        in_specs=in_specs,
        out_specs=out_specs,
        scratch_shapes=scratch,
        compiler_params=pltpu.CompilerParams(vmem_limit_bytes=58 * 1024 * 1024),
        cost_estimate=pl.CostEstimate(flops=flops, bytes_accessed=1 << 20, transcendentals=0),
    )(*args)


def whole(shape):
    zeros = (0,) * len(shape)
    return pl.BlockSpec(shape, lambda *_: zeros, pipeline_mode=pl.Buffered(1))


def per_page(shape, axis):
    def place(p):
        return tuple(p if k == axis else 0 for k in range(len(shape)))

    return pl.BlockSpec(shape, place)


def sds(shape, dtype):
    return jax.ShapeDtypeStruct(shape, dtype)


def window_fwd(x_ref, bias_ref, gw_ref, gp_ref, w_ref, mix_ref, att_ref, v1_ref, pk_ref):
    rows = x_ref.shape[0]
    x = x_ref[...].astype(f32)
    xn = (normalise(x)[0] * gw_ref[...]).astype(bf)
    for u in range(3):
        mix_ref[u] = dot(xn, w_ref[3 + u]).astype(bf)

    def window(w, carry):
        at = pl.ds(pl.multiple_of(w * PATCH, 16), PATCH)
        bias = bias_ref[w]
        bias = jnp.concatenate([bias, bias], axis=0)
        for p in range(PAIRS):
            c = slice(p * 128, p * 128 + 128)
            out = pair_forward(mix_ref[0, at, c], mix_ref[1, at, c], mix_ref[2, at, c], bias)[0]
            att_ref[at, c] = out.astype(bf)
        return carry

    lax.fori_loop(0, rows // PATCH, window, 0)
    v1 = x_ref[...].astype(f32) + dot(att_ref[...], w_ref[6])
    v1_ref[...] = v1
    pn = (normalise(v1)[0] * gp_ref[...]).astype(bf)
    for u in range(3):
        pk_ref[u] = dot(pn, w_ref[u]).astype(bf)


def read_fwd(rq_ref, k_ref, v_ref, o_ref, lse_ref):
    slots = rq_ref.shape[1]
    lane = lax.broadcasted_iota(jnp.int32, (slots, 128), 1)
    acc = jnp.zeros((slots, 128), f32)
    for p in range(PAIRS):
        c = slice(p * 128, p * 128 + 128)
        out, m, l = pair_forward(rq_ref[0, :, c], k_ref[0, :, c], v_ref[0, :, c], None)
        o_ref[0, :, c] = out
        lse = m + jnp.log(l)
        acc = jnp.where(lane == 2 * p, lse[:slots], acc)
        acc = jnp.where(lane == 2 * p + 1, lse[slots:], acc)
    lse_ref[0] = acc


def write_fwd(v1_ref, wq_ref, wk_ref, wv_ref, bias_ref, wo_ref, wr_ref, v2_ref):
    for p in range(PAIRS):
        c = slice(p * 128, p * 128 + 128)
        out = pair_forward(wq_ref[0, :, c], wk_ref[0, :, c], wv_ref[0, :, c], bias_ref[0])[0]
        wr_ref[:, c] = out.astype(bf)
    v2_ref[...] = v1_ref[...] + dot(wr_ref[...], wo_ref[0])


def mlp_both(
    steps,
    R,
    core_ref,
    x_ref,
    g_ref,
    up_ref,
    down_ref,
    cot_ref,
    out_ref,
    dx_ref,
    keep_up_ref,
    give_up_ref,
    keep_down_ref,
    give_down_ref,
    dg_ref,
    xn_ref,
    y_ref,
    dxn_ref,
    tall_ref,
):
    j = pl.program_id(0)
    core = core_ref[0]
    chunk = up_ref.shape[-1]

    @pl.when(j == 0)
    def _():
        xn_ref[...] = (normalise(x_ref[...])[0] * g_ref[...]).astype(bf)

    xn = xn_ref[...]
    cot = cot_ref[...]
    up = up_ref[0]
    if R:
        chips = chunk // (4 * R)
        pieces = [down_ref[u // 2, u % 2, i] for i in range(chips) for u in range(4)]
        down = jnp.concatenate(pieces, axis=0)
    else:
        down = down_ref[...]
    act, slope = gelu_both(dot(xn, up))
    act = act.astype(bf)
    y = dot(act, down)
    dpre = (dot_t(cot, down) * slope).astype(bf)
    dxn = dot_t(dpre, up)
    dup = t_dot(xn, dpre).astype(bf)

    @pl.when(j // (steps // 2) == core)
    def _():
        keep_up_ref[0] = dup

    @pl.when(j // (steps // 2) != core)
    def _():
        give_up_ref[0] = dup

    if R:
        tall_ref[...] = t_dot(act, cot).astype(bf)
        for i in range(chips):
            for k in range(2):
                keep_down_ref[k, i] = tall_ref[pl.ds(pl.multiple_of((4 * i + k + 2 * core) * R, R), R), :]
                give_down_ref[k, i] = tall_ref[pl.ds(pl.multiple_of((4 * i + k + 2 - 2 * core) * R, R), R), :]
    else:
        keep_down_ref[...] = t_dot(act, cot).astype(bf)

    @pl.when(j == 0)
    def _():
        y_ref[...] = y
        dxn_ref[...] = dxn

    @pl.when(j > 0)
    def _():
        y_ref[...] += y
        dxn_ref[...] += dxn

    @pl.when(j == steps - 1)
    def _():
        x = x_ref[...]
        out_ref[...] = (x + y_ref[...]).astype(bf)
        hat, inv = normalise(x)
        dx, dg = norm_back(dxn_ref[...], hat, inv, g_ref[...])
        dx_ref[...] = cot_ref[...].astype(f32) + dx
        dg_ref[...] = dg


def write_bwd(dv2_ref, wr_ref, wq_ref, wk_ref, wv_ref, bias_ref, wo_ref, dwq_ref, dwk_ref, dwv_ref, dwo_ref, acc_ref):
    page = pl.program_id(0)
    d = dv2_ref[...].astype(bf)
    dwr = dot_t(d, wo_ref[0]).astype(bf)
    part = t_dot(wr_ref[...], d)

    @pl.when(page == 0)
    def _():
        acc_ref[...] = part

    @pl.when(page > 0)
    def _():
        acc_ref[...] += part

    dwo_ref[...] = acc_ref[...].astype(bf)
    for p in range(PAIRS):
        c = slice(p * 128, p * 128 + 128)
        dq, dk, dv = pair_backward(
            wq_ref[0, :, c], wk_ref[0, :, c], wv_ref[0, :, c], dwr[:, c], wr_ref[:, c], bias_ref[0]
        )
        dwq_ref[:, c] = dq.astype(bf)
        dwk_ref[0, :, c] = dk.astype(bf)
        dwv_ref[0, :, c] = dv.astype(bf)


def read_bwd(rq_ref, k_ref, v_ref, d_ref, r_ref, lse_ref, dq_ref, dk_ref, dv_ref):
    slots = rq_ref.shape[1]
    lse = lse_ref[0]
    for p in range(PAIRS):
        c = slice(p * 128, p * 128 + 128)
        both = jnp.concatenate([lse[:, 2 * p : 2 * p + 1], lse[:, 2 * p + 1 : 2 * p + 2]], axis=0)
        dq, dk, dv = pair_backward(
            rq_ref[0, :, c], k_ref[0, :, c], v_ref[0, :, c], d_ref[0, :, c], r_ref[0, :, c], None, both
        )
        dq_ref[0, :, c] = dq.astype(bf)
        dk_ref[:, c] = dk.astype(bf)
        dv_ref[:, c] = dv.astype(bf)


def page_bwd(
    core_ref,
    v1_ref,
    dv2_ref,
    dk_ref,
    dv_ref,
    dwq_ref,
    gp_ref,
    wp_ref,
    dwo_ref,
    dv1_ref,
    keep_ref,
    give_ref,
    dg_ref,
    acc_ref,
    gacc_ref,
):
    page = pl.program_id(0)
    hat, inv = normalise(v1_ref[...])
    pn = (hat * gp_ref[...]).astype(bf)
    grads = (dk_ref, dv_ref, dwq_ref)
    dpn = dot_t(dk_ref[...], wp_ref[0]) + dot_t(dv_ref[...], wp_ref[1]) + dot_t(dwq_ref[...], wp_ref[2])
    dx, dg = norm_back(dpn, hat, inv, gp_ref[...])
    dv1_ref[...] = dv2_ref[...] + dx

    @pl.when(page == 0)
    def _():
        gacc_ref[...] = dg
        for u in range(3):
            acc_ref[u] = t_dot(pn, grads[u][...])

    @pl.when(page > 0)
    def _():
        gacc_ref[...] += dg
        for u in range(3):
            acc_ref[u] += t_dot(pn, grads[u][...])

    @pl.when(page == pl.num_programs(0) - 1)
    def _():
        dg_ref[...] = gacc_ref[...]

    def split(first_ref, second_ref):
        first_ref[...] = acc_ref[:2].astype(bf)
        second_ref[0] = acc_ref[2].astype(bf)
        second_ref[1] = dwo_ref[...]

    @pl.when((page == pl.num_programs(0) - 1) & (core_ref[0] == 0))
    def _():
        split(keep_ref, give_ref)

    @pl.when((page == pl.num_programs(0) - 1) & (core_ref[0] == 1))
    def _():
        split(give_ref, keep_ref)


def window_bwd(
    core_ref,
    dv1_ref,
    x_ref,
    mix_ref,
    att_ref,
    bias_ref,
    gw_ref,
    w_ref,
    dmix_ref,
    keep_ref,
    give_ref,
    acc_ref,
    datt_ref,
):
    page = pl.program_id(0)
    rows = x_ref.shape[0]
    d1b = dv1_ref[...].astype(bf)
    datt_ref[...] = dot_t(d1b, w_ref[6]).astype(bf)

    def window(w, carry):
        at = pl.ds(pl.multiple_of(w * PATCH, 16), PATCH)
        bias = bias_ref[w]
        bias = jnp.concatenate([bias, bias], axis=0)
        for p in range(PAIRS):
            c = slice(p * 128, p * 128 + 128)
            dq, dk, dv = pair_backward(
                mix_ref[0, at, c], mix_ref[1, at, c], mix_ref[2, at, c], datt_ref[at, c], att_ref[at, c], bias
            )
            dmix_ref[0, at, c] = dq.astype(bf)
            dmix_ref[1, at, c] = dk.astype(bf)
            dmix_ref[2, at, c] = dv.astype(bf)
        return carry

    lax.fori_loop(0, rows // PATCH, window, 0)
    xn = (normalise(x_ref[...].astype(f32))[0] * gw_ref[...]).astype(bf)

    @pl.when(page == 0)
    def _():
        for u in range(3):
            acc_ref[u] = t_dot(xn, dmix_ref[u])
        acc_ref[3] = t_dot(att_ref[...], d1b)

    @pl.when(page > 0)
    def _():
        for u in range(3):
            acc_ref[u] += t_dot(xn, dmix_ref[u])
        acc_ref[3] += t_dot(att_ref[...], d1b)

    def split(first_ref, second_ref):
        first_ref[...] = acc_ref[:2].astype(bf)
        second_ref[...] = acc_ref[2:].astype(bf)

    @pl.when((page == pl.num_programs(0) - 1) & (core_ref[0] == 0))
    def _():
        split(keep_ref, give_ref)

    @pl.when((page == pl.num_programs(0) - 1) & (core_ref[0] == 1))
    def _():
        split(give_ref, keep_ref)


def window_end(dv1_ref, x_ref, dmix_ref, gw_ref, w_ref, grad_ref, dg_ref, gacc_ref):
    page = pl.program_id(0)
    hat, inv = normalise(x_ref[...].astype(f32))
    dxn = dot_t(dmix_ref[0], w_ref[3]) + dot_t(dmix_ref[1], w_ref[4]) + dot_t(dmix_ref[2], w_ref[5])
    dx, dg = norm_back(dxn.astype(bf).astype(f32), hat, inv, gw_ref[...])
    grad_ref[...] = (dv1_ref[...] + dx).astype(bf)

    @pl.when(page == 0)
    def _():
        gacc_ref[...] = dg

    @pl.when(page > 0)
    def _():
        gacc_ref[...] += dg

    dg_ref[...] = gacc_ref[...]


def head_cols(part, h):
    return slice(part * GCOLS + h * HEAD, part * GCOLS + (h + 1) * HEAD)


def slots_fwd(x_ref, g_ref, w_ref, bias_ref, mix_ref, att_ref):
    xn = (normalise(x_ref[...].astype(f32))[0] * g_ref[...]).astype(bf)
    mix_ref[...] = dot(xn, w_ref[...]).astype(bf)
    outs = []
    for h in range(GHEADS):
        s = dot_t(mix_ref[:, head_cols(0, h)], mix_ref[:, head_cols(1, h)]) * SCALE + bias_ref[...]
        e = jnp.exp(s - jnp.max(s, axis=-1, keepdims=True))
        l = jnp.sum(e, axis=-1, keepdims=True)
        outs.append(dot(e.astype(bf), mix_ref[:, head_cols(2, h)]) / l)
    att_ref[...] = jnp.concatenate(outs, axis=-1).astype(bf)


def slots_mid(x_ref, att_ref, wo_ref, g_ref, w_ref, s1_ref, out_ref):
    s1 = x_ref[...].astype(f32) + dot(att_ref[...], wo_ref[0])
    s1_ref[...] = s1
    rn = (normalise(s1)[0] * g_ref[...]).astype(bf)
    out_ref[...] = dot(rn, w_ref[...]).astype(bf)


def query_mlp(s1_ref, read_ref, wo_ref, g_ref, up_ref, down_ref, cot_ref, s2_ref, part_ref, dup_ref, ddown_ref):
    s2 = s1_ref[...] + dot(read_ref[...], wo_ref[0])
    s2_ref[...] = s2
    xn = (normalise(s2)[0] * g_ref[...]).astype(bf)
    act, slope = gelu_both(dot(xn, up_ref[...]))
    act = act.astype(bf)
    part_ref[0] = dot(act, down_ref[...]).astype(bf)
    cot = cot_ref[...]
    dpre = (dot_t(cot, down_ref[...]) * slope).astype(bf)
    part_ref[1] = dot_t(dpre, up_ref[...]).astype(bf)
    dup_ref[...] = t_dot(xn, dpre).astype(bf)
    ddown_ref[...] = t_dot(act, cot).astype(bf)


def query_back(s2_ref, sum_ref, cot_ref, g_ref, wo_ref, out_ref, ds2_ref, dread_ref, dg_ref):
    s2 = s2_ref[...]
    out_ref[...] = (s2 + sum_ref[0].astype(f32)).astype(bf)
    hat, inv = normalise(s2)
    dx, dg = norm_back(sum_ref[1].astype(f32), hat, inv, g_ref[...])
    ds2 = cot_ref[...].astype(f32) + dx
    ds2_ref[...] = ds2
    dg_ref[...] = dg
    dread_ref[...] = dot_t(ds2.astype(bf), wo_ref[0]).astype(bf)


def reader_back(s1_ref, g_ref, w_ref, d_ref, part_ref, dw_ref):
    rn = (normalise(s1_ref[...])[0] * g_ref[...]).astype(bf)
    part_ref[...] = dot_t(d_ref[...], w_ref[...]).astype(bf)
    dw_ref[...] = t_dot(rn, d_ref[...]).astype(bf)


def slots_back(x_ref, s1_ref, ds2_ref, drn_ref, gr_ref, wo_ref, mix_ref, att_ref, bias_ref, gs_ref, w_ref, ds1_ref, part_ref, dw_ref, dg_ref):
    hat, inv = normalise(s1_ref[...])
    dx, dg = norm_back(drn_ref[...].astype(f32), hat, inv, gr_ref[...])
    dg_ref[...] = dg
    ds1 = ds2_ref[...] + dx
    ds1_ref[...] = ds1
    datt = dot_t(ds1.astype(bf), wo_ref[0]).astype(bf)
    att = att_ref[...]
    grads = [[], [], []]
    for h in range(GHEADS):
        q, k, v = (mix_ref[:, head_cols(part, h)] for part in range(3))
        d = datt[:, head_cols(0, h)]
        s = dot_t(q, k) * SCALE + bias_ref[...]
        e = jnp.exp(s - jnp.max(s, axis=-1, keepdims=True))
        p = e * (1.0 / jnp.sum(e, axis=-1, keepdims=True))
        corr = jnp.sum(d.astype(f32) * att[:, head_cols(0, h)].astype(f32), axis=-1, keepdims=True)
        dsc = (p * (dot_t(d, v) - corr)).astype(bf)
        grads[0].append(dot(dsc, k) * SCALE)
        grads[1].append(t_dot(dsc, q) * SCALE)
        grads[2].append(t_dot(p.astype(bf), d))
    dmix = jnp.concatenate(grads[0] + grads[1] + grads[2], axis=-1).astype(bf)
    part_ref[...] = dot_t(dmix, w_ref[...]).astype(bf)
    xn = (normalise(x_ref[...].astype(f32))[0] * gs_ref[...]).astype(bf)
    dw_ref[...] = t_dot(xn, dmix).astype(bf)


def slots_end(x_ref, g_ref, dxn_ref, ds1_ref, out_ref, dg_ref):
    hat, inv = normalise(x_ref[...].astype(f32))
    dx, dg = norm_back(dxn_ref[...].astype(f32), hat, inv, g_ref[...])
    out_ref[...] = (ds1_ref[...] + dx).astype(bf)
    dg_ref[...] = dg


def simple(body, name, args, outs):
    arrays = [a[0] if isinstance(a, tuple) else a for a in args]
    specs = [a[1] if isinstance(a, tuple) else whole(a.shape) for a in args]
    return call(
        body,
        name,
        tuple(sds(*o) for o in outs),
        specs,
        tuple(whole(o[0]) for o in outs),
        (1,),
        arrays,
        flops=1 << 30,
    )


def place_units(place, mine, other, n, R):
    nz, half = mine[0].shape[0], n // 2
    table = jnp.stack([place.core, place.chip % 4]).astype(jnp.int32)

    def body(table_ref, *refs):
        pieces, out_ref, sem = refs[:8], refs[8], refs[9]
        core, chip = table_ref[0], table_ref[1]
        copies = []
        for whose in range(2):
            owner = jnp.bitwise_xor(core, whose)
            for i in range(4):
                mask = jnp.where(owner == 0, i, (0, 2, 1, 3)[i])
                at = jnp.bitwise_xor(chip, mask)
                for u in range(half):
                    copy = pltpu.make_async_copy(
                        pieces[4 * whose + i].at[:, pl.ds(u * R, R)], out_ref.at[owner * half + u, :, at], sem.at[len(copies)]
                    )
                    copy.start()
                    copies.append(copy)
        for copy in copies:
            copy.wait()

    out = pl.pallas_call(
        body,
        name="place_units",
        out_shape=jax.ShapeDtypeStruct((n, nz, 4, R, D), bf),
        in_specs=[pl.BlockSpec(memory_space=pltpu.SMEM)] + [pl.BlockSpec(memory_space=pl.ANY)] * 8,
        out_specs=pl.BlockSpec(memory_space=pltpu.VMEM),
        scratch_shapes=[pltpu.SemaphoreType.DMA((8 * half,))],
        compiler_params=pltpu.CompilerParams(vmem_limit_bytes=58 * 1024 * 1024),
        cost_estimate=pl.CostEstimate(flops=0, bytes_accessed=n * D * D * 4, transcendentals=0),
    )(table, *mine, *other)
    return out.reshape(n, D, D)


def pick(stack, index, axis=0):
    return lax.dynamic_index_in_dim(stack, index, axis, keepdims=False)


def ordered(first, mine, other):
    return jnp.stack([jnp.where(first, mine, other), jnp.where(first, other, mine)])


class Place:
    def __init__(self):
        self.nz = lax.axis_size("dp")
        self.nf = lax.axis_size("fsdp")
        self.nq = self.nf // 2
        self.z = lax.axis_index("dp")
        self.f = lax.axis_index("fsdp")
        self.core = self.f % 2
        self.even = self.core == 0
        self.chip = self.f // 2
        self.group = self.chip % GROUPS

    def sibling(self, x):
        return lax.ppermute(x, "fsdp", [(f, f ^ 1) for f in range(self.nf)])

    def hop(self, x, mask, odd_mask=None):
        odd_mask = mask if odd_mask is None else odd_mask
        route = [(f, f ^ ((odd_mask if f % 2 else mask) << 1)) for f in range(self.nf)]
        return lax.ppermute(x, "fsdp", route)

    def along(self, x):
        route = []
        for z in range(self.nz):
            for f in range(self.nf):
                to = z + 1 if f % 2 == 0 else z - 1
                inside = 0 <= to < self.nz
                route.append((z * self.nf + f, to * self.nf + f if inside else z * self.nf + (f ^ 1)))
        return lax.ppermute(x, ("dp", "fsdp"), route)

    def gather_line(self, block, half):
        def part(x, which):
            return jnp.concatenate([lax.dynamic_slice_in_dim(x, which * half, half, 0), x[2 * half :]])

        got, now = [], block
        for _ in range(self.nz - 1):
            now = self.along(now)
            got.append(now)
        other = self.sibling(jnp.stack([part(x, 1 - self.core) for x in got]))
        row = jnp.concatenate([jnp.stack([part(x, self.core) for x in got + [block]]), other])
        out = []
        for z in range(self.nz):
            steps = jnp.abs(self.z - z)
            passed = jnp.where(self.even, z < self.z, z > self.z)
            at = jnp.where(passed, steps - 1, self.nz + steps - 1)
            out.append(pick(row, jnp.where(steps == 0, self.nz - 1, at)))
        return jnp.stack(out)

    def gather_square(self, block, bit):
        a, b = 1 << bit, 2 << bit
        first = self.hop(block, a, b)
        second = self.hop(block, b, a)
        return [block, first, second, self.hop(first, b, a)]

    def reduce_square(self, parts, bit):
        a, b = 1 << bit, 2 << bit
        here = (self.chip >> bit) % 4
        first = jnp.where(self.even, 1, 2)
        second = self.hop(parts(here ^ (3 - first)).astype(bf), b, a)
        corner = self.hop(parts(here ^ 3).astype(bf), b, a)
        moving = (parts(here ^ first) + corner.astype(f32)).astype(bf)
        first = self.hop(moving, a, b)
        return (parts(here) + first.astype(f32) + second.astype(f32)).astype(bf)

    def arranged(self, pieces, bit, odd):
        here = (self.chip >> bit) % 4
        stack = jnp.stack(pieces)
        at = [0, 1, 2, 3]
        swapped = jnp.where(odd, jnp.array([0, 2, 1, 3]), jnp.array(at))
        return jnp.stack([pick(stack, swapped[here ^ k]) for k in at])

    def gather_chips(self, now, n, R):
        half = n // 2
        bits = range(0, self.nq.bit_length() - 1, 2)
        for bit in bits[:-1]:
            now = self.arranged(self.gather_square(now, bit), bit, ~self.even)
            now = jnp.moveaxis(now, 0, -3)
        bit = bits[-1]
        mine = self.gather_square(now, bit)
        other = [self.sibling(piece) for piece in mine]
        more = self.arranged([piece[..., half * R :, :] for piece in mine], bit, ~self.even)
        more = jnp.moveaxis(more, 1, -3).reshape(self.nq, self.nz, -1, D)
        if R % 16 == 0 and len(bits) == 1:
            return place_units(self, mine, other, n, R), more
        mine = self.arranged([piece[..., : half * R, :] for piece in mine], bit, ~self.even)
        other = self.arranged([piece[..., : half * R, :] for piece in other], bit, self.even)
        units = ordered(self.even, mine, other)
        units = units.reshape((2, 4, self.nz, -1, half, R, D))
        units = jnp.transpose(units, (0, 4, 2, 1, 3, 5, 6))
        return units.reshape(n, D, D), more

    def scatter_whole(self, pairs):
        R = D // (self.nz * self.nq)
        others = [self.sibling(give) for _, give in pairs]
        bits = range(0, self.nq.bit_length() - 1, 2)

        def parts(i):
            blocks = []
            for (keep, _), other in zip(pairs, others):
                shape = (keep.shape[0], self.nz, 4, -1, R, D)
                block = pick(keep.reshape(shape), i, 2).astype(f32) + pick(other.reshape(shape), i, 2).astype(f32)
                blocks.append(jnp.swapaxes(block, 0, 1))
            return jnp.concatenate(blocks, axis=1)

        now = self.reduce_square(parts, bits[-1])
        for bit in reversed(bits[:-1]):
            whole_now = now.reshape(now.shape[:2] + (4, -1, R, D))
            now = self.reduce_square(lambda i: pick(whole_now, i, 2).astype(f32), bit)
        now = now.reshape(self.nz, -1, D)
        return lax.psum_scatter(now, "dp", scatter_dimension=0, tiled=False).reshape(-1, R, D)

    def gather_groups(self, x):
        out = x[None]
        for bit in range(2):
            got = self.hop(out, 1 << bit)
            upper = (self.chip >> bit) % 2 == 1
            out = jnp.concatenate([jnp.where(upper, got, out), jnp.where(upper, out, got)])
        return out

    def sum_groups(self, x):
        x = x + self.hop(x, 1, 2)
        return x + self.hop(x, 2, 1)

    def to_groups(self, blocks, combine):
        def at(mask):
            return jax.tree.map(lambda leaf: pick(leaf, self.group ^ mask), blocks)

        first = jnp.where(self.even, 1, 2)
        second = 3 - first
        pairs = jax.tree.map(lambda *leaves: jnp.stack(leaves), at(second), at(3))
        pairs = combine(jax.tree.map(lambda *leaves: jnp.stack(leaves), at(0), at(first)), pairs, (2, 1))
        out = combine(
            jax.tree.map(lambda leaf: leaf[0], pairs), jax.tree.map(lambda leaf: leaf[1], pairs), (1, 2)
        )
        bit = 2
        while (1 << bit) < self.nq:
            out = combine(out, out, (1 << bit, 1 << bit))
            bit += 1
        return out

    def owned_rows(self, mine, axis=0):
        own = lax.dynamic_slice_in_dim(mine, self.f * Q_DEV, Q_DEV, axis)
        give = lax.dynamic_slice_in_dim(mine, (self.f ^ 1) * Q_DEV, Q_DEV, axis)
        return ordered(self.even, own, self.sibling(give))


def split_three(x):
    hi = lax.reduce_precision(x, 8, 7)
    mid = lax.reduce_precision(x - hi, 8, 7)
    return [hi.astype(bf), mid.astype(bf), (x - hi - mid).astype(bf)]


def join_three(x):
    a, b, c = jnp.split(x.astype(f32), 3, axis=-1)
    return (a + b) + c


def columns(weight):
    rows, width = weight.shape
    return [weight[:, k * D : (k + 1) * D] for k in range(width // D)]


def strip_bias(place, bands, height):
    half = WIN // 2
    rows = (place.f % bands) * height + jnp.arange(height, dtype=jnp.int32)
    cols = (place.f // bands) * WIN + jnp.arange(WIN, dtype=jnp.int32)

    def label(at, total):
        return (at >= total - WIN).astype(jnp.int32) + (at >= total - half).astype(jnp.int32)

    labels = label(rows, height * bands)[:, None] * 3 + label(cols, WIN * WCOLS)
    labels = labels.reshape(height // WIN, PATCH)
    return jnp.where(labels[:, :, None] == labels[:, None, :], 0.0, -1e30).astype(f32)


def roll_in(x, place, bands):
    half = WIN // 2
    below = x[:, :half]
    if bands > 1:
        route = [(f // bands * bands + (f + 1) % bands, f) for f in range(place.nf)]
        below = lax.ppermute(below, "fsdp", route)
    x = jnp.concatenate([x[:, half:], below], axis=1)
    beside = lax.ppermute(x[:, :, :half], "fsdp", [((f + bands) % place.nf, f) for f in range(place.nf)])
    return jnp.concatenate([x[:, :, half:], beside], axis=2)


def roll_out(x, place, bands):
    half = WIN // 2
    beside = lax.ppermute(x[:, :, half:], "fsdp", [(f, (f + bands) % place.nf) for f in range(place.nf)])
    x = jnp.concatenate([beside, x[:, :, :half]], axis=2)
    above = x[:, -half:]
    if bands > 1:
        route = [(f, f // bands * bands + (f + 1) % bands) for f in range(place.nf)]
        above = lax.ppermute(above, "fsdp", route)
    return jnp.concatenate([above, x[:, :-half]], axis=1)


def local(
    visual,
    query_slots,
    lengths,
    slot_order,
    norm_window,
    window_qkv,
    window_out,
    norm_slots,
    slots_qkv,
    slots_out,
    norm_reader,
    norm_page,
    reader_qkv,
    reader_out,
    writer_qkv,
    writer_out,
    norm_visual_mlp,
    visual_up,
    visual_down,
    norm_query_mlp,
    query_up,
    query_down,
    visual_cot,
    query_cot,
):
    place = Place()
    nz, nf, nq, core, even = place.nz, place.nf, place.nq, place.core, place.even
    extra = nq // GROUPS
    bands = nf // WCOLS
    height = visual.shape[1]
    page_rows = height * WIN
    rows = MICRO * page_rows
    slots = Q_DEV * nf
    r = window_out.shape[0]
    R = 2 * r

    def chip_half(units):
        half = len(units) // 2
        flat = jnp.stack(units).reshape(2, half, r, D)
        got = place.sibling(pick(flat, 1 - core))
        both = ordered(even, pick(flat, core), got)
        return jnp.swapaxes(both, 0, 1).reshape(half, R, D)

    gains = jnp.stack([norm_window, norm_slots, norm_reader, norm_page, norm_visual_mlp, norm_query_mlp])
    gain_rows = jnp.zeros((8, D), bf).at[:6, :r].set(gains)
    units = columns(reader_qkv)[1:] + columns(writer_qkv)[:1] + columns(window_qkv)
    units = units + [window_out, writer_out, slots_out, reader_out]
    flat = jnp.concatenate(units + [gain_rows])
    other = place.sibling(flat)
    n = len(units)
    main = ordered(even, flat[: n * r], other[: n * r]).reshape(2, n, r, D)
    block = jnp.concatenate(
        [jnp.swapaxes(main, 0, 1).reshape(n * R, D), ordered(even, flat[n * r :], other[n * r :]).reshape(16, D)]
    )
    w_one, gain_all = place.gather_chips(place.gather_line(block, n // 2 * R), n, R)
    gain_all = gain_all.reshape(nq, nz, 2, 8, D)[:, :, :, :6, :r]
    gain_all = jnp.transpose(gain_all, (3, 1, 0, 2, 4)).reshape(6, 1, D).astype(f32)
    g_window, g_slots, g_reader, g_page, g_vmlp, g_qmlp = (gain_all[k] for k in range(6))
    one_unit = (1, D, D)

    def unit(u):
        return w_one, pl.BlockSpec(one_unit, lambda *_: (u, 0, 0), pipeline_mode=pl.Buffered(1))

    up = jnp.stack(columns(visual_up)).reshape(2, 2, r, D)
    up = ordered(even, pick(up, core), place.sibling(pick(up, 1 - core)))
    up = jnp.swapaxes(up, 0, 1).reshape(2 * R, D)
    now = lax.all_gather(jnp.concatenate([up, visual_down]), "dp")
    w_two = place.gather_chips(now, 8, R)[0]
    direct = R if R % 16 == 0 else 0

    def group_cols(weight):
        wide = weight.reshape(weight.shape[0], -1, GROUPS, GCOLS)
        return jnp.swapaxes(wide, 1, 2).reshape(weight.shape[0], GROUPS, -1)

    def hidden_cols(weight):
        wide = weight.reshape(weight.shape[0], nz, extra, GROUPS, 4 * D // (nz * nq))
        return jnp.transpose(wide, (0, 3, 1, 2, 4)).reshape(weight.shape[0], GROUPS, D)

    by_group = jnp.concatenate(
        [
            group_cols(slots_qkv),
            group_cols(reader_qkv[:, :D]),
            group_cols(writer_qkv[:, D:]),
            hidden_cols(query_up),
        ],
        axis=-1,
    )
    by_group = jnp.swapaxes(by_group, 0, 1)
    arrived = [pick(by_group, place.group)]
    for mask in range(1, nq):
        arrived.append(place.hop(pick(by_group, place.group ^ (mask % GROUPS)), mask))
    arrived = jnp.stack(arrived)
    arrived = jnp.stack([pick(arrived, place.chip ^ k) for k in range(nq)])
    width = arrived.shape[-1]
    downs = [query_down]
    for mask in range(GROUPS, nq, GROUPS):
        downs.append(place.hop(query_down, mask))
    downs = jnp.stack(downs)
    downs = jnp.stack([pick(downs, (place.chip // GROUPS) ^ k) for k in range(extra)])

    def col_half(x, which):
        half = x.shape[-1] // 2
        return lax.dynamic_slice_in_dim(x, which * half, half, x.ndim - 1)

    got = place.sibling(
        jnp.concatenate([col_half(arrived, 1 - core).reshape(nq * r, -1), col_half(downs, 1 - core).reshape(nq * r, -1)], axis=1)
    )
    cols = ordered(even, col_half(arrived, core), got[:, : width // 2].reshape(nq, r, -1))
    cols = jnp.swapaxes(cols, 0, 1).reshape(nq * R, -1)
    downs = ordered(even, col_half(downs, core), got[:, width // 2 :].reshape(extra, 2 * R, -1))
    downs = jnp.swapaxes(downs, 0, 1).reshape(nq * R, -1)
    mine = lax.all_gather(jnp.concatenate([cols, downs], axis=1), "dp").reshape(D, -1)
    other = place.sibling(mine)
    one, two = jnp.where(even, mine, other), jnp.where(even, other, mine)
    w_cols = jnp.concatenate([one[:, : width // 2], two[:, : width // 2]], axis=1)
    w_qdown = jnp.concatenate([one[:, width // 2 :], two[:, width // 2 :]], axis=1)
    w_sq, w_rd, w_qup = w_cols[:, : 3 * GCOLS], w_cols[:, 3 * GCOLS : 6 * GCOLS], w_cols[:, 6 * GCOLS :]

    ends = jnp.stack([query_slots, query_cot])
    give = pick(ends, 1 - core, 1)
    ends = ordered(even, pick(ends, core, 1), place.sibling(give))
    ends = jnp.swapaxes(ends, 0, 1).reshape(2, 2 * Q_DEV, D)
    bit = 0
    while (1 << bit) < nq:
        got = place.hop(ends, 1 << bit)
        upper = (place.chip >> bit) % 2 == 1
        ends = jnp.concatenate([jnp.where(upper, got, ends), jnp.where(upper, ends, got)], axis=1)
        bit += 1
    xs, xs_cot = ends[0], ends[1]

    bias = strip_bias(place, bands, height)
    x = roll_in(visual, place, bands).reshape(rows, D)
    cot = roll_in(visual_cot, place, bands).reshape(rows, D)

    positions = (slot_order[:, :, None] * Q_DEV + jnp.arange(Q_DEV, dtype=jnp.int32)).reshape(MICRO, slots)
    live = jnp.where(positions < lengths[:, None], 0.0, -1e30).astype(f32).reshape(MICRO, 1, slots)
    own_live = pick(live, core)

    mix_q, att_own = simple(
        slots_fwd, "slots_fwd", (xs, g_slots, w_sq, own_live), [((slots, 3 * GCOLS), bf), ((slots, GCOLS), bf)]
    )
    att_q = jnp.swapaxes(place.gather_groups(att_own), 0, 1).reshape(slots, D)
    s1, rd_own = simple(
        slots_mid, "slots_mid", (xs, att_q, unit(8), g_reader, w_rd), [((slots, D), f32), ((slots, 3 * GCOLS), bf)]
    )
    rd_page = place.gather_groups(rd_own)
    rd = ordered(even, rd_page, place.sibling(rd_page)).reshape(MICRO, GROUPS, slots, 3, GCOLS)
    rd = jnp.transpose(rd, (3, 0, 2, 1, 4)).reshape(3, MICRO, slots, D)
    rq, wk, wv = rd[0], rd[1], rd[2]

    act_block = per_page((page_rows, D), 0)
    mix, att, v1, pk = call(
        window_fwd,
        "window_fwd",
        (sds((3, rows, D), bf), sds((rows, D), bf), sds((rows, D), f32), sds((3, rows, D), bf)),
        [
            act_block,
            whole(bias.shape),
            whole((1, D)),
            whole((1, D)),
            whole((7, D, D)),
        ],
        (per_page((3, page_rows, D), 1), act_block, act_block, per_page((3, page_rows, D), 1)),
        (MICRO,),
        (x, bias, g_window, g_page, w_one),
        flops=2 * rows * 7 * D * D,
    )
    slot_block = per_page((1, slots, D), 0)
    stat_block = per_page((1, slots, 128), 0)

    def of_pk(u):
        return pl.BlockSpec((1, page_rows, D), lambda p: (u, p, 0))

    o_part, lse_part = call(
        read_fwd,
        "read_fwd",
        (sds((MICRO, slots, D), f32), sds((MICRO, slots, 128), f32)),
        [slot_block, of_pk(0), of_pk(1)],
        (slot_block, stat_block),
        (MICRO,),
        (rq, pk, pk),
        flops=2 * rows * slots * D * 4,
    )

    def merge(kept, sent, route):
        o, lse = kept
        message = jnp.concatenate(sent, axis=-1)
        got = place.sibling(message) if route is None else place.hop(message, *route)
        width = o.shape[-1]
        o_two, lse_two = got[..., :width], got[..., width:]
        top = jnp.maximum(lse, lse_two)
        a, b = jnp.exp(lse - top), jnp.exp(lse_two - top)
        share = jnp.repeat(a / (a + b), HEAD, axis=-1)
        return o * share + o_two * (1.0 - share), top + jnp.log(a + b)

    heads_part = lse_part[..., :HEADS]
    page_o, page_lse = merge(
        (pick(o_part, core), pick(heads_part, core)), (pick(o_part, 1 - core), pick(heads_part, 1 - core)), None
    )
    blocks = (
        jnp.swapaxes(page_o.reshape(slots, GROUPS, GCOLS), 0, 1),
        jnp.swapaxes(page_lse.reshape(slots, GROUPS, GHEADS), 0, 1),
    )
    reading, lse_own = place.to_groups(blocks, merge)
    message = jnp.concatenate([reading.astype(bf)] + split_three(lse_own), axis=-1)
    message = place.gather_groups(message)
    read_q = jnp.swapaxes(message[..., :GCOLS], 0, 1).reshape(slots, D)
    lse_page = jnp.swapaxes(join_three(message[..., GCOLS:]), 0, 1).reshape(slots, HEADS)

    s2, parts, d_qup, d_qdown = simple(
        query_mlp,
        "query_mlp",
        (s1, read_q, unit(9), g_qmlp, w_qup, w_qdown, xs_cot),
        [((slots, D), f32), ((2, slots, D), bf), ((D, D), bf), ((D, D), bf)],
    )
    sums = place.sum_groups(parts)
    q_out, ds2, d_read, dg_qmlp = simple(
        query_back,
        "query_back",
        (s2, sums, xs_cot, g_qmlp, unit(9)),
        [((slots, D), bf), ((slots, D), f32), ((slots, D), bf), ((1, D), f32)],
    )
    query_out = place.owned_rows(q_out)
    message = jnp.concatenate([d_read, read_q] + split_three(lse_page), axis=-1)
    message = ordered(even, message, place.sibling(message))
    d_read_all, read_all = message[..., :D], message[..., D : 2 * D]
    lse_all = jnp.pad(join_three(message[..., 2 * D :]), ((0, 0), (0, 0), (0, 128 - HEADS)))

    live_block = per_page((1, 1, slots), 0)
    writing, v2 = call(
        write_fwd,
        "write_fwd",
        (sds((rows, D), bf), sds((rows, D), f32)),
        [act_block, of_pk(2), slot_block, slot_block, live_block, unit(7)[1]],
        (act_block, act_block),
        (MICRO,),
        (v1, pk, wk, wv, live, w_one),
        flops=2 * rows * D * D,
    )
    chunk = 384
    steps = 4 * D // chunk
    per_unit = D // chunk
    flat_block = whole((rows, D))
    half_steps = steps // 2
    chips = max(chunk // (4 * R), 1)

    def once(*shape):
        return pl.BlockSpec(shape, lambda j, c: (0,) * len(shape), pipeline_mode=pl.Buffered(1))

    def up_at(j):
        u = j // per_unit
        return (u + u // 2 * 2, 0, j % per_unit)

    def half_at(half):
        def place_of(j, c):
            k = jnp.clip(j - half_steps * (c[0] if half == 0 else 1 - c[0]), 0, half_steps - 1)
            return (k // per_unit, 0, k % per_unit)

        return pl.BlockSpec((1, D, chunk), place_of)

    if direct:
        w_down = w_two.reshape(2, 4, nz * nq, R, D)
        down_block = pl.BlockSpec((2, 2, chips, R, D), lambda j, c: (0, 1, j, 0, 0))
        d_down_block = pl.BlockSpec((2, chips, R, D), lambda j, c: (0, j, 0, 0))
        d_down_shapes = [sds((2, nz * nq, R, D), bf)] * 2
    else:
        w_down = w_two.reshape(2, 2, 2, nz, nq, R, D)[:, 1]
        w_down = jnp.transpose(w_down, (2, 3, 0, 1, 4, 5)).reshape(4 * D, D)
        down_block = d_down_block = pl.BlockSpec((chunk, D), lambda j, c: (j, 0))
        d_down_shapes = [sds((4 * D, D), bf)] * 2
    core_id = core.astype(jnp.int32).reshape(1)
    v3, dv2, keep_up, give_up, keep_down, give_down, dg_vmlp = pl.pallas_call(
        partial(mlp_both, steps, direct),
        name="mlp_both",
        out_shape=(sds((rows, D), bf), sds((rows, D), f32), sds((2, D, D), bf), sds((2, D, D), bf))
        + tuple(d_down_shapes)
        + (sds((1, D), f32),),
        grid_spec=pltpu.PrefetchScalarGridSpec(
            num_scalar_prefetch=1,
            grid=(steps,),
            in_specs=[
                once(rows, D),
                once(1, D),
                pl.BlockSpec((1, D, chunk), lambda j, c: up_at(j)),
                down_block,
                once(rows, D),
            ],
            out_specs=(
                once(rows, D),
                once(rows, D),
                half_at(0),
                half_at(1),
                d_down_block,
                d_down_block,
                once(1, D),
            ),
            scratch_shapes=(
                pltpu.VMEM((rows, D), bf),
                pltpu.VMEM((rows, D), f32),
                pltpu.VMEM((rows, D), f32),
                pltpu.VMEM((chunk, D), bf),
            ),
        ),
        compiler_params=pltpu.CompilerParams(vmem_limit_bytes=58 * 1024 * 1024),
        cost_estimate=pl.CostEstimate(flops=2 * rows * 24 * D * D, bytes_accessed=1 << 24, transcendentals=0),
    )(core_id, v2, g_vmlp, w_two, w_down, cot)
    if not direct:
        units_down = jnp.transpose(keep_down.reshape(nz, nq, 2, 2, R, D), (2, 3, 0, 1, 4, 5))
        keep_down, give_down = pick(units_down, core), pick(units_down, 1 - core)
    keep_down, give_down = keep_down.reshape(2, D, D), give_down.reshape(2, D, D)
    mlp_pairs = [(keep_up, give_up), (keep_down, give_down)]
    visual_out = roll_out(v3.reshape(MICRO, height, WIN, D), place, bands)
    dwq, dwk, dwv, d_wo = call(
        write_bwd,
        "write_bwd",
        (sds((rows, D), bf), sds((MICRO, slots, D), bf), sds((MICRO, slots, D), bf), sds((D, D), bf)),
        [act_block, act_block, of_pk(2), slot_block, slot_block, live_block, unit(7)[1]],
        (act_block, slot_block, slot_block, whole((D, D))),
        (MICRO,),
        (dv2, writing, pk, wk, wv, live, w_one),
        scratch=(pltpu.VMEM((D, D), f32),),
        flops=4 * rows * D * D,
    )

    drq, dk, dv = call(
        read_bwd,
        "read_bwd",
        (sds((MICRO, slots, D), bf), sds((rows, D), bf), sds((rows, D), bf)),
        [slot_block, of_pk(0), of_pk(1), slot_block, slot_block, stat_block],
        (slot_block, act_block, act_block),
        (MICRO,),
        (rq, pk, pk, d_read_all, read_all, lse_all),
        flops=2 * rows * slots * D * 10,
    )
    core_block = pl.BlockSpec(memory_space=pltpu.SMEM)
    two_units = whole((2, D, D))
    dv1, keep_page, give_page, dg_page = call(
        page_bwd,
        "page_bwd",
        (sds((rows, D), f32), sds((2, D, D), bf), sds((2, D, D), bf), sds((1, D), f32)),
        [core_block]
        + [act_block, act_block, act_block, act_block, act_block, whole((1, D)), whole((3, D, D)), whole((D, D))],
        (act_block, two_units, two_units, whole((1, D))),
        (MICRO,),
        (core_id, v1, dv2, dk, dv, dwq, g_page, w_one, d_wo),
        scratch=(pltpu.VMEM((3, D, D), f32), pltpu.VMEM((1, D), f32)),
        flops=2 * rows * 6 * D * D,
    )
    three_block = per_page((3, page_rows, D), 1)
    dmix, keep_window, give_window = call(
        window_bwd,
        "window_bwd",
        (sds((3, rows, D), bf), sds((2, D, D), bf), sds((2, D, D), bf)),
        [core_block, act_block, act_block, three_block, act_block, whole(bias.shape), whole((1, D)), whole((7, D, D))],
        (three_block, two_units, two_units),
        (MICRO,),
        (core_id, dv1, x, mix, att, bias, g_window, w_one),
        scratch=(pltpu.VMEM((4, D, D), f32), pltpu.VMEM((page_rows, D), bf)),
        flops=2 * rows * 5 * D * D,
    )
    v_grad, dg_window = call(
        window_end,
        "window_end",
        (sds((rows, D), bf), sds((1, D), f32)),
        [act_block, act_block, three_block, whole((1, D)), whole((7, D, D))],
        (act_block, whole((1, D))),
        (MICRO,),
        (dv1, x, dmix, g_window, w_one),
        scratch=(pltpu.VMEM((1, D), f32),),
        flops=2 * rows * 3 * D * D,
    )
    visual_grad = roll_out(v_grad.reshape(MICRO, height, WIN, D), place, bands)

    def add(kept, sent, route):
        got = place.sibling(sent) if route is None else place.hop(sent, *route)
        return (kept.astype(f32) + got.astype(f32)).astype(bf)

    d_slots = jnp.stack([drq, dwk, dwv], axis=2)
    d_slots = add(pick(d_slots, core), pick(d_slots, 1 - core), None)
    d_slots = jnp.transpose(d_slots.reshape(slots, 3, GROUPS, GCOLS), (2, 0, 1, 3))
    d_rd = place.to_groups(d_slots.reshape(GROUPS, slots, 3 * GCOLS), add)
    part, d_rdw = simple(
        reader_back, "reader_back", (s1, g_reader, w_rd, d_rd), [((slots, D), bf), ((D, 3 * GCOLS), bf)]
    )
    drn = place.sum_groups(part)
    w_so_rows = lax.dynamic_slice(w_one, (8, place.group * GCOLS, 0), (1, GCOLS, D))
    ds1, part, d_sqw, dg_reader = simple(
        slots_back,
        "slots_back",
        (xs, s1, ds2, drn, g_reader, w_so_rows, mix_q, att_own, own_live, g_slots, w_sq),
        [((slots, D), f32), ((slots, D), bf), ((D, 3 * GCOLS), bf), ((1, D), f32)],
    )
    dxn = place.sum_groups(part)
    x_grad, dg_slots = simple(
        slots_end, "slots_end", (xs, g_slots, dxn, ds1), [((slots, D), bf), ((1, D), f32)]
    )
    query_grad = place.owned_rows(x_grad)

    def own_cols(grad):
        return lax.dynamic_slice_in_dim(grad, place.group * GCOLS, GCOLS, 1).astype(bf)

    d_so = t_dot(att_q, own_cols(ds1)).astype(bf)
    d_ro = t_dot(read_q, own_cols(ds2)).astype(bf)

    def own_units(mine):
        mine = jnp.swapaxes(mine.reshape(-1, 2, r, D), 0, 1)
        both = ordered(even, pick(mine, core), place.sibling(pick(mine, 1 - core)))
        return both.reshape(-1, r, D).astype(f32)

    mine = place.scatter_whole(mlp_pairs)
    grad_up = own_units(mine[:2])
    grad_down = mine[2:].reshape(2 * R, D).astype(f32)
    grad_page = own_units(place.scatter_whole([(keep_page, give_page)]))
    grad_win = own_units(place.scatter_whole([(keep_window, give_window)]))

    d_cols = jnp.concatenate([d_sqw, d_rdw, d_qup, d_so, d_ro], axis=1)
    width = d_cols.shape[1] // 2
    both = jnp.concatenate([col_half(d_cols, core), col_half(d_qdown, core)], axis=1).astype(f32)
    both = both + place.sibling(
        jnp.concatenate([col_half(d_cols, 1 - core), col_half(d_qdown, 1 - core)], axis=1)
    ).astype(f32)
    both = (both * (1.0 / extra)).astype(bf).reshape(nz, nq * R, -1)
    gain_rows = jnp.concatenate([dg_window, dg_page, dg_vmlp] + [g / nq for g in (dg_slots, dg_reader, dg_qmlp)])
    gain_rows = jnp.transpose(gain_rows.reshape(6, nz, nq, 2 * r), (1, 2, 0, 3)).reshape(nz, 1, nq * 12 * r)
    gain_rows = jnp.pad(gain_rows.astype(bf), ((0, 0), (0, 7), (0, both.shape[-1] - nq * 12 * r)))
    mine = lax.psum_scatter(jnp.concatenate([both, gain_rows], axis=1), "dp", scatter_dimension=0)
    cols = mine[: nq * R, :width].reshape(nq, R, width)
    gain_row = mine[nq * R, : nq * 12 * r].reshape(nq, 1, 12 * r)
    cols = jnp.concatenate([cols, jnp.pad(gain_row, ((0, 0), (0, 7), (0, width - 12 * r)))], axis=1)
    total = [pick(cols, place.chip).astype(f32)]
    for mask in range(1, nq):
        total.append(place.hop(pick(cols, place.chip ^ mask), mask).astype(f32))
    gain_sum = sum(part[R, : 12 * r] for part in total)
    total = jnp.stack([part[:R] for part in total])
    by_group = jnp.stack(
        [sum(pick(total, place.chip ^ (k + GROUPS * e)) for e in range(extra)) for k in range(GROUPS)]
    )
    downs = mine[: nq * R, width:].reshape(extra, 4 * R, -1) * jnp.asarray(extra, bf)
    downs = pick(downs, place.chip // GROUPS)

    def halved(x, axis, which):
        half = x.shape[axis] // 2
        return lax.dynamic_slice_in_dim(x, which * half, half, axis)

    give = jnp.concatenate(
        [
            halved(by_group, 1, 1 - core).reshape(-1).astype(f32),
            halved(downs, 0, 1 - core).reshape(-1).astype(f32),
            gain_sum,
        ]
    )
    got = place.sibling(give)
    cut = GROUPS * r * width
    by_group = ordered(even, halved(by_group, 1, core), got[:cut].reshape(GROUPS, r, width))
    by_group = jnp.transpose(by_group, (1, 2, 0, 3)).reshape(GROUPS, r, 2 * width)
    downs = ordered(even, halved(downs, 0, core).astype(f32), got[cut : -12 * r].reshape(2 * R, -1))
    grad_qdown = jnp.swapaxes(downs, 0, 1).reshape(2 * R, D)
    both = pick((gain_sum + got[-12 * r :]).reshape(6, 2, r), core, 1)

    def columns_back(part):
        wide = part.reshape(GROUPS, r, -1, GCOLS)
        return jnp.transpose(wide, (1, 2, 0, 3)).reshape(r, -1)

    grad_sq = columns_back(by_group[..., : 3 * GCOLS])
    grad_rd = columns_back(by_group[..., 3 * GCOLS : 6 * GCOLS])
    hidden = by_group[..., 6 * GCOLS : 10 * GCOLS].reshape(GROUPS, r, nz, extra, 4 * D // (nz * nq))
    grad_qup = jnp.transpose(hidden, (1, 2, 3, 0, 4)).reshape(r, 4 * D)
    grad_so = columns_back(by_group[..., 10 * GCOLS : 11 * GCOLS])
    grad_ro = columns_back(by_group[..., 11 * GCOLS :])

    def wide(units):
        return jnp.concatenate([units[k] for k in range(units.shape[0])], axis=1)

    return (
        visual_out,
        query_out,
        visual_grad,
        query_grad,
        both[0],
        wide(grad_win[:3]),
        grad_win[3],
        both[3],
        grad_sq,
        grad_so,
        both[4],
        both[1],
        jnp.concatenate([grad_rd[:, :D], wide(grad_page[:2])], axis=1),
        grad_ro,
        jnp.concatenate([grad_page[2], grad_rd[:, D:]], axis=1),
        grad_page[3],
        both[2],
        wide(grad_up),
        grad_down,
        both[5],
        grad_qup,
        grad_qdown,
    )


def solution(mesh):
    page = P("dp", "fsdp", None, None)
    slot = P("dp", "fsdp", None)
    gain = P(("dp", "fsdp"))
    matrix = P(("dp", "fsdp"), None)
    weights = (
        gain,
        matrix,
        matrix,
        gain,
        matrix,
        matrix,
        gain,
        gain,
        matrix,
        matrix,
        matrix,
        matrix,
        gain,
        matrix,
        matrix,
        gain,
        matrix,
        matrix,
    )
    return jax.shard_map(
        local,
        mesh=mesh,
        in_specs=(page, slot, P("dp"), P("dp", None)) + weights + (page, slot),
        out_specs=(page, slot, page, slot) + weights,
        check_vma=False,
    )
```

```python
from functools import partial

import jax
import jax.numpy as jnp
from jax import lax
from jax.experimental import pallas as pl
from jax.experimental.pallas import tpu as pltpu
from jax.sharding import PartitionSpec as P

D = 768
HEADS = 12
HEAD = 64
WIN = 12
WCOLS = 8
Q_DEV = 16
MICRO = 2
PATCH = WIN * WIN
PAIRS = HEADS // 2
GROUPS = 4
GHEADS = HEADS // GROUPS
GCOLS = GHEADS * HEAD
SCALE = HEAD ** (-0.5)

bf = jnp.bfloat16
f32 = jnp.float32


def dot(a, b):
    return lax.dot_general(a, b, (((1,), (0,)), ((), ())), preferred_element_type=f32)


def dot_t(a, b):
    return lax.dot_general(a, b, (((1,), (1,)), ((), ())), preferred_element_type=f32)


def t_dot(a, b):
    return lax.dot_general(a, b, (((0,), (0,)), ((), ())), preferred_element_type=f32)


def normalise(x):
    centred = x - jnp.mean(x, axis=-1, keepdims=True)
    inv = lax.rsqrt(jnp.mean(centred * centred, axis=-1, keepdims=True) + 1e-05)
    return centred * inv, inv


def norm_back(grad, hat, inv, gain):
    scaled = grad * gain
    mean_one = jnp.mean(scaled, axis=-1, keepdims=True)
    mean_two = jnp.mean(scaled * hat, axis=-1, keepdims=True)
    return inv * (scaled - mean_one - hat * mean_two), jnp.sum(grad * hat, axis=0, keepdims=True)


def gelu_both(u):
    k = 0.7978845608028654
    t = jnp.tanh(k * (u + 0.044715 * u * u * u))
    slope = 0.5 * (1.0 + t) + 0.5 * u * (1.0 - t * t) * k * (1.0 + 3 * 0.044715 * u * u)
    return 0.5 * u * (1.0 + t), slope


def low_lanes(rows):
    return lax.broadcasted_iota(jnp.int32, (rows, 2 * HEAD), 1) < HEAD


def twofold(pair, mask):
    zero = jnp.zeros_like(pair)
    return jnp.concatenate([jnp.where(mask, pair, zero), jnp.where(mask, zero, pair)], axis=0)


def onefold(stacked, mask):
    rows = stacked.shape[0] // 2
    return jnp.where(mask, stacked[:rows], stacked[rows:])


def pair_forward(q2, k2, v2, bias):
    mask = low_lanes(q2.shape[0])
    s = dot_t(twofold(q2, mask), k2) * SCALE
    if bias is not None:
        s = s + bias
    m = jnp.max(s, axis=-1, keepdims=True)
    e = jnp.exp(s - m)
    l = jnp.sum(e, axis=-1, keepdims=True)
    out = dot(e.astype(bf), v2) / l
    return onefold(out, mask), m, l


def pair_backward(q2, k2, v2, d2, a2, bias, lse=None):
    mask = low_lanes(q2.shape[0])
    qs = twofold(q2, mask)
    ds = twofold(d2, mask)
    s = dot_t(qs, k2) * SCALE
    if bias is not None:
        s = s + bias
    if lse is None:
        e = jnp.exp(s - jnp.max(s, axis=-1, keepdims=True))
        p = e * (1.0 / jnp.sum(e, axis=-1, keepdims=True))
    else:
        p = jnp.exp(s - lse)
    corr = jnp.sum(ds.astype(f32) * twofold(a2, mask).astype(f32), axis=-1, keepdims=True)
    dp = dot_t(ds, v2)
    dsc = (p * (dp - corr)).astype(bf)
    dq = onefold(dot(dsc, k2), mask) * SCALE
    dk = t_dot(dsc, qs) * SCALE
    dv = t_dot(p.astype(bf), ds)
    return dq, dk, dv


def call(body, name, out_shape, in_specs, out_specs, grid, args, scratch=(), flops=0):
    return pl.pallas_call(
        body,
        name=name,
        out_shape=out_shape,
        grid=grid,
        in_specs=in_specs,
        out_specs=out_specs,
        scratch_shapes=scratch,
        compiler_params=pltpu.CompilerParams(vmem_limit_bytes=58 * 1024 * 1024),
        cost_estimate=pl.CostEstimate(flops=flops, bytes_accessed=1 << 20, transcendentals=0),
    )(*args)


def whole(shape):
    zeros = (0,) * len(shape)
    return pl.BlockSpec(shape, lambda *_: zeros, pipeline_mode=pl.Buffered(1))


def per_page(shape, axis):
    def place(p):
        return tuple(p if k == axis else 0 for k in range(len(shape)))

    return pl.BlockSpec(shape, place)


def sds(shape, dtype):
    return jax.ShapeDtypeStruct(shape, dtype)


def window_fwd(x_ref, bias_ref, gw_ref, w_ref, mix_ref, att_ref, v1_ref):
    rows = x_ref.shape[0]
    x = x_ref[...].astype(f32)
    xn = (normalise(x)[0] * gw_ref[...]).astype(bf)
    for u in range(3):
        mix_ref[u] = dot(xn, w_ref[u]).astype(bf)

    def window(w, carry):
        at = pl.ds(pl.multiple_of(w * PATCH, 16), PATCH)
        bias = bias_ref[w]
        bias = jnp.concatenate([bias, bias], axis=0)
        for p in range(PAIRS):
            c = slice(p * 128, p * 128 + 128)
            out = pair_forward(mix_ref[0, at, c], mix_ref[1, at, c], mix_ref[2, at, c], bias)[0]
            att_ref[at, c] = out.astype(bf)
        return carry

    lax.fori_loop(0, rows // PATCH, window, 0)
    v1_ref[...] = x_ref[...].astype(f32) + dot(att_ref[...], w_ref[3])


def normed_units(x_ref, g_ref, w_ref, out_ref):
    xn = (normalise(x_ref[...])[0] * g_ref[...]).astype(bf)
    for u in range(3):
        out_ref[u] = dot(xn, w_ref[u]).astype(bf)


def read_fwd(rq_ref, k_ref, v_ref, o_ref, lse_ref):
    slots = rq_ref.shape[1]
    lane = lax.broadcasted_iota(jnp.int32, (slots, 128), 1)
    acc = jnp.zeros((slots, 128), f32)
    for p in range(PAIRS):
        c = slice(p * 128, p * 128 + 128)
        out, m, l = pair_forward(rq_ref[0, :, c], k_ref[0, :, c], v_ref[0, :, c], None)
        o_ref[0, :, c] = out
        lse = m + jnp.log(l)
        acc = jnp.where(lane == 2 * p, lse[:slots], acc)
        acc = jnp.where(lane == 2 * p + 1, lse[slots:], acc)
    lse_ref[0] = acc


def write_fwd(v1_ref, wq_ref, wk_ref, wv_ref, bias_ref, wo_ref, wr_ref, v2_ref):
    for p in range(PAIRS):
        c = slice(p * 128, p * 128 + 128)
        out = pair_forward(wq_ref[0, :, c], wk_ref[0, :, c], wv_ref[0, :, c], bias_ref[0])[0]
        wr_ref[:, c] = out.astype(bf)
    v2_ref[...] = v1_ref[...] + dot(wr_ref[...], wo_ref[0])


def mlp_both(steps, last, rows_of_core, core_ref, x_ref, g_ref, up_ref, down_ref, cot_ref, *refs):
    if last:
        y_in_ref, dxn_in_ref, out_ref, dx_ref, dg_ref = refs[:5]
        refs = refs[5:]
        xn_ref, y_ref, dxn_ref = refs[-3:]
        outs = refs[:-3]
    else:
        y_ref, dxn_ref = refs[:2]
        xn_ref = refs[-1]
        outs = refs[2:-1]
    half = len(outs) // 2
    j = pl.program_id(0)

    @pl.when(j == 0)
    def _():
        xn_ref[...] = (normalise(x_ref[...])[0] * g_ref[...]).astype(bf)

    xn = xn_ref[...]
    cot = cot_ref[...]
    up = up_ref[0]
    down = down_ref[...]
    act, slope = gelu_both(dot(xn, up))
    act = act.astype(bf)
    y = dot(act, down)
    dpre = (dot_t(cot, down) * slope).astype(bf)
    dxn = dot_t(dpre, up)
    emit_unit(core_ref, t_dot(xn, dpre), outs[:half], 0)
    d_down = t_dot(act, cot)
    if half == 1:
        outs[1][...] = d_down.astype(bf)
    else:
        span = 2 * rows_of_core
        for i in range(d_down.shape[0] // span):
            emit(core_ref, d_down[i * span : (i + 1) * span], outs[2], outs[3], i)

    @pl.when(j == 0)
    def _():
        y_ref[...] = y_in_ref[...] + y if last else y
        dxn_ref[...] = dxn_in_ref[...] + dxn if last else dxn

    @pl.when(j > 0)
    def _():
        y_ref[...] += y
        dxn_ref[...] += dxn

    if last:

        @pl.when(j == steps - 1)
        def _():
            x = x_ref[...]
            out_ref[...] = (x + y_ref[...]).astype(bf)
            hat, inv = normalise(x)
            dx, dg = norm_back(dxn_ref[...], hat, inv, g_ref[...])
            dx_ref[...] = cot_ref[...].astype(f32) + dx
            dg_ref[...] = dg


def write_bwd(core_ref, dv2_ref, wr_ref, wq_ref, wk_ref, wv_ref, bias_ref, wo_ref, dwq_ref, dwk_ref, dwv_ref, *refs):
    outs, acc_ref = refs[:-1], refs[-1]
    page = pl.program_id(0)
    d = dv2_ref[...].astype(bf)
    dwr = dot_t(d, wo_ref[0]).astype(bf)
    part = t_dot(wr_ref[...], d)

    @pl.when(page == 0)
    def _():
        acc_ref[...] = part

    @pl.when(page > 0)
    def _():
        acc_ref[...] += part

    @pl.when(page == pl.num_programs(0) - 1)
    def _():
        emit_unit(core_ref, acc_ref[...], outs, 0)

    for p in range(PAIRS):
        c = slice(p * 128, p * 128 + 128)
        dq, dk, dv = pair_backward(
            wq_ref[0, :, c], wk_ref[0, :, c], wv_ref[0, :, c], dwr[:, c], wr_ref[:, c], bias_ref[0]
        )
        dwq_ref[:, c] = dq.astype(bf)
        dwk_ref[0, :, c] = dk.astype(bf)
        dwv_ref[0, :, c] = dv.astype(bf)


def read_bwd(rq_ref, k_ref, v_ref, d_ref, r_ref, lse_ref, dq_ref, dk_ref, dv_ref):
    slots = rq_ref.shape[1]
    lse = lse_ref[0]
    for p in range(PAIRS):
        c = slice(p * 128, p * 128 + 128)
        both = jnp.concatenate([lse[:, 2 * p : 2 * p + 1], lse[:, 2 * p + 1 : 2 * p + 2]], axis=0)
        dq, dk, dv = pair_backward(
            rq_ref[0, :, c], k_ref[0, :, c], v_ref[0, :, c], d_ref[0, :, c], r_ref[0, :, c], None, both
        )
        dq_ref[0, :, c] = dq.astype(bf)
        dk_ref[:, c] = dk.astype(bf)
        dv_ref[:, c] = dv.astype(bf)


def emit(core_ref, rows, keep_ref, give_ref, at):
    half = rows.shape[0] // 2
    first, second = rows[:half], rows[half:]
    here = core_ref[0] == 0
    keep_ref[at] = jnp.where(here, first, second).astype(bf)
    give_ref[at] = jnp.where(here, second, first).astype(bf)


def emit_unit(core_ref, unit, outs, u):
    if len(outs) == 1:
        outs[0][u] = unit.astype(bf)
        return
    chips = outs[0].shape[0]
    span = unit.shape[0] // chips
    for i in range(chips):
        emit(core_ref, unit[i * span : (i + 1) * span], outs[0], outs[1], (i, u))


def page_bwd(core_ref, v1_ref, dv2_ref, dk_ref, dv_ref, dwq_ref, gp_ref, wp_ref, dv1_ref, dg_ref, *refs):
    outs, acc_ref, gacc_ref = refs[:-2], refs[-2], refs[-1]
    page = pl.program_id(0)
    hat, inv = normalise(v1_ref[...])
    pn = (hat * gp_ref[...]).astype(bf)
    grads = (dk_ref, dv_ref, dwq_ref)
    dpn = dot_t(dk_ref[...], wp_ref[0]) + dot_t(dv_ref[...], wp_ref[1]) + dot_t(dwq_ref[...], wp_ref[2])
    dx, dg = norm_back(dpn, hat, inv, gp_ref[...])
    dv1_ref[...] = dv2_ref[...] + dx

    @pl.when(page == 0)
    def _():
        gacc_ref[...] = dg
        for u in range(3):
            acc_ref[u] = t_dot(pn, grads[u][...])

    @pl.when(page > 0)
    def _():
        gacc_ref[...] += dg
        for u in range(3):
            acc_ref[u] += t_dot(pn, grads[u][...])

    @pl.when(page == pl.num_programs(0) - 1)
    def _():
        dg_ref[...] = gacc_ref[...]
        for u in range(3):
            emit_unit(core_ref, acc_ref[u], outs, u)


def window_bwd(dv1_ref, mix_ref, att_ref, bias_ref, w_ref, *refs):
    dmix_ref, datt_ref = refs[-2:]
    rows = att_ref.shape[0]
    datt_ref[...] = dot_t(dv1_ref[...].astype(bf), w_ref[3]).astype(bf)

    def window(w, carry):
        at = pl.ds(pl.multiple_of(w * PATCH, 16), PATCH)
        bias = bias_ref[w]
        bias = jnp.concatenate([bias, bias], axis=0)
        for p in range(PAIRS):
            c = slice(p * 128, p * 128 + 128)
            dq, dk, dv = pair_backward(
                mix_ref[0, at, c], mix_ref[1, at, c], mix_ref[2, at, c], datt_ref[at, c], att_ref[at, c], bias
            )
            dmix_ref[0, at, c] = dq.astype(bf)
            dmix_ref[1, at, c] = dk.astype(bf)
            dmix_ref[2, at, c] = dv.astype(bf)
        return carry

    lax.fori_loop(0, rows // PATCH, window, 0)


def window_grads(core_ref, dv1_ref, x_ref, dmix_ref, att_ref, gw_ref, *refs):
    outs, acc_ref = refs[:-1], refs[-1]
    page = pl.program_id(0)
    xn = (normalise(x_ref[...].astype(f32))[0] * gw_ref[...]).astype(bf)
    d1b = dv1_ref[...].astype(bf)

    @pl.when(page == 0)
    def _():
        for u in range(3):
            acc_ref[u] = t_dot(xn, dmix_ref[u])
        acc_ref[3] = t_dot(att_ref[...], d1b)

    @pl.when(page > 0)
    def _():
        for u in range(3):
            acc_ref[u] += t_dot(xn, dmix_ref[u])
        acc_ref[3] += t_dot(att_ref[...], d1b)

    @pl.when(page == pl.num_programs(0) - 1)
    def _():
        for u in range(4):
            emit_unit(core_ref, acc_ref[u], outs, u)


def window_end(dv1_ref, x_ref, dmix_ref, gw_ref, w_ref, grad_ref, dg_ref, gacc_ref):
    page = pl.program_id(0)
    hat, inv = normalise(x_ref[...].astype(f32))
    dxn = dot_t(dmix_ref[0], w_ref[0]) + dot_t(dmix_ref[1], w_ref[1]) + dot_t(dmix_ref[2], w_ref[2])
    dx, dg = norm_back(dxn.astype(bf).astype(f32), hat, inv, gw_ref[...])
    grad_ref[...] = (dv1_ref[...] + dx).astype(bf)

    @pl.when(page == 0)
    def _():
        gacc_ref[...] = dg

    @pl.when(page > 0)
    def _():
        gacc_ref[...] += dg

    dg_ref[...] = gacc_ref[...]


def slots_fwd(x_ref, g_ref, w_ref, bias_ref, mix_ref, att_ref, s1_ref):
    x = x_ref[...].astype(f32)
    xn = (normalise(x)[0] * g_ref[...]).astype(bf)
    for u in range(3):
        mix_ref[u] = dot(xn, w_ref[u]).astype(bf)
    for p in range(PAIRS):
        c = slice(p * 128, p * 128 + 128)
        out = pair_forward(mix_ref[0, :, c], mix_ref[1, :, c], mix_ref[2, :, c], bias_ref[...])[0]
        att_ref[:, c] = out.astype(bf)
    s1_ref[...] = x + dot(att_ref[...], w_ref[3])


def own_columns(x, chip, span, step):
    total = x.shape[1]
    count = total // step * span
    row = lax.broadcasted_iota(jnp.int32, (total, count), 0)
    col = lax.broadcasted_iota(jnp.int32, (total, count), 1)
    at = lax.div(col, span) * step + chip * span + lax.rem(col, span)
    return dot(x, jnp.where(row == at, 1.0, 0.0).astype(bf)).astype(bf)


def query_mlp(
    span,
    step,
    chip_ref,
    s1_ref,
    read_ref,
    wo_ref,
    g_ref,
    up_ref,
    down_ref,
    cot_ref,
    out_ref,
    ds2_ref,
    dread_ref,
    dw_ref,
    ddown_ref,
    dg_ref,
):
    chip = chip_ref[0]
    reading = read_ref[...]
    s2 = s1_ref[...] + dot(reading, wo_ref[0])
    hat, inv = normalise(s2)
    xn = (hat * g_ref[...]).astype(bf)
    x_own = own_columns(xn, chip, span, step)
    cot = cot_ref[...]
    y, dxn = s2, None
    for k in range(4):
        up, down = up_ref[k], down_ref[k * D : (k + 1) * D]
        act, slope = gelu_both(dot(xn, up))
        act = act.astype(bf)
        y = y + dot(act, down)
        dpre = (dot_t(cot, down) * slope).astype(bf)
        part = dot_t(dpre, up)
        dxn = part if dxn is None else dxn + part
        dw_ref[k] = t_dot(x_own, dpre).astype(bf)
        act_own = own_columns(act, chip, 4 * span, 4 * step)
        rows = act_own.shape[1]
        ddown_ref[k * rows : (k + 1) * rows] = t_dot(act_own, cot).astype(bf)
    out_ref[...] = y.astype(bf)
    dx, dg = norm_back(dxn, hat, inv, g_ref[...])
    ds2 = cot.astype(f32) + dx
    ds2_ref[...] = ds2
    dg_ref[...] = dg
    d2b = ds2.astype(bf)
    dread_ref[...] = dot_t(d2b, wo_ref[0]).astype(bf)
    dw_ref[4] = t_dot(own_columns(reading, chip, span, step), d2b).astype(bf)


def query_back(
    span,
    step,
    chip_ref,
    x_ref,
    s1_ref,
    ds2_ref,
    d_ref,
    gr_ref,
    wr_ref,
    ws_ref,
    mix_ref,
    att_ref,
    bias_ref,
    gs_ref,
    out_ref,
    dw_ref,
    dgs_ref,
    dgr_ref,
    dmix_ref,
):
    chip = chip_ref[0]
    hat, inv = normalise(s1_ref[...])
    rn_own = own_columns((hat * gr_ref[...]).astype(bf), chip, span, step)
    drn = dot_t(d_ref[0], wr_ref[0]) + dot_t(d_ref[1], wr_ref[1]) + dot_t(d_ref[2], wr_ref[2])
    dx, dg = norm_back(drn, hat, inv, gr_ref[...])
    dgr_ref[...] = dg
    for u in range(3):
        dw_ref[4 + u] = t_dot(rn_own, d_ref[u]).astype(bf)
    ds1 = ds2_ref[...] + dx
    d1b = ds1.astype(bf)
    datt = dot_t(d1b, ws_ref[3]).astype(bf)
    dw_ref[3] = t_dot(own_columns(att_ref[...], chip, span, step), d1b).astype(bf)
    for p in range(PAIRS):
        c = slice(p * 128, p * 128 + 128)
        grads = pair_backward(
            mix_ref[0, :, c], mix_ref[1, :, c], mix_ref[2, :, c], datt[:, c], att_ref[:, c], bias_ref[...]
        )
        for u in range(3):
            dmix_ref[u, :, c] = grads[u].astype(bf)
    hat, inv = normalise(x_ref[...].astype(f32))
    xn_own = own_columns((hat * gs_ref[...]).astype(bf), chip, span, step)
    dxn = dot_t(dmix_ref[0], ws_ref[0]) + dot_t(dmix_ref[1], ws_ref[1]) + dot_t(dmix_ref[2], ws_ref[2])
    dx, dg = norm_back(dxn, hat, inv, gs_ref[...])
    dgs_ref[...] = dg
    out_ref[...] = (ds1 + dx).astype(bf)
    for u in range(3):
        dw_ref[u] = t_dot(xn_own, dmix_ref[u]).astype(bf)


def simple(body, name, args, outs, scratch=()):
    arrays = [a[0] if isinstance(a, tuple) else a for a in args]
    specs = [
        a[1]
        if isinstance(a, tuple)
        else pl.BlockSpec(memory_space=pltpu.SMEM)
        if a.ndim == 1
        else whole(a.shape)
        for a in args
    ]
    return call(
        body,
        name,
        tuple(sds(*o) for o in outs),
        specs,
        tuple(whole(o[0]) for o in outs),
        (1,),
        arrays,
        scratch=scratch,
        flops=1 << 30,
    )


def pack_rows(place, arrays, gains):
    window, out, slots, rows_of_slots, reader, rows_of_reader, writer, rows_of_writer, up, down, qup, qdown = arrays
    r = window.shape[0]

    def units(w):
        return [w[:, k * D : (k + 1) * D] for k in range(w.shape[1] // D)]

    def groups(win, o, sl, so, rd, ro, wr, wo, u, d, qu, qd, g):
        rd, wr = units(rd), units(wr)
        return (
            units(win) + [o] + units(sl) + [so, g],
            rd[1:] + wr[:1] + rd[:1] + wr[1:] + [wo],
            units(u) + [d[k] for k in range(4)],
            units(qu) + [ro] + [qd[k] for k in range(4)],
        )

    down, qdown = down.reshape(4, r, D), qdown.reshape(4, r, D)
    arrays = (window, out, slots, rows_of_slots, reader, rows_of_reader, writer, rows_of_writer, up, down, qup, qdown)
    if r % 8:
        return [jnp.stack(group) for group in groups(*arrays, gains)]

    def body(*refs):
        for group, out_ref in zip(groups(*refs[:13]), refs[13:]):
            for k, w in enumerate(group):
                out_ref[k] = w[...]

    return simple(body, "pack_rows", arrays + (gains,), [((n, r, D), bf) for n in (9, 7, 8, 9)])


def place_units(place, pieces, plain, tall):
    nz, n, r = pieces[0][0].shape[:3]
    left = n - plain - 4 * tall
    table = jnp.stack([place.core, place.chip % 4, place.z]).astype(jnp.int32)

    def body(table_ref, *args):
        refs, outs, (s_ref, sem) = args[:8], args[8:-2], args[-2:]
        core, chip, z = table_ref[0], table_ref[1], table_ref[2]
        now = pl.program_id(0)

        def targets():
            for c in range(2):
                owner = jnp.bitwise_xor(core, c)
                for i in range(4):
                    mask = jnp.where(owner == 0, i, (0, 2, 1, 3)[i])
                    yield 4 * c + i, s_ref.at[owner, jnp.bitwise_xor(chip, mask)]

        @pl.when(now == 0)
        def _():
            for k, there in targets():
                for m in range(nz):
                    at = jnp.bitwise_xor(z, m)
                    pltpu.make_async_copy(refs[k].at[m], there.at[at], sem.at[k, at]).start()

        for k, there in targets():
            pltpu.make_async_copy(refs[k].at[0], there.at[now], sem.at[k, now]).wait()
        for q in range(4):
            for u in range(plain):
                rows = [s_ref[c, q, now, u].astype(f32) for c in range(2)]
                outs[0][u, q] = jnp.concatenate(rows, axis=0).astype(bf)
            if tall:
                rows = [s_ref[c, q, now, plain + k].astype(f32) for c in range(2) for k in range(4)]
                outs[1][q] = jnp.concatenate(rows, axis=0).astype(bf)
            if left:
                rows = [s_ref[c, q, now, plain].astype(f32)[:1] for c in range(2)]
                outs[-1][q] = jnp.concatenate(rows + [jnp.zeros((6, D), f32)], axis=0)

    shapes = [jax.ShapeDtypeStruct((plain, 4 * nz, 2 * r, D), bf)]
    blocks = [pl.BlockSpec((plain, 4, 2 * r, D), lambda i: (0, i, 0, 0))]
    if tall:
        shapes.append(jax.ShapeDtypeStruct((4 * nz, 8 * r, D), bf))
        blocks.append(pl.BlockSpec((4, 8 * r, D), lambda i: (i, 0, 0)))
    if left:
        shapes.append(jax.ShapeDtypeStruct((4 * nz, 8, D), f32))
        blocks.append(pl.BlockSpec((4, 8, D), lambda i: (i, 0, 0)))
    out = pl.pallas_call(
        body,
        name="place_units",
        grid=(nz,),
        out_shape=tuple(shapes),
        in_specs=[pl.BlockSpec(memory_space=pltpu.SMEM)] + [pl.BlockSpec(memory_space=pl.ANY)] * 8,
        out_specs=tuple(blocks),
        scratch_shapes=[pltpu.VMEM((2, 4, nz, n, r, D), bf), pltpu.SemaphoreType.DMA((8, nz))],
        compiler_params=pltpu.CompilerParams(vmem_limit_bytes=60 * 1024 * 1024),
        cost_estimate=pl.CostEstimate(flops=0, bytes_accessed=n * D * D * 4, transcendentals=0),
    )(table, *pieces[0], *pieces[1])
    out = list(out)
    out[0] = out[0].reshape(plain, D, D)
    if tall:
        out[1] = out[1].reshape(4 * D, D)
    return out


def pick(stack, index, axis=0):
    return lax.dynamic_index_in_dim(stack, index, axis, keepdims=False)


def ordered(first, mine, other):
    return jnp.stack([jnp.where(first, mine, other), jnp.where(first, other, mine)])


class Place:
    def __init__(self):
        self.nz = lax.axis_size("dp")
        self.nf = lax.axis_size("fsdp")
        self.nq = self.nf // 2
        self.z = lax.axis_index("dp")
        self.f = lax.axis_index("fsdp")
        self.core = self.f % 2
        self.even = self.core == 0
        self.chip = self.f // 2
        self.group = self.chip % GROUPS

    def sibling(self, x):
        return lax.ppermute(x, "fsdp", [(f, f ^ 1) for f in range(self.nf)])

    def hop(self, x, mask, odd_mask=None):
        odd_mask = mask if odd_mask is None else odd_mask
        route = [(f, f ^ ((odd_mask if f % 2 else mask) << 1)) for f in range(self.nf)]
        return lax.ppermute(x, "fsdp", route)

    def across(self, x, mask):
        return lax.ppermute(x, "dp", [(z, z ^ mask) for z in range(self.nz)])

    def send_line(self, x):
        return [self.across(x, m) for m in range(1, self.nz)]

    def send_terms(self, now):
        return [self.across(pick(now, self.z ^ m), m) for m in range(1, self.nz)]

    def gather_square(self, block, bit):
        a, b = 1 << bit, 2 << bit
        first = self.hop(block, a, b)
        second = self.hop(block, b, a)
        return [block, first, second, self.hop(first, b, a)]

    def first_hop(self, x):
        return self.hop(x, 1, 2)

    def second_hop(self, x):
        return self.hop(x, 2, 1)

    def arranged(self, pieces, bit, odd):
        here = (self.chip >> bit) % 4
        stack = jnp.stack(pieces)
        at = [0, 1, 2, 3]
        swapped = jnp.where(odd, jnp.array([0, 2, 1, 3]), jnp.array(at))
        return jnp.stack([pick(stack, swapped[here ^ k]) for k in at])

    def gather_plain(self, block):
        stack = jnp.stack([block] + self.send_line(block))
        now = jnp.stack([pick(stack, self.z ^ k) for k in range(self.nz)])
        levels = 0
        for bit in range(0, self.nq.bit_length() - 1, 2):
            now = self.arranged(self.gather_square(now, bit), bit, ~self.even)
            levels += 1
        now = ordered(self.even, now, self.sibling(now))
        n, r = block.shape[:2]
        now = now.reshape(2, self.nq, self.nz, n, r, D)
        return jnp.transpose(now, (3, 2, 1, 0, 4, 5))

    def chip_terms(self, pairs):
        def parts(i):
            blocks = []
            for keep, other in pairs:
                shape = (self.nz, 4) + (() if self.nq == 4 else (self.nq // 4,)) + keep.shape[2:]
                blocks.append(pick(keep.reshape(shape), i, 1).astype(f32) + pick(other.reshape(shape), i, 1).astype(f32))
            return jnp.concatenate(blocks, axis=-3)

        return parts

    def halves(self, x, r):
        x = x.reshape((-1, self.nz, self.nq, 2, r, x.shape[-1]))

        def rows(which):
            return jnp.moveaxis(pick(x, which, 3), 0, 2)

        return rows(self.core), rows(1 - self.core)

    def square_terms(self, parts):
        bit = (self.nq.bit_length() - 1) - 2
        here = (self.chip >> bit) % 4
        first = jnp.where(self.even, 1, 2)
        return [parts(here ^ mask) for mask in (3 - first, jnp.full_like(first, 3), first, jnp.zeros_like(first))]

    def outer_hop(self, which, x):
        bit = (self.nq.bit_length() - 1) - 2
        a, b = 1 << bit, 2 << bit
        return self.hop(x, a, b) if which == 0 else self.hop(x, b, a)

    def inner_square(self, now):
        if now.ndim > 4:
            first = jnp.where(self.even, 1, 2)
            here = self.chip % 4

            def at(mask):
                return pick(now, here ^ mask, 1).astype(f32)

            second = self.hop(at(3 - first).astype(bf), 2, 1)
            corner = self.hop(at(3).astype(bf), 2, 1)
            moved = self.hop((at(first) + corner.astype(f32)).astype(bf), 1, 2)
            now = (at(0) + moved.astype(f32) + second.astype(f32)).astype(bf)
        return now

    def own_terms(self, now):
        return pick(now, self.z).astype(f32)

    def group_hops(self, x):
        return [self.hop(x, mask) for mask in range(1, GROUPS)]

    def in_order(self, pieces):
        stack = jnp.stack(pieces)
        return jnp.stack([pick(stack, self.group ^ k) for k in range(GROUPS)])

    def to_groups(self, blocks):
        return [self.hop(pick(blocks, self.group ^ mask), mask) for mask in range(1, GROUPS)]

    def owned_rows(self, mine, axis=0):
        own = lax.dynamic_slice_in_dim(mine, self.f * Q_DEV, Q_DEV, axis)
        give = lax.dynamic_slice_in_dim(mine, (self.f ^ 1) * Q_DEV, Q_DEV, axis)
        return ordered(self.even, own, self.sibling(give))


def tie(*arrays):
    return lax.optimization_barrier(arrays)


def stage(*moves):
    operands = tie(*[operand for _, operand in moves])
    return tie(*[move(operand) for (move, _), operand in zip(moves, operands)])


def split_three(x):
    hi = lax.reduce_precision(x, 8, 7)
    mid = lax.reduce_precision(x - hi, 8, 7)
    return [hi.astype(bf), mid.astype(bf), (x - hi - mid).astype(bf)]


def join_three(x):
    a, b, c = jnp.split(x.astype(f32), 3, axis=-1)
    return (a + b) + c


def columns(weight):
    rows, width = weight.shape
    return [weight[:, k * D : (k + 1) * D] for k in range(width // D)]


def strip_bias(place, bands, height):
    half = WIN // 2
    rows = (place.f % bands) * height + jnp.arange(height, dtype=jnp.int32)
    cols = (place.f // bands) * WIN + jnp.arange(WIN, dtype=jnp.int32)

    def label(at, total):
        return (at >= total - WIN).astype(jnp.int32) + (at >= total - half).astype(jnp.int32)

    labels = label(rows, height * bands)[:, None] * 3 + label(cols, WIN * WCOLS)
    labels = labels.reshape(height // WIN, PATCH)
    return jnp.where(labels[:, :, None] == labels[:, None, :], 0.0, -1e30).astype(f32)


def roll_beside(x, place, bands):
    route = [((f + bands) % place.nf, f) for f in range(place.nf)]
    return lax.ppermute(x, "fsdp", route)


def roll_in(x, beside, place, bands):
    half = WIN // 2
    pages, height = x.shape[:2]
    if bands > 1:
        x = jnp.concatenate([x[:, :, half:], beside], axis=2)
        route = [(f // bands * bands + (f + 1) % bands, f) for f in range(place.nf)]
        below = lax.ppermute(x[:, :half], "fsdp", route)
        return jnp.concatenate([x[:, half:], below], axis=1).reshape(-1, D)

    def body(x_ref, b_ref, out_ref, tall_ref):
        for to in range(height):
            row = (to + half) % height
            tall_ref[to * WIN : to * WIN + half] = x_ref[0, row].astype(f32)[half:]
            tall_ref[to * WIN + half : (to + 1) * WIN] = b_ref[0, row].astype(f32)
        out_ref[...] = tall_ref[...].astype(bf)

    return call(
        body,
        "roll_in",
        sds((pages * height * WIN, D), bf),
        [per_page((1, height, WIN, D), 0), per_page((1, height, half, D), 0)],
        per_page((height * WIN, D), 0),
        (pages,),
        (x, beside),
        scratch=(pltpu.VMEM((height * WIN, D), f32),),
        flops=1 << 20,
    )


def roll_out(x, place, bands):
    half = WIN // 2
    beside = lax.ppermute(x[:, :, half:], "fsdp", [(f, (f + bands) % place.nf) for f in range(place.nf)])
    x = jnp.concatenate([beside, x[:, :, :half]], axis=2)
    above = x[:, -half:]
    if bands > 1:
        route = [(f, f // bands * bands + (f + 1) % bands) for f in range(place.nf)]
        above = lax.ppermute(above, "fsdp", route)
    return jnp.concatenate([above, x[:, :-half]], axis=1)


def local(
    visual,
    query_slots,
    lengths,
    slot_order,
    norm_window,
    window_qkv,
    window_out,
    norm_slots,
    slots_qkv,
    slots_out,
    norm_reader,
    norm_page,
    reader_qkv,
    reader_out,
    writer_qkv,
    writer_out,
    norm_visual_mlp,
    visual_up,
    visual_down,
    norm_query_mlp,
    query_up,
    query_down,
    visual_cot,
    query_cot,
):
    place = Place()
    nz, nf, nq, core, even = place.nz, place.nf, place.nq, place.core, place.even
    extra = nq // GROUPS
    bands = nf // WCOLS
    height = visual.shape[1]
    page_rows = height * WIN
    rows = MICRO * page_rows
    slots = Q_DEV * nf
    r = window_out.shape[0]

    fast = r % 8 == 0 and nq == 4
    gains = jnp.stack([norm_window, norm_slots, norm_reader, norm_page, norm_visual_mlp, norm_query_mlp])
    gains = jnp.zeros((r, D), bf).at[0, : 6 * r].set(gains.reshape(6 * r))
    arrays = (
        window_qkv,
        window_out,
        slots_qkv,
        slots_out,
        reader_qkv,
        reader_out,
        writer_qkv,
        writer_out,
        visual_up,
        visual_down,
        query_up,
        query_down,
    )
    one, two, three, four = pack_rows(place, arrays, gains)

    def squares(x):
        return [place.first_hop(x), place.second_hop(x)]

    def siblings(x):
        return jax.tree.map(place.sibling, x)

    def assemble(block, pieces, others, plain, tall):
        if fast:
            return place_units(place, [pieces, others], plain, tall)
        units = place.gather_plain(block)
        out = [units[:plain].reshape(plain, D, D)]
        if tall:
            out.append(jnp.transpose(units[plain:], (1, 2, 3, 0, 4, 5)).reshape(4 * D, D))
        elif block.shape[0] > plain:
            rows_left = units[plain, ..., 0, :].reshape(nz * nq, 2, D).astype(f32)
            out.append(jnp.pad(rows_left, ((0, 0), (0, 6), (0, 0))))
        return out

    ends = jnp.stack([query_slots, query_cot])
    positions = (slot_order[:, :, None] * Q_DEV + jnp.arange(Q_DEV, dtype=jnp.int32)).reshape(MICRO, slots)
    live = jnp.where(positions < lengths[:, None], 0.0, -1e30).astype(f32).reshape(MICRO, 1, slots)
    own_live = pick(live, core)
    bias = strip_bias(place, bands, height)
    chip_id = place.chip.astype(jnp.int32).reshape(1)
    core_id = core.astype(jnp.int32).reshape(1)

    def spread(x, bit):
        return place.hop(x, 1 << bit)

    def spread_order(x, got, bit):
        upper = (place.chip >> bit) % 2 == 1
        return jnp.concatenate([jnp.where(upper, got, x), jnp.where(upper, x, got)], axis=1)

    def all_dp(block, got):
        return jnp.stack([block] + list(got))

    got, ends_two, beside_x = stage(
        (place.send_line, one),
        (place.sibling, pick(ends, 1 - core, 1)),
        (partial(roll_beside, place=place, bands=bands), visual[:, :, : WIN // 2]),
    )
    all_one = all_dp(one, got)
    ends = jnp.swapaxes(ordered(even, pick(ends, core, 1), ends_two), 0, 1).reshape(2, 2 * Q_DEV, D)
    got, (f_one, s_one) = stage((place.send_line, two), (squares, all_one))
    all_two = all_dp(two, got)
    x = roll_in(visual, beside_x, place, bands)
    c_one, sib_one, sib_f_one, sib_s_one, ends_two = stage(
        (place.second_hop, f_one),
        (place.sibling, all_one),
        (place.sibling, f_one),
        (place.sibling, s_one),
        (partial(spread, bit=0), ends),
    )
    ends = spread_order(ends, ends_two, 0)
    got, (f_two, s_two) = stage((place.send_line, three), (squares, all_two))
    all_three = all_dp(three, got)
    c_two, ends_two, sib_c_one, sib_two, beside_cot = stage(
        (place.second_hop, f_two),
        (partial(spread, bit=1), ends),
        (place.sibling, c_one),
        (place.sibling, all_two),
        (partial(roll_beside, place=place, bands=bands), visual_cot[:, :, : WIN // 2]),
    )
    ends = spread_order(ends, ends_two, 1)
    for bit in range(2, nq.bit_length() - 1):
        ends = spread_order(ends, spread(ends, bit), bit)
    xs, xs_cot = ends[0], ends[1]

    act_block = per_page((page_rows, D), 0)
    three_block = per_page((3, page_rows, D), 1)

    def part_of(size, index, full):
        return full, pl.BlockSpec((size, D, D), lambda *_: (index, 0, 0), pipeline_mode=pl.Buffered(1))

    def run_first(args):
        sib_c, x, xs = args
        w_one, gain_all = assemble(one, [all_one, f_one, s_one, c_one], [sib_one, sib_f_one, sib_s_one, sib_c], 8, 0)
        gain_all = gain_all[:, :2, : 6 * r].reshape(nz * nq * 2, 6, r)
        gain_all = jnp.transpose(gain_all, (1, 0, 2)).reshape(6, 1, D)
        windows = call(
            window_fwd,
            "window_fwd",
            (sds((3, rows, D), bf), sds((rows, D), bf), sds((rows, D), f32)),
            [act_block, whole(bias.shape), whole((1, D)), part_of(4, 0, None)[1]],
            (three_block, act_block, act_block),
            (MICRO,),
            (x, bias, gain_all[0], w_one),
            flops=2 * rows * 4 * D * D,
        )
        heard = simple(
            slots_fwd,
            "slots_fwd",
            (xs, gain_all[1], part_of(4, 1, w_one), own_live),
            [((3, slots, D), bf), ((slots, D), bf), ((slots, D), f32)],
        )
        return w_one, gain_all, windows, heard

    (f_three, s_three), sib_f_two, sib_s_two, sib_c_two, first = stage(
        (squares, all_three),
        (place.sibling, f_two),
        (place.sibling, s_two),
        (place.sibling, c_two),
        (run_first, (sib_c_one, x, xs)),
    )
    cot = roll_in(visual_cot, beside_cot, place, bands)
    w_one, gain_all, (mix, att, v1), (mix_q, att_q, s1) = first
    g_window, g_slots, g_reader, g_page, g_vmlp, g_qmlp = (gain_all[k] for k in range(6))

    def run_second(args):
        sib_c, v1, s1 = args
        (w_two,) = assemble(two, [all_two, f_two, s_two, c_two], [sib_two, sib_f_two, sib_s_two, sib_c], 7, 0)
        (rd_own,) = simple(
            normed_units, "slots_units", (s1, g_reader, part_of(3, 1, w_two)), [((3, slots, D), bf)]
        )
        pk = call(
            normed_units,
            "page_units",
            sds((3, rows, D), bf),
            [act_block, whole((1, D)), part_of(3, 0, None)[1]],
            three_block,
            (MICRO,),
            (v1, g_page, w_two),
            flops=2 * rows * 3 * D * D,
        )
        return w_two, rd_own, pk

    c_three, sib_three, sib_f_three, sib_s_three, (w_two, rd_own, pk) = stage(
        (place.second_hop, f_three),
        (place.sibling, all_three),
        (place.sibling, f_three),
        (place.sibling, s_three),
        (run_second, (sib_c_two, v1, s1)),
    )
    rd_two, sib_c_three = stage((place.sibling, rd_own), (place.sibling, c_three))
    rd = jnp.swapaxes(ordered(even, rd_own, rd_two), 0, 1)
    rq, wk, wv = rd[0], rd[1], rd[2]
    slot_block = per_page((1, slots, D), 0)
    stat_block = per_page((1, slots, 128), 0)

    def of_pk(u):
        return pl.BlockSpec((1, page_rows, D), lambda p: (u, p, 0))

    o_part, lse_part = call(
        read_fwd,
        "read_fwd",
        (sds((MICRO, slots, D), f32), sds((MICRO, slots, 128), f32)),
        [slot_block, of_pk(0), of_pk(1)],
        (slot_block, stat_block),
        (MICRO,),
        (rq, pk, pk),
        flops=2 * rows * slots * D * 4,
    )

    def merge(terms):
        width = terms[0].shape[-1] // (HEAD + 1) * HEAD
        lse = jnp.stack([t[..., width:] for t in terms])
        top = jnp.max(lse, axis=0)
        weights = jnp.exp(lse - top)
        total = jnp.sum(weights, axis=0)
        shares = weights / total
        out = sum(t[..., :width] * jnp.repeat(share, HEAD, axis=-1) for t, share in zip(terms, shares))
        return jnp.concatenate([out, top + jnp.log(total)], axis=-1)

    terms = jnp.concatenate([o_part, lse_part[..., :HEADS]], axis=-1)
    live_block = per_page((1, 1, slots), 0)

    def run_write(args):
        return call(
            write_fwd,
            "write_fwd",
            (sds((rows, D), bf), sds((rows, D), f32)),
            [act_block, of_pk(2), slot_block, slot_block, live_block, part_of(1, 6, None)[1]],
            (act_block, act_block),
            (MICRO,),
            args,
            flops=2 * rows * D * D,
        )

    terms_two, (writing, v2), (w_up, w_down) = stage(
        (place.sibling, pick(terms, 1 - core)),
        (run_write, (v1, pk, wk, wv, live, w_two)),
        (
            lambda sib_c: assemble(
                three, [all_three, f_three, s_three, c_three], [sib_three, sib_f_three, sib_s_three, sib_c], 4, 1
            ),
            sib_c_three,
        ),
    )
    terms = merge([pick(terms, core), terms_two])
    blocks = jnp.concatenate(
        [terms[:, :D].reshape(slots, GROUPS, GCOLS), terms[:, D:].reshape(slots, GROUPS, GHEADS)], axis=-1
    )
    blocks = jnp.swapaxes(blocks, 0, 1)
    chunk = 384
    steps = 2 * D // chunk
    per_unit = D // chunk

    def once(*shape):
        return pl.BlockSpec(shape, lambda j: (0,) * len(shape), pipeline_mode=pl.Buffered(1))

    smem = pl.BlockSpec(memory_space=pltpu.SMEM)
    zq = nz * nq
    if fast:
        up_shapes = [sds((zq, 2, r, D), bf)] * 2
        up_outs = [pl.BlockSpec((zq, 1, r, chunk), lambda j: (0, j // per_unit, 0, j % per_unit))] * 2
        down_shapes = [sds((zq // 2, 4 * r, D), bf)] * 2
        down_outs = [pl.BlockSpec((chunk // (8 * r), 4 * r, D), lambda j: (j, 0, 0))] * 2
    else:
        up_shapes = [sds((2, D, D), bf)]
        up_outs = [pl.BlockSpec((1, D, chunk), lambda j: (j // per_unit, 0, j % per_unit))]
        down_shapes = [sds((2 * D, D), bf)]
        down_outs = [pl.BlockSpec((chunk, D), lambda j: (j, 0))]

    def run_mlp(last, args):
        at = steps if last else 0
        up_in = pl.BlockSpec((1, D, chunk), lambda j: ((j + at) // per_unit, 0, (j + at) % per_unit))
        down_in = pl.BlockSpec((chunk, D), lambda j: (j + at, 0))
        wide = once(rows, D)
        scratch = (pltpu.VMEM((rows, D), bf),)
        if last:
            shapes = [sds((rows, D), bf), sds((rows, D), f32), sds((1, D), f32)]
            outs = [wide, wide, once(1, D)]
            scratch = scratch + (pltpu.VMEM((rows, D), f32), pltpu.VMEM((rows, D), f32))
        else:
            shapes = [sds((rows, D), f32), sds((rows, D), f32)]
            outs = [wide, wide]
        out = call(
            partial(mlp_both, steps, last, 4 * r),
            "mlp_both",
            tuple(shapes + up_shapes + down_shapes),
            [smem, wide, once(1, D), up_in, down_in, wide] + [wide, wide] * last,
            tuple(outs + up_outs + down_outs),
            (steps,),
            (core_id,) + args,
            scratch=scratch,
            flops=2 * rows * 12 * D * D,
        )
        count = len(outs)
        if fast:
            up = [y.reshape(nz, nq, 2, r, D) for y in out[count : count + 2]]
            down = [y.reshape(nz // 2, nq, 4, r, D) for y in out[count + 2 :]]
        else:
            up = place.halves(out[count], r)
            d = out[count + 1].reshape(nz // 2, nq, 2, 4, r, D)
            down = [pick(d, which, 2) for which in (core, 1 - core)]
        return tuple(out[:count]) + (list(up), list(down))

    def run_grads(body, name, shapes, specs, outs, args, units, scratch, flops):
        if fast:
            unit_shapes = [sds((zq, units, r, D), bf)] * 2
        else:
            unit_shapes = [sds((units, D, D), bf)]
        unit_outs = [whole(y.shape) for y in unit_shapes]
        out = call(
            body,
            name,
            tuple(shapes + unit_shapes),
            [smem] + specs,
            tuple(outs + unit_outs),
            (MICRO,),
            (core_id,) + args,
            scratch=scratch,
            flops=flops,
        )
        count = len(outs)
        if fast:
            pair = [y.reshape(nz, nq, units, r, D) for y in out[count:]]
        else:
            pair = list(place.halves(out[count], r))
        return tuple(out[:count]) + (pair,)

    got = stage((place.to_groups, blocks))[0]
    reading = merge([pick(blocks, place.group)] + list(got))
    for bit in range(2, nq.bit_length() - 1):
        reading = merge([reading, place.hop(reading, 1 << bit)])
    message = jnp.concatenate([reading[:, :GCOLS].astype(bf)] + split_three(reading[:, GCOLS:]), axis=-1)
    got, (y, dxn, up_one, down_one) = stage(
        (place.send_line, four), (partial(run_mlp, False), (v2, g_vmlp, w_up, w_down, cot))
    )
    all_four = all_dp(four, got)
    reads, (f_four, s_four), (v3, dv2, dg_vmlp, up_two, down_two) = stage(
        (place.group_hops, message),
        (squares, all_four),
        (partial(run_mlp, True), (v2, g_vmlp, w_up, w_down, cot, y, dxn)),
    )
    reads = place.in_order([message] + list(reads))
    lse_page = jnp.swapaxes(reads[..., GCOLS:], 0, 1).reshape(slots, 3 * HEADS)
    read_q = jnp.swapaxes(reads[..., :GCOLS], 0, 1).reshape(slots, D)

    def run_write_bwd(args):
        return run_grads(
            write_bwd,
            "write_bwd",
            [sds((rows, D), bf), sds((MICRO, slots, D), bf), sds((MICRO, slots, D), bf)],
            [act_block, act_block, of_pk(2), slot_block, slot_block, live_block, part_of(1, 6, None)[1]],
            [act_block, slot_block, slot_block],
            args,
            1,
            (pltpu.VMEM((D, D), f32),),
            4 * rows * D * D,
        )

    c_four, sib_four, sib_f_four, sib_s_four, (dwq, dwk, dwv, pair_wo) = stage(
        (place.second_hop, f_four),
        (place.sibling, all_four),
        (place.sibling, f_four),
        (place.sibling, s_four),
        (run_write_bwd, (dv2, writing, pk, wk, wv, live, w_two)),
    )
    sib_c_four, *net_got = stage(
        (place.sibling, c_four),
        (place.sibling, up_one[1]),
        (place.sibling, up_two[1]),
        (place.sibling, down_one[1]),
        (place.sibling, down_two[1]),
    )
    keep_down = jnp.concatenate([down_one[0], down_two[0]])
    down_got = jnp.concatenate([net_got[2], net_got[3]])
    second, corner, first, own_net = place.square_terms(
        place.chip_terms([(up_one[0], net_got[0]), (up_two[0], net_got[1]), (keep_down, down_got)])
    )

    def run_query(args):
        units, w_down = assemble(
            four, [all_four, f_four, s_four, c_four], [sib_four, sib_f_four, sib_s_four, sib_c_four], 5, 1
        )
        s1, read_q = args
        up_block = pl.BlockSpec((4, D, D), lambda *_: (0, 0, 0), pipeline_mode=pl.Buffered(1))
        return simple(
            partial(query_mlp, 2 * r, D // nz),
            "query_mlp",
            (chip_id, s1, read_q, part_of(1, 4, units), g_qmlp, (units, up_block), w_down, xs_cot),
            [
                ((slots, D), bf),
                ((slots, D), f32),
                ((slots, D), bf),
                ((5, 2 * r * nz, D), bf),
                ((8 * r * nz, D), bf),
                ((1, D), f32),
            ],
        )

    second, corner, (q_out, ds2, d_read, d_early, d_qdown, dg_qmlp) = stage(
        (partial(place.outer_hop, 1), second.astype(bf)),
        (partial(place.outer_hop, 1), corner.astype(bf)),
        (run_query, (s1, read_q)),
    )
    own_net = own_net + second.astype(f32)
    first = (first + corner.astype(f32)).astype(bf)

    def chip_halves(x, r):
        x = x.reshape(x.shape[0], nz, 2, r, D)
        return [jnp.swapaxes(pick(x, which, 2), 0, 1) for which in (core, 1 - core)]

    tall = [y.reshape(nz, 4, r, D) for y in chip_halves(d_qdown[None], 4 * r)]
    keep_early, give_early = (
        jnp.concatenate([a, b], axis=1) for a, b in zip(chip_halves(d_early, r), tall)
    )
    three_parts = jnp.concatenate([d_read, read_q, lse_page], axis=-1)
    parts_two, early_got = stage((place.sibling, three_parts), (place.sibling, give_early))
    three_parts = ordered(even, three_parts, parts_two)
    d_read_all, read_all = three_parts[..., :D], three_parts[..., D : 2 * D]
    lse_all = join_three(three_parts[..., 2 * D :].reshape(MICRO, slots, GROUPS, 3 * GHEADS))
    lse_all = jnp.pad(lse_all.reshape(MICRO, slots, HEADS), ((0, 0), (0, 0), (0, 128 - HEADS)))
    early = (keep_early.astype(f32) + early_got.astype(f32)).astype(bf)
    early_sum = lax.psum_scatter(early.reshape(nz, 9 * r, D), "dp", scatter_dimension=0).reshape(9, r, D)
    early_sum = early_sum.astype(f32)

    def run_read_bwd(args):
        return call(
            read_bwd,
            "read_bwd",
            (sds((MICRO, slots, D), bf), sds((rows, D), bf), sds((rows, D), bf)),
            [slot_block, of_pk(0), of_pk(1), slot_block, slot_block, stat_block],
            (slot_block, act_block, act_block),
            (MICRO,),
            args,
            flops=2 * rows * slots * D * 10,
        )

    first, (drq, dk, dv) = stage(
        (partial(place.outer_hop, 0), first), (run_read_bwd, (rq, pk, pk, d_read_all, read_all, lse_all))
    )

    def run_page_bwd(args):
        return run_grads(
            page_bwd,
            "page_bwd",
            [sds((rows, D), f32), sds((1, D), f32)],
            [act_block, act_block, act_block, act_block, act_block, whole((1, D)), whole((3, D, D))],
            [act_block, whole((1, D))],
            args,
            3,
            (pltpu.VMEM((3, D, D), f32), pltpu.VMEM((1, D), f32)),
            2 * rows * 6 * D * D,
        )

    d_slots = jnp.stack([drq, dwk, dwv], axis=1)
    own_net = place.inner_square((own_net + first.astype(f32)).astype(bf))
    net_sum = lax.psum_scatter(own_net.reshape(nz, 8 * r, D), "dp", scatter_dimension=0).reshape(8, r, D)
    slots_two, (dv1, dg_page, pair_page) = stage(
        (place.sibling, pick(d_slots, 1 - core)), (run_page_bwd, (v1, dv2, dk, dv, dwq, g_page, w_two))
    )
    d_slots = (pick(d_slots, core).astype(f32) + slots_two.astype(f32)).astype(bf)
    d_slots = jnp.transpose(d_slots.reshape(3, slots, GROUPS, GCOLS), (2, 0, 1, 3))

    def run_window_bwd(page, args):
        here = pl.BlockSpec((page_rows, D), lambda i: (page, 0))
        three_here = pl.BlockSpec((3, page_rows, D), lambda i: (0, page, 0))
        return pl.pallas_call(
            window_bwd,
            name="window_bwd",
            out_shape=sds((3, rows, D), bf),
            grid=(1,),
            in_specs=[here, three_here, here, whole(bias.shape), part_of(4, 0, None)[1]]
            + [pl.BlockSpec(memory_space=pl.ANY)] * page,
            out_specs=three_here,
            scratch_shapes=(pltpu.VMEM((page_rows, D), bf),),
            input_output_aliases={5: 0} if page else {},
            compiler_params=pltpu.CompilerParams(vmem_limit_bytes=58 * 1024 * 1024),
            cost_estimate=pl.CostEstimate(flops=rows * 2 * D * D, bytes_accessed=1 << 20, transcendentals=0),
        )(*args)

    page_got, got, dmix = stage(
        (siblings, [pair_page[1], pair_wo[1]]),
        (place.to_groups, d_slots),
        (partial(run_window_bwd, 0), (dv1, mix, att, bias, w_one)),
    )
    d_rd = sum(x.astype(f32) for x in [pick(d_slots, place.group)] + list(got)).astype(bf)
    for bit in range(2, nq.bit_length() - 1):
        d_rd = (d_rd.astype(f32) + place.hop(d_rd, 1 << bit).astype(f32)).astype(bf)
    second, corner, first, own_page = place.square_terms(
        place.chip_terms([(pair_page[0], page_got[0]), (pair_wo[0], page_got[1])])
    )
    rds, second, corner, dmix = stage(
        (place.group_hops, d_rd),
        (partial(place.outer_hop, 1), second.astype(bf)),
        (partial(place.outer_hop, 1), corner.astype(bf)),
        (partial(run_window_bwd, 1), (dv1, mix, att, bias, w_one, dmix)),
    )
    own_page = own_page + second.astype(f32)
    first = (first + corner.astype(f32)).astype(bf)
    d_rd = jnp.transpose(place.in_order([d_rd] + list(rds)), (1, 2, 0, 3)).reshape(3, slots, D)

    def run_query_back(args):
        return simple(
            partial(query_back, 2 * r, D // nz),
            "query_back",
            (*args[:6], part_of(3, 1, args[6]), part_of(4, 1, args[7]), *args[8:]),
            [((slots, D), bf), ((7, 2 * r * nz, D), bf), ((1, D), f32), ((1, D), f32)],
            scratch=(pltpu.VMEM((3, slots, D), bf),),
        )

    def run_window_grads(args):
        return run_grads(
            window_grads,
            "window_grads",
            [],
            [act_block, act_block, three_block, act_block, whole((1, D))],
            [],
            args,
            4,
            (pltpu.VMEM((4, D, D), f32),),
            2 * rows * 4 * D * D,
        )

    first, (pair_window,) = stage(
        (partial(place.outer_hop, 0), first), (run_window_grads, (dv1, x, dmix, att, g_window))
    )
    own_page = place.inner_square((own_page + first.astype(f32)).astype(bf))
    page_sum = lax.psum_scatter(own_page.reshape(nz, 4 * r, D), "dp", scatter_dimension=0).reshape(4, r, D)
    window_got, (x_grad, d_late, dg_slots, dg_reader) = stage(
        (place.sibling, pair_window[1]),
        (
            run_query_back,
            (chip_id, xs, s1, ds2, d_rd, g_reader, w_two, w_one, mix_q, att_q, own_live, g_slots),
        ),
    )
    keep_late, give_late = chip_halves(d_late, r)
    second, corner, first, own_window = place.square_terms(place.chip_terms([(pair_window[0], window_got)]))
    second, late_got = tie(second.astype(bf), place.sibling(give_late))
    late = (keep_late.astype(f32) + late_got.astype(f32)).astype(bf)

    def run_window_end(args):
        return call(
            window_end,
            "window_end",
            (sds((rows, D), bf), sds((1, D), f32)),
            [act_block, act_block, three_block, whole((1, D)), part_of(4, 0, None)[1]],
            (act_block, whole((1, D))),
            (MICRO,),
            args,
            scratch=(pltpu.VMEM((1, D), f32),),
            flops=2 * rows * 3 * D * D,
        )

    second, corner, late_passed, (v_grad, dg_window) = stage(
        (partial(place.outer_hop, 1), second),
        (partial(place.outer_hop, 1), corner.astype(bf)),
        (place.send_terms, late),
        (run_window_end, (dv1, x, dmix, g_window, w_one)),
    )
    own_window = own_window + second.astype(f32)
    first = (first + corner.astype(f32)).astype(bf)
    late_sum = place.own_terms(late) + sum(y.astype(f32) for y in late_passed)
    own_gains = jnp.concatenate([dg_window, dg_page, dg_vmlp])
    query_gains = jnp.concatenate([dg_slots, dg_reader, dg_qmlp])
    first, chip_gains = stage(
        (partial(place.outer_hop, 0), first),
        (lambda x: [place.hop(x, mask) for mask in range(1, nq)], own_gains),
    )
    own_window = place.inner_square((own_window + first.astype(f32)).astype(bf))
    gain_rows = jnp.concatenate([own_gains + sum(chip_gains), query_gains]).reshape(6, nz, nq, 2, r)
    gain_rows = pick(gain_rows, place.chip, 2)
    gain_rows = pick(gain_rows, core, 2) + place.sibling(pick(gain_rows, 1 - core, 2))
    gain_rows = jnp.swapaxes(gain_rows, 0, 1).reshape(nz, 1, 1, 6 * r).astype(bf)
    gain_rows = jnp.pad(gain_rows, ((0, 0), (0, 0), (0, r - 1), (0, D - 6 * r)))
    own_window = jnp.concatenate([own_window, gain_rows], axis=1)
    window_passed = place.send_terms(own_window)
    grad_win = place.own_terms(own_window) + sum(y.astype(f32) for y in window_passed)
    both = grad_win[4, 0, : 6 * r].reshape(6, r)

    visual_out = roll_out(v3.reshape(MICRO, height, WIN, D), place, bands)
    visual_grad = roll_out(v_grad.reshape(MICRO, height, WIN, D), place, bands)
    query_out = place.owned_rows(q_out)
    query_grad = place.owned_rows(x_grad)

    grad_page = page_sum.astype(f32)
    grad_up = net_sum[:4].astype(f32)
    grad_down = net_sum[4:].reshape(4 * r, D).astype(f32)
    grad_qup = jnp.concatenate([early_sum[k] for k in range(4)], axis=1)
    grad_ro = early_sum[4]
    grad_qdown = early_sum[5:].reshape(4 * r, D)
    grad_sq = jnp.concatenate([late_sum[k] for k in range(3)], axis=1)
    grad_so = late_sum[3]
    grad_rd = jnp.concatenate([late_sum[4 + k] for k in range(3)], axis=1)

    def wide(units):
        return jnp.concatenate([units[k] for k in range(units.shape[0])], axis=1)

    return (
        visual_out,
        query_out,
        visual_grad,
        query_grad,
        both[0],
        wide(grad_win[:3]),
        grad_win[3],
        both[3],
        grad_sq,
        grad_so,
        both[4],
        both[1],
        jnp.concatenate([grad_rd[:, :D], wide(grad_page[:2])], axis=1),
        grad_ro,
        jnp.concatenate([grad_page[2], grad_rd[:, D:]], axis=1),
        grad_page[3],
        both[2],
        wide(grad_up),
        grad_down,
        both[5],
        grad_qup,
        grad_qdown,
    )


def solution(mesh):
    page = P("dp", "fsdp", None, None)
    slot = P("dp", "fsdp", None)
    gain = P(("dp", "fsdp"))
    matrix = P(("dp", "fsdp"), None)
    weights = (
        gain,
        matrix,
        matrix,
        gain,
        matrix,
        matrix,
        gain,
        gain,
        matrix,
        matrix,
        matrix,
        matrix,
        gain,
        matrix,
        matrix,
        gain,
        matrix,
        matrix,
    )
    return jax.shard_map(
        local,
        mesh=mesh,
        in_specs=(page, slot, P("dp"), P("dp", None)) + weights + (page, slot),
        out_specs=(page, slot, page, slot) + weights,
        check_vma=False,
    )
```

```python
from functools import partial

import jax
import jax.numpy as jnp
from jax import lax
from jax.experimental import pallas as pl
from jax.experimental.pallas import tpu as pltpu
from jax.sharding import PartitionSpec as P

D = 768
HEADS = 12
HEAD = 64
WIN = 12
WCOLS = 8
Q_DEV = 16
MICRO = 2
PATCH = WIN * WIN
PAIRS = HEADS // 2
GROUPS = 4
GHEADS = HEADS // GROUPS
GCOLS = GHEADS * HEAD
SCALE = HEAD ** (-0.5)

bf = jnp.bfloat16
f32 = jnp.float32


def dot(a, b):
    return lax.dot_general(a, b, (((1,), (0,)), ((), ())), preferred_element_type=f32)


def dot_t(a, b):
    return lax.dot_general(a, b, (((1,), (1,)), ((), ())), preferred_element_type=f32)


def t_dot(a, b):
    return lax.dot_general(a, b, (((0,), (0,)), ((), ())), preferred_element_type=f32)


def normalise(x):
    centred = x - jnp.mean(x, axis=-1, keepdims=True)
    inv = lax.rsqrt(jnp.mean(centred * centred, axis=-1, keepdims=True) + 1e-05)
    return centred * inv, inv


def norm_back(grad, hat, inv, gain):
    scaled = grad * gain
    mean_one = jnp.mean(scaled, axis=-1, keepdims=True)
    mean_two = jnp.mean(scaled * hat, axis=-1, keepdims=True)
    return inv * (scaled - mean_one - hat * mean_two), jnp.sum(grad * hat, axis=0, keepdims=True)


def gelu_both(u):
    k = 0.7978845608028654
    t = jnp.tanh(k * (u + 0.044715 * u * u * u))
    slope = 0.5 * (1.0 + t) + 0.5 * u * (1.0 - t * t) * k * (1.0 + 3 * 0.044715 * u * u)
    return 0.5 * u * (1.0 + t), slope


def low_lanes(rows):
    return lax.broadcasted_iota(jnp.int32, (rows, 2 * HEAD), 1) < HEAD


def twofold(pair, mask):
    zero = jnp.zeros_like(pair)
    return jnp.concatenate([jnp.where(mask, pair, zero), jnp.where(mask, zero, pair)], axis=0)


def onefold(stacked, mask):
    rows = stacked.shape[0] // 2
    return jnp.where(mask, stacked[:rows], stacked[rows:])


def groups_of_pairs(q_rows, k_rows):
    together = max(1, min(PAIRS, 700000 // (2 * q_rows * k_rows)))
    return [range(p, min(p + together, PAIRS)) for p in range(0, PAIRS, together)]


def lanes(p):
    return slice(p * 2 * HEAD, (p + 1) * 2 * HEAD)


def scaled(q2, mask):
    return twofold(q2 * jnp.asarray(SCALE, bf), mask)


def pairs_forward(q, k, v, bias):
    mask = low_lanes(q[0].shape[0])
    s = [dot_t(scaled(q2, mask), k2) for q2, k2 in zip(q, k)]
    if bias is not None:
        s = [x + bias for x in s]
    m = [jnp.max(x, axis=-1, keepdims=True) for x in s]
    e = [jnp.exp(x - top) for x, top in zip(s, m)]
    l = [jnp.sum(x, axis=-1, keepdims=True) for x in e]
    out = [dot(x.astype(bf), v2) for x, v2 in zip(e, v)]
    return [(onefold(x / total, mask), top, total) for x, top, total in zip(out, m, l)]


def pairs_backward(q, k, v, d, a, bias, lse=None):
    mask = low_lanes(q[0].shape[0])
    qs = [scaled(q2, mask) for q2 in q]
    ds = [twofold(d2, mask) for d2 in d]
    s = [dot_t(q2, k2) for q2, k2 in zip(qs, k)]
    dp = [dot_t(d2, v2) for d2, v2 in zip(ds, v)]
    corr = [
        jnp.sum(d2.astype(f32) * twofold(a2, mask).astype(f32), axis=-1, keepdims=True) for d2, a2 in zip(ds, a)
    ]
    if bias is not None:
        s = [x + bias for x in s]
    if lse is None:
        e = [jnp.exp(x - jnp.max(x, axis=-1, keepdims=True)) for x in s]
        p = [x * (1.0 / jnp.sum(x, axis=-1, keepdims=True)) for x in e]
    else:
        p = [jnp.exp(x - y) for x, y in zip(s, lse)]
    dsc = [(x * (y - c)).astype(bf) for x, y, c in zip(p, dp, corr)]
    dq = [onefold(dot(x, k2), mask) * SCALE for x, k2 in zip(dsc, k)]
    dk = [t_dot(x, q2) for x, q2 in zip(dsc, qs)]
    dv = [t_dot(x.astype(bf), d2) for x, d2 in zip(p, ds)]
    return list(zip(dq, dk, dv))


def call(body, name, out_shape, in_specs, out_specs, grid, args, scratch=(), flops=0):
    return pl.pallas_call(
        body,
        name=name,
        out_shape=out_shape,
        grid=grid,
        in_specs=in_specs,
        out_specs=out_specs,
        scratch_shapes=scratch,
        compiler_params=pltpu.CompilerParams(vmem_limit_bytes=58 * 1024 * 1024),
        cost_estimate=pl.CostEstimate(flops=flops, bytes_accessed=1 << 20, transcendentals=0),
    )(*args)


def whole(shape):
    zeros = (0,) * len(shape)
    return pl.BlockSpec(shape, lambda *_: zeros, pipeline_mode=pl.Buffered(1))


def per_page(shape, axis):
    def place(p):
        return tuple(p if k == axis else 0 for k in range(len(shape)))

    return pl.BlockSpec(shape, place)


def sds(shape, dtype):
    return jax.ShapeDtypeStruct(shape, dtype)


def window_fwd(x_ref, bias_ref, gw_ref, w_ref, mix_ref, att_ref, v1_ref):
    rows = x_ref.shape[0]
    x = x_ref[...].astype(f32)
    xn = (normalise(x)[0] * gw_ref[...]).astype(bf)
    for u in range(3):
        mix_ref[u] = dot(xn, w_ref[u]).astype(bf)

    def window(w, carry):
        at = pl.ds(pl.multiple_of(w * PATCH, 16), PATCH)
        bias = bias_ref[w]
        bias = jnp.concatenate([bias, bias], axis=0)
        for group in groups_of_pairs(PATCH, PATCH):
            cs = [lanes(p) for p in group]
            outs = pairs_forward(*([mix_ref[u, at, c] for c in cs] for u in range(3)), bias)
            for c, (out, _, _) in zip(cs, outs):
                att_ref[at, c] = out.astype(bf)
        return carry

    lax.fori_loop(0, rows // PATCH, window, 0)
    v1_ref[...] = x_ref[...].astype(f32) + dot(att_ref[...], w_ref[3])


def normed_units(x_ref, g_ref, w_ref, out_ref):
    xn = (normalise(x_ref[...])[0] * g_ref[...]).astype(bf)
    for u in range(3):
        out_ref[u] = dot(xn, w_ref[u]).astype(bf)


def read_fwd(rq_ref, k_ref, v_ref, o_ref, lse_ref):
    slots = rq_ref.shape[1]
    lane = lax.broadcasted_iota(jnp.int32, (slots, 128), 1)
    acc = jnp.zeros((slots, 128), f32)
    for group in groups_of_pairs(slots, k_ref.shape[1]):
        cs = [lanes(p) for p in group]
        outs = pairs_forward(*([ref[0, :, c] for c in cs] for ref in (rq_ref, k_ref, v_ref)), None)
        for p, c, (out, m, l) in zip(group, cs, outs):
            o_ref[0, :, c] = out
            lse = m + jnp.log(l)
            acc = jnp.where(lane == 2 * p, lse[:slots], acc)
            acc = jnp.where(lane == 2 * p + 1, lse[slots:], acc)
    lse_ref[0] = acc


def write_fwd(v1_ref, wq_ref, wk_ref, wv_ref, bias_ref, wo_ref, wr_ref, v2_ref):
    for group in groups_of_pairs(wq_ref.shape[1], wk_ref.shape[1]):
        cs = [lanes(p) for p in group]
        outs = pairs_forward(*([ref[0, :, c] for c in cs] for ref in (wq_ref, wk_ref, wv_ref)), bias_ref[0])
        for c, (out, _, _) in zip(cs, outs):
            wr_ref[:, c] = out.astype(bf)
    v2_ref[...] = v1_ref[...] + dot(wr_ref[...], wo_ref[0])


def mlp_both(steps, last, rows_of_core, core_ref, x_ref, g_ref, up_ref, down_ref, cot_ref, *refs):
    if last:
        y_in_ref, dxn_in_ref, out_ref, dx_ref, dg_ref = refs[:5]
        refs = refs[5:]
        xn_ref, y_ref, dxn_ref = refs[-3:]
        outs = refs[:-3]
    else:
        y_ref, dxn_ref = refs[:2]
        xn_ref = refs[-1]
        outs = refs[2:-1]
    half = len(outs) // 2
    j = pl.program_id(0)

    @pl.when(j == 0)
    def _():
        xn_ref[...] = (normalise(x_ref[...])[0] * g_ref[...]).astype(bf)

    xn = xn_ref[...]
    cot = cot_ref[...]
    up = up_ref[0]
    down = down_ref[...]
    act, slope = gelu_both(dot(xn, up))
    act = act.astype(bf)
    y = dot(act, down)
    dpre = (dot_t(cot, down) * slope).astype(bf)
    dxn = dot_t(dpre, up)
    emit_unit(core_ref, t_dot(xn, dpre), outs[:half], 0)
    d_down = t_dot(act, cot)
    if half == 1:
        outs[1][...] = d_down.astype(bf)
    else:
        span = 2 * rows_of_core
        for i in range(d_down.shape[0] // span):
            emit(core_ref, d_down[i * span : (i + 1) * span], outs[2], outs[3], (i, 0))

    @pl.when(j == 0)
    def _():
        y_ref[...] = y_in_ref[...] + y if last else y
        dxn_ref[...] = dxn_in_ref[...] + dxn if last else dxn

    @pl.when(j > 0)
    def _():
        y_ref[...] += y
        dxn_ref[...] += dxn

    if last:

        @pl.when(j == steps - 1)
        def _():
            x = x_ref[...]
            out_ref[...] = (x + y_ref[...]).astype(bf)
            hat, inv = normalise(x)
            dx, dg = norm_back(dxn_ref[...], hat, inv, g_ref[...])
            dx_ref[...] = cot_ref[...].astype(f32) + dx
            dg_ref[...] = dg


def write_bwd(core_ref, dv2_ref, wr_ref, wq_ref, wk_ref, wv_ref, bias_ref, wo_ref, dwq_ref, dwk_ref, dwv_ref, *refs):
    outs, acc_ref = refs[:-1], refs[-1]
    page = pl.program_id(0)
    d = dv2_ref[...].astype(bf)
    dwr = dot_t(d, wo_ref[0]).astype(bf)
    part = t_dot(wr_ref[...], d)

    @pl.when(page == 0)
    def _():
        acc_ref[...] = part

    @pl.when(page > 0)
    def _():
        acc_ref[...] += part

    @pl.when(page == pl.num_programs(0) - 1)
    def _():
        emit_unit(core_ref, acc_ref[...], outs, 0)

    for group in groups_of_pairs(wq_ref.shape[1], wk_ref.shape[1]):
        cs = [lanes(p) for p in group]
        parts = ([ref[0, :, c] for c in cs] for ref in (wq_ref, wk_ref, wv_ref))
        grads = pairs_backward(*parts, [dwr[:, c] for c in cs], [wr_ref[:, c] for c in cs], bias_ref[0])
        for c, (dq, dk, dv) in zip(cs, grads):
            dwq_ref[:, c] = dq.astype(bf)
            dwk_ref[0, :, c] = dk.astype(bf)
            dwv_ref[0, :, c] = dv.astype(bf)


def read_bwd(rq_ref, k_ref, v_ref, d_ref, r_ref, lse_ref, dq_ref, dk_ref, dv_ref):
    slots = rq_ref.shape[1]
    lse = lse_ref[0]
    for group in groups_of_pairs(slots, k_ref.shape[1]):
        cs = [lanes(p) for p in group]
        both = [jnp.concatenate([lse[:, 2 * p + k : 2 * p + k + 1] for k in range(2)], axis=0) for p in group]
        parts = ([ref[0, :, c] for c in cs] for ref in (rq_ref, k_ref, v_ref, d_ref, r_ref))
        for c, (dq, dk, dv) in zip(cs, pairs_backward(*parts, None, both)):
            dq_ref[0, :, c] = dq.astype(bf)
            dk_ref[:, c] = dk.astype(bf)
            dv_ref[:, c] = dv.astype(bf)


def emit(core_ref, rows, keep_ref, give_ref, at):
    half = rows.shape[0] // 2
    first, second = rows[:half], rows[half:]
    here = core_ref[0] == 0
    keep_ref[at] = jnp.where(here, first, second).astype(bf)
    give_ref[at] = jnp.where(here, second, first).astype(bf)


def emit_unit(core_ref, unit, outs, u):
    if len(outs) == 1:
        outs[0][u] = unit.astype(bf)
        return
    nq, nz = outs[0].shape[:2]
    span = unit.shape[0] // (nq * nz)
    for z in range(nz):
        for q in range(nq):
            i = z * nq + q
            emit(core_ref, unit[i * span : (i + 1) * span], outs[0], outs[1], (q, z, u))


def page_bwd(core_ref, v1_ref, dv2_ref, dk_ref, dv_ref, dwq_ref, gp_ref, wp_ref, dv1_ref, dg_ref, *refs):
    outs, acc_ref, gacc_ref = refs[:-2], refs[-2], refs[-1]
    page = pl.program_id(0)
    hat, inv = normalise(v1_ref[...])
    pn = (hat * gp_ref[...]).astype(bf)
    grads = (dk_ref, dv_ref, dwq_ref)
    dpn = dot_t(dk_ref[...], wp_ref[0]) + dot_t(dv_ref[...], wp_ref[1]) + dot_t(dwq_ref[...], wp_ref[2])
    dx, dg = norm_back(dpn, hat, inv, gp_ref[...])
    dv1_ref[...] = dv2_ref[...] + dx

    @pl.when(page == 0)
    def _():
        gacc_ref[...] = dg
        for u in range(3):
            acc_ref[u] = t_dot(pn, grads[u][...])

    @pl.when(page > 0)
    def _():
        gacc_ref[...] += dg
        for u in range(3):
            acc_ref[u] += t_dot(pn, grads[u][...])

    @pl.when(page == pl.num_programs(0) - 1)
    def _():
        dg_ref[...] = gacc_ref[...]
        for u in range(3):
            emit_unit(core_ref, acc_ref[u], outs, u)


def window_bwd(dv1_ref, mix_ref, att_ref, bias_ref, w_ref, *refs):
    dmix_ref, datt_ref = refs[-2:]
    rows = att_ref.shape[0]
    datt_ref[...] = dot_t(dv1_ref[...].astype(bf), w_ref[3]).astype(bf)

    def window(w, carry):
        at = pl.ds(pl.multiple_of(w * PATCH, 16), PATCH)
        bias = bias_ref[w]
        bias = jnp.concatenate([bias, bias], axis=0)
        for group in groups_of_pairs(PATCH, PATCH):
            cs = [lanes(p) for p in group]
            parts = ([mix_ref[u, at, c] for c in cs] for u in range(3))
            grads = pairs_backward(*parts, [datt_ref[at, c] for c in cs], [att_ref[at, c] for c in cs], bias)
            for c, grad in zip(cs, grads):
                for u in range(3):
                    dmix_ref[u, at, c] = grad[u].astype(bf)
        return carry

    lax.fori_loop(0, rows // PATCH, window, 0)


def window_grads(core_ref, dv1_ref, x_ref, dmix_ref, att_ref, gw_ref, *refs):
    outs, acc_ref = refs[:-1], refs[-1]
    page = pl.program_id(0)
    xn = (normalise(x_ref[...].astype(f32))[0] * gw_ref[...]).astype(bf)
    d1b = dv1_ref[...].astype(bf)

    @pl.when(page == 0)
    def _():
        for u in range(3):
            acc_ref[u] = t_dot(xn, dmix_ref[u])
        acc_ref[3] = t_dot(att_ref[...], d1b)

    @pl.when(page > 0)
    def _():
        for u in range(3):
            acc_ref[u] += t_dot(xn, dmix_ref[u])
        acc_ref[3] += t_dot(att_ref[...], d1b)

    @pl.when(page == pl.num_programs(0) - 1)
    def _():
        for u in range(4):
            emit_unit(core_ref, acc_ref[u], outs, u)


def window_end(dv1_ref, x_ref, dmix_ref, gw_ref, w_ref, grad_ref, dg_ref, gacc_ref):
    page = pl.program_id(0)
    hat, inv = normalise(x_ref[...].astype(f32))
    dxn = dot_t(dmix_ref[0], w_ref[0]) + dot_t(dmix_ref[1], w_ref[1]) + dot_t(dmix_ref[2], w_ref[2])
    dx, dg = norm_back(dxn.astype(bf).astype(f32), hat, inv, gw_ref[...])
    grad_ref[...] = (dv1_ref[...] + dx).astype(bf)

    @pl.when(page == 0)
    def _():
        gacc_ref[...] = dg

    @pl.when(page > 0)
    def _():
        gacc_ref[...] += dg

    dg_ref[...] = gacc_ref[...]


def slots_fwd(x_ref, g_ref, w_ref, bias_ref, mix_ref, att_ref, s1_ref):
    x = x_ref[...].astype(f32)
    xn = (normalise(x)[0] * g_ref[...]).astype(bf)
    for u in range(3):
        mix_ref[u] = dot(xn, w_ref[u]).astype(bf)
    for group in groups_of_pairs(x.shape[0], x.shape[0]):
        cs = [lanes(p) for p in group]
        outs = pairs_forward(*([mix_ref[u, :, c] for c in cs] for u in range(3)), bias_ref[...])
        for c, (out, _, _) in zip(cs, outs):
            att_ref[:, c] = out.astype(bf)
    s1_ref[...] = x + dot(att_ref[...], w_ref[3])


def own_columns(x, chip, span, step):
    total = x.shape[1]
    count = total // step * span
    row = lax.broadcasted_iota(jnp.int32, (total, count), 0)
    col = lax.broadcasted_iota(jnp.int32, (total, count), 1)
    at = lax.div(col, span) * step + chip * span + lax.rem(col, span)
    return dot(x, jnp.where(row == at, 1.0, 0.0).astype(bf)).astype(bf)


def emit_chip(core_ref, unit, outs, u, r):
    if len(outs) == 1:
        outs[0][u] = unit.astype(bf)
        return
    for z in range(unit.shape[0] // (2 * r)):
        emit(core_ref, unit[z * 2 * r : (z + 1) * 2 * r], outs[0], outs[1], (z, u))


def query_mlp(
    span,
    step,
    chip_ref,
    core_ref,
    s1_ref,
    read_ref,
    wo_ref,
    g_ref,
    up_ref,
    down_ref,
    cot_ref,
    out_ref,
    ds2_ref,
    dread_ref,
    dg_ref,
    *outs,
):
    chip = chip_ref[0]
    split = len(outs) // 2
    reading = read_ref[...]
    s2 = s1_ref[...] + dot(reading, wo_ref[0])
    hat, inv = normalise(s2)
    xn = (hat * g_ref[...]).astype(bf)
    x_own = own_columns(xn, chip, span, step)
    cot = cot_ref[...]
    y, dxn = s2, None
    for k in range(4):
        up, down = up_ref[k], down_ref[k * D : (k + 1) * D]
        act, slope = gelu_both(dot(xn, up))
        act = act.astype(bf)
        y = y + dot(act, down)
        dpre = (dot_t(cot, down) * slope).astype(bf)
        part = dot_t(dpre, up)
        dxn = part if dxn is None else dxn + part
        emit_chip(core_ref, t_dot(x_own, dpre), outs[:split], k, span // 2)
        act_own = own_columns(act, chip, 4 * span, 4 * step)
        rows = act_own.shape[1]
        d_down = t_dot(act_own, cot)
        if split == 1:
            outs[1][0, k * rows : (k + 1) * rows] = d_down.astype(bf)
        else:
            emit(core_ref, d_down, outs[2], outs[3], (k, 0))
    out_ref[...] = y.astype(bf)
    dx, dg = norm_back(dxn, hat, inv, g_ref[...])
    ds2 = cot.astype(f32) + dx
    ds2_ref[...] = ds2
    dg_ref[...] = dg
    d2b = ds2.astype(bf)
    dread_ref[...] = dot_t(d2b, wo_ref[0]).astype(bf)
    emit_chip(core_ref, t_dot(own_columns(reading, chip, span, step), d2b), outs[:split], 4, span // 2)


def query_back(
    span,
    step,
    chip_ref,
    core_ref,
    x_ref,
    s1_ref,
    ds2_ref,
    d_ref,
    gr_ref,
    wr_ref,
    ws_ref,
    mix_ref,
    att_ref,
    bias_ref,
    gs_ref,
    out_ref,
    dgs_ref,
    dgr_ref,
    *refs,
):
    outs, dmix_ref = refs[:-1], refs[-1]
    chip = chip_ref[0]
    hat, inv = normalise(s1_ref[...])
    rn_own = own_columns((hat * gr_ref[...]).astype(bf), chip, span, step)
    drn = dot_t(d_ref[0], wr_ref[0]) + dot_t(d_ref[1], wr_ref[1]) + dot_t(d_ref[2], wr_ref[2])
    dx, dg = norm_back(drn, hat, inv, gr_ref[...])
    dgr_ref[...] = dg
    for u in range(3):
        emit_chip(core_ref, t_dot(rn_own, d_ref[u]), outs, 4 + u, span // 2)
    ds1 = ds2_ref[...] + dx
    d1b = ds1.astype(bf)
    datt = dot_t(d1b, ws_ref[3]).astype(bf)
    emit_chip(core_ref, t_dot(own_columns(att_ref[...], chip, span, step), d1b), outs, 3, span // 2)
    for group in groups_of_pairs(datt.shape[0], datt.shape[0]):
        cs = [lanes(p) for p in group]
        parts = ([mix_ref[u, :, c] for c in cs] for u in range(3))
        grads = pairs_backward(*parts, [datt[:, c] for c in cs], [att_ref[:, c] for c in cs], bias_ref[...])
        for c, grad in zip(cs, grads):
            for u in range(3):
                dmix_ref[u, :, c] = grad[u].astype(bf)
    hat, inv = normalise(x_ref[...].astype(f32))
    xn_own = own_columns((hat * gs_ref[...]).astype(bf), chip, span, step)
    dxn = dot_t(dmix_ref[0], ws_ref[0]) + dot_t(dmix_ref[1], ws_ref[1]) + dot_t(dmix_ref[2], ws_ref[2])
    dx, dg = norm_back(dxn, hat, inv, gs_ref[...])
    dgs_ref[...] = dg
    out_ref[...] = (ds1 + dx).astype(bf)
    for u in range(3):
        emit_chip(core_ref, t_dot(xn_own, dmix_ref[u]), outs, u, span // 2)


def simple(body, name, args, outs, scratch=()):
    arrays = [a[0] if isinstance(a, tuple) else a for a in args]
    specs = [
        a[1]
        if isinstance(a, tuple)
        else pl.BlockSpec(memory_space=pltpu.SMEM)
        if a.ndim == 1
        else whole(a.shape)
        for a in args
    ]
    return call(
        body,
        name,
        tuple(sds(*o) for o in outs),
        specs,
        tuple(whole(o[0]) for o in outs),
        (1,),
        arrays,
        scratch=scratch,
        flops=1 << 30,
    )


def pack_rows(place, arrays, gains):
    window, out, slots, rows_of_slots, reader, rows_of_reader, writer, rows_of_writer, up, down, qup, qdown = arrays
    r = window.shape[0]

    def units(w):
        return [w[:, k * D : (k + 1) * D] for k in range(w.shape[1] // D)]

    def groups(win, o, sl, so, rd, ro, wr, wo, u, d, qu, qd, g):
        rd, wr = units(rd), units(wr)
        return (
            units(win) + [o] + units(sl) + [so, g],
            rd[1:] + wr[:1] + rd[:1] + wr[1:] + [wo],
            units(u) + [d[k] for k in range(4)],
            units(qu) + [ro] + [qd[k] for k in range(4)],
        )

    down, qdown = down.reshape(4, r, D), qdown.reshape(4, r, D)
    arrays = (window, out, slots, rows_of_slots, reader, rows_of_reader, writer, rows_of_writer, up, down, qup, qdown)
    if r % 8:
        return [jnp.stack(group) for group in groups(*arrays, gains)]

    def body(*refs):
        for group, out_ref in zip(groups(*refs[:13]), refs[13:]):
            for k, w in enumerate(group):
                out_ref[k] = w[...]

    return simple(body, "pack_rows", arrays + (gains,), [((n, r, D), bf) for n in (9, 7, 8, 9)])


def place_units(place, pieces, plain, tall):
    nz, n, r = pieces[0][0].shape[:3]
    left = n - plain - 4 * tall
    table = jnp.stack([place.core, place.chip % 4, place.z]).astype(jnp.int32)

    def body(table_ref, *args):
        refs, outs, (s_ref, sem) = args[:8], args[8:-2], args[-2:]
        core, chip, z = table_ref[0], table_ref[1], table_ref[2]
        now = pl.program_id(0)

        def targets():
            for c in range(2):
                owner = jnp.bitwise_xor(core, c)
                for i in range(4):
                    mask = jnp.where(owner == 0, i, (0, 2, 1, 3)[i])
                    yield 4 * c + i, s_ref.at[owner, jnp.bitwise_xor(chip, mask)]

        @pl.when(now == 0)
        def _():
            for to in range(nz):
                for k, there in targets():
                    pltpu.make_async_copy(refs[k].at[jnp.bitwise_xor(z, to)], there.at[to], sem.at[k, to]).start()

        for k, there in targets():
            pltpu.make_async_copy(refs[k].at[0], there.at[now], sem.at[k, now]).wait()
        for q in range(4):
            for u in range(plain):
                rows = [s_ref[c, q, now, u].astype(f32) for c in range(2)]
                outs[0][u, q] = jnp.concatenate(rows, axis=0).astype(bf)
            if tall:
                rows = [s_ref[c, q, now, plain + k].astype(f32) for c in range(2) for k in range(4)]
                outs[1][q] = jnp.concatenate(rows, axis=0).astype(bf)
            if left:
                rows = [s_ref[c, q, now, plain].astype(f32)[:1] for c in range(2)]
                outs[-1][q] = jnp.concatenate(rows + [jnp.zeros((6, D), f32)], axis=0)

    shapes = [jax.ShapeDtypeStruct((plain, 4 * nz, 2 * r, D), bf)]
    blocks = [pl.BlockSpec((plain, 4, 2 * r, D), lambda i: (0, i, 0, 0))]
    if tall:
        shapes.append(jax.ShapeDtypeStruct((4 * nz, 8 * r, D), bf))
        blocks.append(pl.BlockSpec((4, 8 * r, D), lambda i: (i, 0, 0)))
    if left:
        shapes.append(jax.ShapeDtypeStruct((4 * nz, 8, D), f32))
        blocks.append(pl.BlockSpec((4, 8, D), lambda i: (i, 0, 0)))
    out = pl.pallas_call(
        body,
        name="place_units",
        grid=(nz,),
        out_shape=tuple(shapes),
        in_specs=[pl.BlockSpec(memory_space=pltpu.SMEM)] + [pl.BlockSpec(memory_space=pl.ANY)] * 8,
        out_specs=tuple(blocks),
        scratch_shapes=[pltpu.VMEM((2, 4, nz, n, r, D), bf), pltpu.SemaphoreType.DMA((8, nz))],
        compiler_params=pltpu.CompilerParams(vmem_limit_bytes=60 * 1024 * 1024),
        cost_estimate=pl.CostEstimate(flops=0, bytes_accessed=n * D * D * 4, transcendentals=0),
    )(table, *pieces[0], *pieces[1])
    out = list(out)
    out[0] = out[0].reshape(plain, D, D)
    if tall:
        out[1] = out[1].reshape(4 * D, D)
    return out


def pick(stack, index, axis=0):
    return lax.dynamic_index_in_dim(stack, index, axis, keepdims=False)


def ordered(first, mine, other):
    return jnp.stack([jnp.where(first, mine, other), jnp.where(first, other, mine)])


class Place:
    def __init__(self):
        self.nz = lax.axis_size("dp")
        self.nf = lax.axis_size("fsdp")
        self.nq = self.nf // 2
        self.z = lax.axis_index("dp")
        self.f = lax.axis_index("fsdp")
        self.core = self.f % 2
        self.even = self.core == 0
        self.chip = self.f // 2
        self.group = self.chip % GROUPS

    def sibling(self, x):
        return lax.ppermute(x, "fsdp", [(f, f ^ 1) for f in range(self.nf)])

    def hop(self, x, mask, odd_mask=None):
        odd_mask = mask if odd_mask is None else odd_mask
        route = [(f, f ^ ((odd_mask if f % 2 else mask) << 1)) for f in range(self.nf)]
        return lax.ppermute(x, "fsdp", route)

    def across(self, x, mask):
        return lax.ppermute(x, "dp", [(z, z ^ mask) for z in range(self.nz)])

    def send_line(self, x):
        return [self.across(x, m) for m in range(1, self.nz)]

    def send_terms(self, now):
        return [self.across(pick(now, self.z ^ m), m) for m in range(1, self.nz)]

    def gather_square(self, block, bit):
        a, b = 1 << bit, 2 << bit
        first = self.hop(block, a, b)
        second = self.hop(block, b, a)
        return [block, first, second, self.hop(first, b, a)]

    def first_hop(self, x):
        return self.hop(x, 1, 2)

    def second_hop(self, x):
        return self.hop(x, 2, 1)

    def arranged(self, pieces, bit, odd):
        here = (self.chip >> bit) % 4
        stack = jnp.stack(pieces)
        at = [0, 1, 2, 3]
        swapped = jnp.where(odd, jnp.array([0, 2, 1, 3]), jnp.array(at))
        return jnp.stack([pick(stack, swapped[here ^ k]) for k in at])

    def gather_plain(self, block):
        stack = jnp.stack([block] + self.send_line(block))
        now = jnp.stack([pick(stack, self.z ^ k) for k in range(self.nz)])
        levels = 0
        for bit in range(0, self.nq.bit_length() - 1, 2):
            now = self.arranged(self.gather_square(now, bit), bit, ~self.even)
            levels += 1
        now = ordered(self.even, now, self.sibling(now))
        n, r = block.shape[:2]
        now = now.reshape(2, self.nq, self.nz, n, r, D)
        return jnp.transpose(now, (3, 2, 1, 0, 4, 5))

    def chip_terms(self, pairs):
        def parts(i, kind=f32):
            blocks = []
            for pair in pairs:
                along = []
                for keep, other in pair if isinstance(pair[0], (tuple, list)) else [pair]:
                    shape = (4,) + (() if self.nq == 4 else (self.nq // 4,)) + keep.shape[1:]
                    block = pick(keep.reshape(shape), i).astype(f32) + pick(other.reshape(shape), i).astype(f32)
                    along.append((block if self.nq == 4 else jnp.swapaxes(block, 0, 1)).astype(kind))
                blocks.append(along[0] if len(along) == 1 else jnp.concatenate(along))
            return jnp.concatenate(blocks, axis=-3)

        return parts

    def halves(self, x, r):
        x = x.reshape((-1, self.nz, self.nq, 2, r, x.shape[-1]))

        def rows(which):
            return jnp.transpose(pick(x, which, 3), (2, 1, 0, 3, 4))

        return rows(self.core), rows(1 - self.core)

    def square_terms(self, parts):
        bit = (self.nq.bit_length() - 1) - 2
        here = (self.chip >> bit) % 4
        first = jnp.where(self.even, 1, 2)
        masks = (3 - first, jnp.full_like(first, 3), first, jnp.zeros_like(first))
        return [parts(here ^ mask, kind) for mask, kind in zip(masks, (bf, bf, f32, f32))]

    def outer_hop(self, which, x):
        bit = (self.nq.bit_length() - 1) - 2
        a, b = 1 << bit, 2 << bit
        return self.hop(x, a, b) if which == 0 else self.hop(x, b, a)

    def inner_square(self, now):
        if now.ndim > 4:
            first = jnp.where(self.even, 1, 2)
            here = self.chip % 4

            def at(mask):
                return pick(now, here ^ mask, 1).astype(f32)

            second = self.hop(at(3 - first).astype(bf), 2, 1)
            corner = self.hop(at(3).astype(bf), 2, 1)
            moved = self.hop((at(first) + corner.astype(f32)).astype(bf), 1, 2)
            now = (at(0) + moved.astype(f32) + second.astype(f32)).astype(bf)
        return now

    def own_terms(self, now):
        return pick(now, self.z).astype(f32)

    def group_hops(self, x):
        return [self.hop(x, mask) for mask in range(1, GROUPS)]

    def in_order(self, pieces):
        stack = jnp.stack(pieces)
        return jnp.stack([pick(stack, self.group ^ k) for k in range(GROUPS)])

    def to_groups(self, blocks):
        return [self.hop(pick(blocks, self.group ^ mask), mask) for mask in range(1, GROUPS)]

    def owned_rows(self, mine, axis=0):
        own = lax.dynamic_slice_in_dim(mine, self.f * Q_DEV, Q_DEV, axis)
        give = lax.dynamic_slice_in_dim(mine, (self.f ^ 1) * Q_DEV, Q_DEV, axis)
        return ordered(self.even, own, self.sibling(give))


def tie(*arrays):
    return lax.optimization_barrier(arrays)


def stage(*moves):
    operands = tie(*[operand for _, operand in moves])
    return tie(*[move(operand) for (move, _), operand in zip(moves, operands)])


def split_three(x):
    hi = lax.reduce_precision(x, 8, 7)
    mid = lax.reduce_precision(x - hi, 8, 7)
    return [hi.astype(bf), mid.astype(bf), (x - hi - mid).astype(bf)]


def join_three(x):
    a, b, c = jnp.split(x.astype(f32), 3, axis=-1)
    return (a + b) + c


def columns(weight):
    rows, width = weight.shape
    return [weight[:, k * D : (k + 1) * D] for k in range(width // D)]


def strip_bias(place, bands, height):
    half = WIN // 2
    rows = (place.f % bands) * height + jnp.arange(height, dtype=jnp.int32)
    cols = (place.f // bands) * WIN + jnp.arange(WIN, dtype=jnp.int32)

    def label(at, total):
        return (at >= total - WIN).astype(jnp.int32) + (at >= total - half).astype(jnp.int32)

    labels = label(rows, height * bands)[:, None] * 3 + label(cols, WIN * WCOLS)
    labels = labels.reshape(height // WIN, PATCH)
    return jnp.where(labels[:, :, None] == labels[:, None, :], 0.0, -1e30).astype(f32)


def roll_beside(x, place, bands):
    route = [((f + bands) % place.nf, f) for f in range(place.nf)]
    return lax.ppermute(x, "fsdp", route)


def roll_in(x, beside, place, bands):
    half = WIN // 2
    pages, height = x.shape[:2]
    if bands > 1:
        x = jnp.concatenate([x[:, :, half:], beside.reshape(pages, height, half, D)], axis=2)
        route = [(f // bands * bands + (f + 1) % bands, f) for f in range(place.nf)]
        below = lax.ppermute(x[:, :half], "fsdp", route)
        return jnp.concatenate([x[:, half:], below], axis=1).reshape(-1, D)

    def body(x_ref, b_ref, out_ref, tall_ref, side_ref):
        side_ref[...] = b_ref[...].astype(f32)
        for to in range(height):
            row = (to + half) % height
            tall_ref[to * WIN : to * WIN + half] = x_ref[0, row].astype(f32)[half:]
            tall_ref[to * WIN + half : (to + 1) * WIN] = side_ref[row * half : (row + 1) * half]
        out_ref[...] = tall_ref[...].astype(bf)

    return call(
        body,
        "roll_in",
        sds((pages * height * WIN, D), bf),
        [per_page((1, height, WIN, D), 0), per_page((height * half, D), 0)],
        per_page((height * WIN, D), 0),
        (pages,),
        (x, beside),
        scratch=(pltpu.VMEM((height * WIN, D), f32), pltpu.VMEM((height * half, D), f32)),
        flops=1 << 20,
    )


def last_columns(x):
    half = WIN // 2
    height = x.shape[0] // MICRO // WIN

    def body(x_ref, out_ref, tall_ref, side_ref):
        tall_ref[...] = x_ref[...].astype(f32)
        for row in range(height):
            side_ref[row * half : (row + 1) * half] = tall_ref[row * WIN + half : (row + 1) * WIN]
        out_ref[...] = side_ref[...].astype(bf)

    return call(
        body,
        "last_columns",
        sds((MICRO * height * half, D), bf),
        [per_page((height * WIN, D), 0)],
        per_page((height * half, D), 0),
        (MICRO,),
        (x,),
        (pltpu.VMEM((height * WIN, D), f32), pltpu.VMEM((height * half, D), f32)),
    )


def roll_out(x, beside, place, bands):
    half = WIN // 2
    height = x.shape[0] // MICRO // WIN
    shape = (MICRO, height, WIN, D)
    if bands > 1:
        x = jnp.concatenate([beside.reshape(MICRO, height, half, D), x.reshape(shape)[:, :, :half]], axis=2)
        rows = [(f, f // bands * bands + (f + 1) % bands) for f in range(place.nf)]
        above = lax.ppermute(x[:, -half:], "fsdp", rows)
        return jnp.concatenate([above, x[:, :-half]], axis=1)

    def body(x_ref, b_ref, out_ref, tall_ref, side_ref):
        tall_ref[...] = x_ref[...].astype(f32)
        side_ref[...] = b_ref[...].astype(f32)
        for row in range(height):
            parts = [side_ref[row * half : (row + 1) * half], tall_ref[row * WIN : row * WIN + half]]
            out_ref[0, (row + half) % height] = jnp.concatenate(parts, axis=0).astype(bf)

    return call(
        body,
        "roll_out",
        sds(shape, bf),
        [per_page((height * WIN, D), 0), per_page((height * half, D), 0)],
        per_page((1,) + shape[1:], 0),
        (MICRO,),
        (x, beside),
        (pltpu.VMEM((height * WIN, D), f32), pltpu.VMEM((height * half, D), f32)),
    )


def local(
    visual,
    query_slots,
    lengths,
    slot_order,
    norm_window,
    window_qkv,
    window_out,
    norm_slots,
    slots_qkv,
    slots_out,
    norm_reader,
    norm_page,
    reader_qkv,
    reader_out,
    writer_qkv,
    writer_out,
    norm_visual_mlp,
    visual_up,
    visual_down,
    norm_query_mlp,
    query_up,
    query_down,
    visual_cot,
    query_cot,
):
    place = Place()
    nz, nf, nq, core, even = place.nz, place.nf, place.nq, place.core, place.even
    extra = nq // GROUPS
    bands = nf // WCOLS
    height = visual.shape[1]
    page_rows = height * WIN
    rows = MICRO * page_rows
    slots = Q_DEV * nf
    r = window_out.shape[0]

    fast = r % 8 == 0 and nq == 4
    gains = jnp.stack([norm_window, norm_slots, norm_reader, norm_page, norm_visual_mlp, norm_query_mlp])
    gains = jnp.zeros((r, D), bf).at[0, : 6 * r].set(gains.reshape(6 * r))
    arrays = (
        window_qkv,
        window_out,
        slots_qkv,
        slots_out,
        reader_qkv,
        reader_out,
        writer_qkv,
        writer_out,
        visual_up,
        visual_down,
        query_up,
        query_down,
    )
    one, two, three, four = pack_rows(place, arrays, gains)

    def squares(x):
        return [place.first_hop(x), place.second_hop(x)]

    def siblings(x):
        return jax.tree.map(place.sibling, x)

    def assemble(block, pieces, others, plain, tall):
        if fast:
            return place_units(place, [pieces, others], plain, tall)
        units = place.gather_plain(block)
        out = [units[:plain].reshape(plain, D, D)]
        if tall:
            out.append(jnp.transpose(units[plain:], (1, 2, 3, 0, 4, 5)).reshape(4 * D, D))
        elif block.shape[0] > plain:
            rows_left = units[plain, ..., 0, :].reshape(nz * nq, 2, D).astype(f32)
            out.append(jnp.pad(rows_left, ((0, 0), (0, 6), (0, 0))))
        return out

    positions = (slot_order[:, :, None] * Q_DEV + jnp.arange(Q_DEV, dtype=jnp.int32)).reshape(MICRO, slots)
    live = jnp.where(positions < lengths[:, None], 0.0, -1e30).astype(f32).reshape(MICRO, 1, slots)
    own_live = pick(live, core)
    bias = strip_bias(place, bands, height)
    chip_id = place.chip.astype(jnp.int32).reshape(1)
    core_id = core.astype(jnp.int32).reshape(1)

    def spread(x, bit):
        return place.hop(x, 1 << bit)

    def spread_order(x, got, bit):
        upper = (place.chip >> bit) % 2 == 1
        return jnp.concatenate([jnp.where(upper, got, x), jnp.where(upper, x, got)], axis=1)

    def all_dp(block, got):
        return jnp.stack([block] + list(got))

    act_block = per_page((page_rows, D), 0)
    three_block = per_page((3, page_rows, D), 1)

    def part_of(size, index, full):
        return full, pl.BlockSpec((size, D, D), lambda *_: (index, 0, 0), pipeline_mode=pl.Buffered(1))

    def run_first(args):
        sib_c, x = args
        w_one, gain_all = assemble(one, [all_one, f_one, s_one, c_one], [sib_one, sib_f_one, sib_s_one, sib_c], 8, 0)
        gain_all = gain_all[:, :2, : 6 * r].reshape(nz * nq * 2, 6, r)
        gain_all = jnp.transpose(gain_all, (1, 0, 2)).reshape(6, 1, D)
        windows = call(
            window_fwd,
            "window_fwd",
            (sds((3, rows, D), bf), sds((rows, D), bf), sds((rows, D), f32)),
            [act_block, whole(bias.shape), whole((1, D)), part_of(4, 0, None)[1]],
            (three_block, act_block, act_block),
            (MICRO,),
            (x, bias, gain_all[0], w_one),
            flops=2 * rows * 4 * D * D,
        )
        return w_one, gain_all, windows

    roll = partial(roll_beside, place=place, bands=bands)
    ends = jnp.stack([query_slots, query_cot])
    got, beside_x, ends_two = stage(
        (place.send_line, one),
        (roll, visual[:, :, : WIN // 2].reshape(-1, D)),
        (place.sibling, pick(ends, 1 - core, 1)),
    )
    all_one = all_dp(one, got)
    ends = jnp.swapaxes(ordered(even, pick(ends, core, 1), ends_two), 0, 1).reshape(2, 2 * Q_DEV, D)
    got, (f_one, s_one) = stage((place.send_line, two), (squares, all_one))
    c_one, ends_two, sib_one, sib_f_one, sib_s_one, x = stage(
        (place.second_hop, f_one),
        (partial(spread, bit=0), ends),
        (place.sibling, all_one),
        (place.sibling, f_one),
        (place.sibling, s_one),
        (lambda args: roll_in(*args, place, bands), (visual, beside_x)),
    )
    ends = spread_order(ends, ends_two, 0)
    sib_c_one, ends_two, got = tie(place.sibling(c_one), spread(ends, 1), got)
    ends = spread_order(ends, ends_two, 1)
    for bit in range(2, nq.bit_length() - 1):
        ends = spread_order(ends, spread(ends, bit), bit)
    xs, xs_cot = ends[0], ends[1]
    all_two = all_dp(two, got)
    got, (f_two, s_two), first = stage(
        (place.send_line, three), (squares, all_two), (run_first, (sib_c_one, x))
    )
    all_three = all_dp(three, got)
    c_two, sib_two, sib_f_two, sib_s_two = stage(
        (place.second_hop, f_two),
        (place.sibling, all_two),
        (place.sibling, f_two),
        (place.sibling, s_two),
    )
    sib_c_two, all_three = tie(place.sibling(c_two), all_three)
    w_one, gain_all, (mix, att, v1) = first
    g_window, g_slots, g_reader, g_page, g_vmlp, g_qmlp = (gain_all[k] for k in range(6))

    def run_second(args):
        sib_c, v1, xs = args
        mix_q, att_q, s1 = simple(
            slots_fwd,
            "slots_fwd",
            (xs, g_slots, part_of(4, 1, w_one), own_live),
            [((3, slots, D), bf), ((slots, D), bf), ((slots, D), f32)],
        )
        (w_two,) = assemble(two, [all_two, f_two, s_two, c_two], [sib_two, sib_f_two, sib_s_two, sib_c], 7, 0)
        (rd_own,) = simple(
            normed_units, "slots_units", (s1, g_reader, part_of(3, 1, w_two)), [((3, slots, D), bf)]
        )
        pk = call(
            normed_units,
            "page_units",
            sds((3, rows, D), bf),
            [act_block, whole((1, D)), part_of(3, 0, None)[1]],
            three_block,
            (MICRO,),
            (v1, g_page, w_two),
            flops=2 * rows * 3 * D * D,
        )
        return w_two, rd_own, pk, mix_q, att_q, s1

    got, (f_three, s_three), (w_two, rd_own, pk, mix_q, att_q, s1) = stage(
        (place.send_line, four), (squares, all_three), (run_second, (sib_c_two, v1, xs))
    )
    rd_two = place.sibling(rd_own)
    rd_two, got = tie(rd_two, got)
    all_four = all_dp(four, got)
    rd = jnp.swapaxes(ordered(even, rd_own, rd_two), 0, 1)
    rq, wk, wv = rd[0], rd[1], rd[2]
    slot_block = per_page((1, slots, D), 0)
    stat_block = per_page((1, slots, 128), 0)

    def of_pk(u):
        return pl.BlockSpec((1, page_rows, D), lambda p: (u, p, 0))

    def merge(terms):
        width = terms[0].shape[-1] // (HEAD + 1) * HEAD
        lse = jnp.stack([t[..., width:] for t in terms])
        top = jnp.max(lse, axis=0)
        weights = jnp.exp(lse - top)
        total = jnp.sum(weights, axis=0)
        shares = weights / total
        out = sum(t[..., :width] * jnp.repeat(share, HEAD, axis=-1) for t, share in zip(terms, shares))
        return jnp.concatenate([out, top + jnp.log(total)], axis=-1)

    def run_read(args):
        return call(
            read_fwd,
            "read_fwd",
            (sds((MICRO, slots, D), f32), sds((MICRO, slots, 128), f32)),
            [slot_block, of_pk(0), of_pk(1)],
            (slot_block, stat_block),
            (MICRO,),
            args,
            flops=2 * rows * slots * D * 4,
        )

    c_three, sib_three, sib_f_three, sib_s_three, (o_part, lse_part) = stage(
        (place.second_hop, f_three),
        (place.sibling, all_three),
        (place.sibling, f_three),
        (place.sibling, s_three),
        (run_read, (rq, pk, pk)),
    )
    terms = jnp.concatenate([o_part, lse_part[..., :HEADS]], axis=-1)
    live_block = per_page((1, 1, slots), 0)

    def run_write(args):
        return call(
            write_fwd,
            "write_fwd",
            (sds((rows, D), bf), sds((rows, D), f32)),
            [act_block, of_pk(2), slot_block, slot_block, live_block, part_of(1, 6, None)[1]],
            (act_block, act_block),
            (MICRO,),
            args,
            flops=2 * rows * D * D,
        )

    terms_two, sib_c_three, beside_cot, (writing, v2) = stage(
        (place.sibling, pick(terms, 1 - core)),
        (place.sibling, c_three),
        (roll, visual_cot[:, :, : WIN // 2].reshape(-1, D)),
        (run_write, (v1, pk, wk, wv, live, w_two)),
    )
    terms = merge([pick(terms, core), terms_two])
    blocks = jnp.concatenate(
        [terms[:, :D].reshape(slots, GROUPS, GCOLS), terms[:, D:].reshape(slots, GROUPS, GHEADS)], axis=-1
    )
    blocks = jnp.swapaxes(blocks, 0, 1)
    got, cot, (w_up, w_down) = stage(
        (place.to_groups, blocks),
        (lambda args: roll_in(*args, place, bands), (visual_cot, beside_cot)),
        (
            lambda sib_c: assemble(
                three, [all_three, f_three, s_three, c_three], [sib_three, sib_f_three, sib_s_three, sib_c], 4, 1
            ),
            sib_c_three,
        ),
    )
    chunk = D
    steps = 2 * D // chunk
    per_unit = D // chunk

    def once(*shape):
        return pl.BlockSpec(shape, lambda j: (0,) * len(shape), pipeline_mode=pl.Buffered(1))

    smem = pl.BlockSpec(memory_space=pltpu.SMEM)
    if fast:
        up_shapes = [sds((nq, nz, 2, r, D), bf)] * 2
        up_outs = [pl.BlockSpec((nq, nz, 1, r, chunk), lambda j: (0, 0, j // per_unit, 0, j % per_unit))] * 2
        several = chunk // (8 * r)
        down_shapes = [sds((nq, nz // 2, 4 * r, D), bf)] * 2
        down_outs = [
            pl.BlockSpec((several, 1, 4 * r, D), lambda j: (j % (nq // several), j // (nq // several), 0, 0))
        ] * 2
    else:
        up_shapes = [sds((2, D, D), bf)]
        up_outs = [pl.BlockSpec((1, D, chunk), lambda j: (j // per_unit, 0, j % per_unit))]
        down_shapes = [sds((2 * D, D), bf)]
        down_outs = [pl.BlockSpec((chunk, D), lambda j: (j, 0))]

    def run_mlp(last, args):
        at = steps if last else 0
        up_in = pl.BlockSpec((1, D, chunk), lambda j: ((j + at) // per_unit, 0, (j + at) % per_unit))
        down_in = pl.BlockSpec((chunk, D), lambda j: (j + at, 0))
        wide = once(rows, D)
        scratch = (pltpu.VMEM((rows, D), bf),)
        if last:
            shapes = [sds((rows, D), bf), sds((rows, D), f32), sds((1, D), f32)]
            outs = [wide, wide, once(1, D)]
            scratch = scratch + (pltpu.VMEM((rows, D), f32), pltpu.VMEM((rows, D), f32))
        else:
            shapes = [sds((rows, D), f32), sds((rows, D), f32)]
            outs = [wide, wide]
        out = call(
            partial(mlp_both, steps, last, 4 * r),
            "mlp_both",
            tuple(shapes + up_shapes + down_shapes),
            [smem, wide, once(1, D), up_in, down_in, wide] + [wide, wide] * last,
            tuple(outs + up_outs + down_outs),
            (steps,),
            (core_id,) + args,
            scratch=scratch,
            flops=2 * rows * 12 * D * D,
        )
        count = len(outs)
        if fast:
            up = out[count : count + 2]
            down = [y.reshape(nq, nz // 2, 4, r, D) for y in out[count + 2 :]]
        else:
            up = place.halves(out[count], r)
            d = out[count + 1].reshape(nz // 2, nq, 2, 4, r, D)
            down = [jnp.swapaxes(pick(d, which, 2), 0, 1) for which in (core, 1 - core)]
        return tuple(out[:count]) + (list(up), list(down))

    def run_grads(body, name, shapes, specs, outs, args, units, scratch, flops):
        if fast:
            unit_shapes = [sds((nq, nz, units, r, D), bf)] * 2
        else:
            unit_shapes = [sds((units, D, D), bf)]
        unit_outs = [whole(y.shape) for y in unit_shapes]
        out = call(
            body,
            name,
            tuple(shapes + unit_shapes),
            [smem] + specs,
            tuple(outs + unit_outs),
            (MICRO,),
            (core_id,) + args,
            scratch=scratch,
            flops=flops,
        )
        count = len(outs)
        if fast:
            pair = list(out[count:])
        else:
            pair = list(place.halves(out[count], r))
        return tuple(out[:count]) + (pair,)

    reading = merge([pick(blocks, place.group)] + list(got))
    for bit in range(2, nq.bit_length() - 1):
        reading = merge([reading, place.hop(reading, 1 << bit)])
    message = jnp.concatenate([reading[:, :GCOLS].astype(bf)] + split_three(reading[:, GCOLS:]), axis=-1)
    reads, (f_four, s_four), (y, dxn, up_one, down_one) = stage(
        (place.group_hops, message),
        (squares, all_four),
        (partial(run_mlp, False), (v2, g_vmlp, w_up, w_down, cot)),
    )
    c_four, sib_four, sib_f_four, sib_s_four, (v3, dv2, dg_vmlp, up_two, down_two) = stage(
        (place.second_hop, f_four),
        (place.sibling, all_four),
        (place.sibling, f_four),
        (place.sibling, s_four),
        (partial(run_mlp, True), (v2, g_vmlp, w_up, w_down, cot, y, dxn)),
    )
    reads = place.in_order([message] + list(reads))
    lse_page = jnp.swapaxes(reads[..., GCOLS:], 0, 1).reshape(slots, 3 * HEADS)
    read_q = jnp.swapaxes(reads[..., :GCOLS], 0, 1).reshape(slots, D)

    def run_write_bwd(args):
        return run_grads(
            write_bwd,
            "write_bwd",
            [sds((rows, D), bf), sds((MICRO, slots, D), bf), sds((MICRO, slots, D), bf)],
            [act_block, act_block, of_pk(2), slot_block, slot_block, live_block, part_of(1, 6, None)[1]],
            [act_block, slot_block, slot_block],
            args,
            1,
            (pltpu.VMEM((D, D), f32),),
            4 * rows * D * D,
        )

    sib_c_four, *net_got, (dwq, dwk, dwv, pair_wo) = stage(
        (place.sibling, c_four),
        (place.sibling, up_one[1]),
        (place.sibling, up_two[1]),
        (place.sibling, down_one[1]),
        (place.sibling, down_two[1]),
        (run_write_bwd, (dv2, writing, pk, wk, wv, live, w_two)),
    )
    down_pairs = [(down_one[0], net_got[2]), (down_two[0], net_got[3])]
    second, corner, first, own_net = place.square_terms(
        place.chip_terms([(up_one[0], net_got[0]), (up_two[0], net_got[1]), down_pairs])
    )

    def run_query(args):
        units, w_down = assemble(
            four, [all_four, f_four, s_four, c_four], [sib_four, sib_f_four, sib_s_four, sib_c_four], 5, 1
        )
        s1, read_q = args
        up_block = pl.BlockSpec((4, D, D), lambda *_: (0, 0, 0), pipeline_mode=pl.Buffered(1))
        return simple(
            partial(query_mlp, 2 * r, D // nz),
            "query_mlp",
            (chip_id, core_id, s1, read_q, part_of(1, 4, units), g_qmlp, (units, up_block), w_down, xs_cot),
            [((slots, D), bf), ((slots, D), f32), ((slots, D), bf), ((1, D), f32)]
            + chip_shapes(5, r)
            + chip_shapes(1, 4 * r),
        )

    def chip_shapes(k, r):
        return [((nz, k, r, D), bf)] * 2 if fast else [((k, nz * 2 * r, D), bf)]

    def chip_pair(outs, r):
        if fast:
            return list(outs)
        x = outs[0].reshape(-1, nz, 2, r, D)
        return [jnp.swapaxes(pick(x, which, 2), 0, 1) for which in (core, 1 - core)]

    second, corner, (q_out, ds2, d_read, dg_qmlp, *d_early) = stage(
        (partial(place.outer_hop, 1), second.astype(bf)),
        (partial(place.outer_hop, 1), corner.astype(bf)),
        (run_query, (s1, read_q)),
    )
    own_net = own_net + second.astype(f32)
    first = (first + corner.astype(f32)).astype(bf)

    count = len(d_early) // 2
    pairs = zip(chip_pair(d_early[:count], r), chip_pair(d_early[count:], 4 * r))
    keep_early, give_early = (jnp.concatenate([a, b.reshape(nz, 4, r, D)], axis=1) for a, b in pairs)
    three_parts = jnp.concatenate([d_read, read_q, lse_page], axis=-1)
    parts_two, early_got = stage((place.sibling, three_parts), (place.sibling, give_early))
    three_parts = ordered(even, three_parts, parts_two)
    d_read_all, read_all = three_parts[..., :D], three_parts[..., D : 2 * D]
    lse_all = join_three(three_parts[..., 2 * D :].reshape(MICRO, slots, GROUPS, 3 * GHEADS))
    lse_all = jnp.pad(lse_all.reshape(MICRO, slots, HEADS), ((0, 0), (0, 0), (0, 128 - HEADS)))
    early = (keep_early.astype(f32) + early_got.astype(f32)).astype(bf)
    early_sum = lax.psum_scatter(early.reshape(nz, 9 * r, D), "dp", scatter_dimension=0).reshape(9, r, D)
    early_sum = early_sum.astype(f32)

    def run_read_bwd(args):
        return call(
            read_bwd,
            "read_bwd",
            (sds((MICRO, slots, D), bf), sds((rows, D), bf), sds((rows, D), bf)),
            [slot_block, of_pk(0), of_pk(1), slot_block, slot_block, stat_block],
            (slot_block, act_block, act_block),
            (MICRO,),
            args,
            flops=2 * rows * slots * D * 10,
        )

    drq, dk, dv = run_read_bwd((rq, pk, pk, d_read_all, read_all, lse_all))

    def run_page_bwd(args):
        return run_grads(
            page_bwd,
            "page_bwd",
            [sds((rows, D), f32), sds((1, D), f32)],
            [act_block, act_block, act_block, act_block, act_block, whole((1, D)), whole((3, D, D))],
            [act_block, whole((1, D))],
            args,
            3,
            (pltpu.VMEM((3, D, D), f32), pltpu.VMEM((1, D), f32)),
            2 * rows * 6 * D * D,
        )

    d_slots = jnp.stack([drq, dwk, dwv], axis=1)
    slots_two, first, (dv1, dg_page, pair_page) = stage(
        (place.sibling, pick(d_slots, 1 - core)),
        (partial(place.outer_hop, 0), first),
        (run_page_bwd, (v1, dv2, dk, dv, dwq, g_page, w_two)),
    )
    own_net = place.inner_square((own_net + first.astype(f32)).astype(bf))
    net_sum = lax.psum_scatter(own_net.reshape(nz, 8 * r, D), "dp", scatter_dimension=0).reshape(8, r, D)
    d_slots = (pick(d_slots, core).astype(f32) + slots_two.astype(f32)).astype(bf)
    d_slots = jnp.transpose(d_slots.reshape(3, slots, GROUPS, GCOLS), (2, 0, 1, 3))

    def run_window_bwd(page, args):
        here = pl.BlockSpec((page_rows, D), lambda i: (page, 0))
        three_here = pl.BlockSpec((3, page_rows, D), lambda i: (0, page, 0))
        return pl.pallas_call(
            window_bwd,
            name="window_bwd",
            out_shape=sds((3, rows, D), bf),
            grid=(1,),
            in_specs=[here, three_here, here, whole(bias.shape), part_of(4, 0, None)[1]]
            + [pl.BlockSpec(memory_space=pl.ANY)] * page,
            out_specs=three_here,
            scratch_shapes=(pltpu.VMEM((page_rows, D), bf),),
            input_output_aliases={5: 0} if page else {},
            compiler_params=pltpu.CompilerParams(vmem_limit_bytes=58 * 1024 * 1024),
            cost_estimate=pl.CostEstimate(flops=rows * 2 * D * D, bytes_accessed=1 << 20, transcendentals=0),
        )(*args)

    page_got, got, dmix = stage(
        (siblings, [pair_page[1], pair_wo[1]]),
        (place.to_groups, d_slots),
        (partial(run_window_bwd, 0), (dv1, mix, att, bias, w_one)),
    )
    d_rd = sum(x.astype(f32) for x in [pick(d_slots, place.group)] + list(got)).astype(bf)
    for bit in range(2, nq.bit_length() - 1):
        d_rd = (d_rd.astype(f32) + place.hop(d_rd, 1 << bit).astype(f32)).astype(bf)
    second, corner, first, own_page = place.square_terms(
        place.chip_terms([(pair_page[0], page_got[0]), (pair_wo[0], page_got[1])])
    )
    rds, second, corner, dmix = stage(
        (place.group_hops, d_rd),
        (partial(place.outer_hop, 1), second.astype(bf)),
        (partial(place.outer_hop, 1), corner.astype(bf)),
        (partial(run_window_bwd, 1), (dv1, mix, att, bias, w_one, dmix)),
    )
    own_page = own_page + second.astype(f32)
    first = (first + corner.astype(f32)).astype(bf)
    d_rd = jnp.transpose(place.in_order([d_rd] + list(rds)), (1, 2, 0, 3)).reshape(3, slots, D)

    def run_query_back(args):
        return simple(
            partial(query_back, 2 * r, D // nz),
            "query_back",
            (*args[:7], part_of(3, 1, args[7]), part_of(4, 1, args[8]), *args[9:]),
            [((slots, D), bf), ((1, D), f32), ((1, D), f32)] + chip_shapes(7, r),
            scratch=(pltpu.VMEM((3, slots, D), bf),),
        )

    def run_window_grads(args):
        return run_grads(
            window_grads,
            "window_grads",
            [],
            [act_block, act_block, three_block, act_block, whole((1, D))],
            [],
            args,
            4,
            (pltpu.VMEM((4, D, D), f32),),
            2 * rows * 4 * D * D,
        )

    first, (pair_window,) = stage(
        (partial(place.outer_hop, 0), first), (run_window_grads, (dv1, x, dmix, att, g_window))
    )
    pair_window, net_sum, early_sum = tie(pair_window, net_sum, early_sum)
    own_page = place.inner_square((own_page + first.astype(f32)).astype(bf))
    (window_got,) = stage((place.sibling, pair_window[1]))
    second, corner, first, own_window = place.square_terms(place.chip_terms([(pair_window[0], window_got)]))
    second, corner, page_passed, (x_grad, dg_slots, dg_reader, *d_late) = stage(
        (partial(place.outer_hop, 1), second.astype(bf)),
        (partial(place.outer_hop, 1), corner.astype(bf)),
        (place.send_terms, own_page),
        (
            run_query_back,
            (chip_id, core_id, xs, s1, ds2, d_rd, g_reader, w_two, w_one, mix_q, att_q, own_live, g_slots),
        ),
    )
    own_window = own_window + second.astype(f32)
    first = (first + corner.astype(f32)).astype(bf)
    keep_late, give_late = chip_pair(d_late, r)

    def run_window_end(args):
        return call(
            window_end,
            "window_end",
            (sds((rows, D), bf), sds((1, D), f32)),
            [act_block, act_block, three_block, whole((1, D)), part_of(4, 0, None)[1]],
            (act_block, whole((1, D))),
            (MICRO,),
            args,
            scratch=(pltpu.VMEM((1, D), f32),),
            flops=2 * rows * 3 * D * D,
        )

    def run_ends(args):
        v3, *rest = args
        v_grad, dg_window = run_window_end(rest)
        return v_grad, dg_window, last_columns(v3), last_columns(v_grad)

    first, late_got, (v_grad, dg_window, side_out, side_grad) = stage(
        (partial(place.outer_hop, 0), first),
        (place.sibling, give_late),
        (run_ends, (v3, dv1, x, dmix, g_window, w_one)),
    )
    own_window = place.inner_square((own_window + first.astype(f32)).astype(bf))
    late = (keep_late.astype(f32) + late_got.astype(f32)).astype(bf)
    last = jnp.concatenate([own_window, late], axis=1)

    def right(x):
        return lax.ppermute(x, "fsdp", [(f, (f + bands) % nf) for f in range(nf)])

    own_gains = jnp.concatenate([dg_window, dg_page, dg_vmlp])
    query_gains = jnp.concatenate([dg_slots, dg_reader, dg_qmlp])
    (chip_gains,) = stage((lambda x: [place.hop(x, mask) for mask in range(1, nq)], own_gains))
    gain_rows = jnp.concatenate([own_gains + sum(chip_gains), query_gains]).reshape(6, nz, nq, 2, r)
    gain_rows = pick(gain_rows, place.chip, 2)
    last_terms = [pick(last, place.z ^ m) for m in range(1, nz)]
    count = max(nz // 2, 1)
    passed_one, side_out, side_grad, gains_two = stage(
        (lambda xs: [place.across(x, m + 1) for m, x in enumerate(xs)], last_terms[:count]),
        (right, side_out),
        (right, side_grad),
        (place.sibling, pick(gain_rows, 1 - core, 2)),
    )
    gain_rows = jnp.swapaxes(pick(gain_rows, core, 2) + gains_two, 0, 1)
    passed_two, gains_passed, visual_out, visual_grad = stage(
        (lambda xs: [place.across(x, m + 1 + count) for m, x in enumerate(xs)], last_terms[count:]),
        (place.send_terms, gain_rows),
        (lambda args: roll_out(*args, place, bands), (v3, side_out)),
        (lambda args: roll_out(*args, place, bands), (v_grad, side_grad)),
    )
    last_sum = place.own_terms(last) + sum(y.astype(f32) for y in list(passed_one) + list(passed_two))
    grad_win, late_sum = last_sum[:4], last_sum[4:]
    both = place.own_terms(gain_rows) + sum(gains_passed)
    q_out, x_grad, net_sum, early_sum, own_page, page_passed, _ = tie(
        q_out, x_grad, net_sum, early_sum, own_page, page_passed, passed_one
    )
    grad_page = place.own_terms(own_page) + sum(y.astype(f32) for y in page_passed)

    query_out = place.owned_rows(q_out)
    query_grad = place.owned_rows(x_grad)

    grad_up = net_sum[:4].astype(f32)
    grad_down = net_sum[4:].reshape(4 * r, D).astype(f32)
    grad_qup = jnp.concatenate([early_sum[k] for k in range(4)], axis=1)
    grad_ro = early_sum[4]
    grad_qdown = early_sum[5:].reshape(4 * r, D)
    grad_sq = jnp.concatenate([late_sum[k] for k in range(3)], axis=1)
    grad_so = late_sum[3]
    grad_rd = jnp.concatenate([late_sum[4 + k] for k in range(3)], axis=1)

    def wide(units):
        return jnp.concatenate([units[k] for k in range(units.shape[0])], axis=1)

    return (
        visual_out,
        query_out,
        visual_grad,
        query_grad,
        both[0],
        wide(grad_win[:3]),
        grad_win[3],
        both[3],
        grad_sq,
        grad_so,
        both[4],
        both[1],
        jnp.concatenate([grad_rd[:, :D], wide(grad_page[:2])], axis=1),
        grad_ro,
        jnp.concatenate([grad_page[2], grad_rd[:, D:]], axis=1),
        grad_page[3],
        both[2],
        wide(grad_up),
        grad_down,
        both[5],
        grad_qup,
        grad_qdown,
    )


def solution(mesh):
    page = P("dp", "fsdp", None, None)
    slot = P("dp", "fsdp", None)
    gain = P(("dp", "fsdp"))
    matrix = P(("dp", "fsdp"), None)
    weights = (
        gain,
        matrix,
        matrix,
        gain,
        matrix,
        matrix,
        gain,
        gain,
        matrix,
        matrix,
        matrix,
        matrix,
        gain,
        matrix,
        matrix,
        gain,
        matrix,
        matrix,
    )
    return jax.shard_map(
        local,
        mesh=mesh,
        in_specs=(page, slot, P("dp"), P("dp", None)) + weights + (page, slot),
        out_specs=(page, slot, page, slot) + weights,
        check_vma=False,
    )
```

```python
from functools import partial

import jax
import jax.numpy as jnp
from jax import lax
from jax.experimental import pallas as pl
from jax.experimental.pallas import tpu as pltpu
from jax.sharding import PartitionSpec as P

D = 768
HEADS = 12
HEAD = 64
WIN = 12
WCOLS = 8
Q_DEV = 16
MICRO = 2
PATCH = WIN * WIN
PAIRS = HEADS // 2
GROUPS = 4
GHEADS = HEADS // GROUPS
GCOLS = GHEADS * HEAD
SCALE = HEAD ** (-0.5)

bf = jnp.bfloat16
f32 = jnp.float32


def dot(a, b):
    return lax.dot_general(a, b, (((1,), (0,)), ((), ())), preferred_element_type=f32)


def dot_t(a, b):
    return lax.dot_general(a, b, (((1,), (1,)), ((), ())), preferred_element_type=f32)


def t_dot(a, b):
    return lax.dot_general(a, b, (((0,), (0,)), ((), ())), preferred_element_type=f32)


def normalise(x):
    centred = x - jnp.mean(x, axis=-1, keepdims=True)
    inv = lax.rsqrt(jnp.mean(centred * centred, axis=-1, keepdims=True) + 1e-05)
    return centred * inv, inv


def norm_back(grad, hat, inv, gain):
    scaled = grad * gain
    mean_one = jnp.mean(scaled, axis=-1, keepdims=True)
    mean_two = jnp.mean(scaled * hat, axis=-1, keepdims=True)
    return inv * (scaled - mean_one - hat * mean_two), jnp.sum(grad * hat, axis=0, keepdims=True)


def gelu_both(u):
    k = 0.7978845608028654
    t = jnp.tanh(k * (u + 0.044715 * u * u * u))
    slope = 0.5 * (1.0 + t) + 0.5 * u * (1.0 - t * t) * k * (1.0 + 3 * 0.044715 * u * u)
    return 0.5 * u * (1.0 + t), slope


def low_lanes(rows):
    return lax.broadcasted_iota(jnp.int32, (rows, 2 * HEAD), 1) < HEAD


def twofold(pair, mask):
    zero = jnp.zeros_like(pair)
    return jnp.concatenate([jnp.where(mask, pair, zero), jnp.where(mask, zero, pair)], axis=0)


def onefold(stacked, mask):
    rows = stacked.shape[0] // 2
    return jnp.where(mask, stacked[:rows], stacked[rows:])


def groups_of_pairs(q_rows, k_rows):
    together = max(1, min(PAIRS, 700000 // (2 * q_rows * k_rows)))
    return [range(p, min(p + together, PAIRS)) for p in range(0, PAIRS, together)]


def lanes(p):
    return slice(p * 2 * HEAD, (p + 1) * 2 * HEAD)


def scaled(q2, mask):
    return twofold(q2 * jnp.asarray(SCALE, bf), mask)


def pairs_forward(q, k, v, bias):
    mask = low_lanes(q[0].shape[0])
    s = [dot_t(scaled(q2, mask), k2) for q2, k2 in zip(q, k)]
    if bias is not None:
        s = [x + bias for x in s]
    m = [jnp.max(x, axis=-1, keepdims=True) for x in s]
    e = [jnp.exp(x - top) for x, top in zip(s, m)]
    l = [jnp.sum(x, axis=-1, keepdims=True) for x in e]
    out = [dot(x.astype(bf), v2) for x, v2 in zip(e, v)]
    return [(onefold(x / total, mask), top, total) for x, top, total in zip(out, m, l)]


def pairs_backward(q, k, v, d, a, bias, lse=None):
    mask = low_lanes(q[0].shape[0])
    qs = [scaled(q2, mask) for q2 in q]
    ds = [twofold(d2, mask) for d2 in d]
    s = [dot_t(q2, k2) for q2, k2 in zip(qs, k)]
    dp = [dot_t(d2, v2) for d2, v2 in zip(ds, v)]
    corr = [
        jnp.sum(d2.astype(f32) * twofold(a2, mask).astype(f32), axis=-1, keepdims=True) for d2, a2 in zip(ds, a)
    ]
    if bias is not None:
        s = [x + bias for x in s]
    if lse is None:
        e = [jnp.exp(x - jnp.max(x, axis=-1, keepdims=True)) for x in s]
        p = [x * (1.0 / jnp.sum(x, axis=-1, keepdims=True)) for x in e]
    else:
        p = [jnp.exp(x - y) for x, y in zip(s, lse)]
    dsc = [(x * (y - c)).astype(bf) for x, y, c in zip(p, dp, corr)]
    dq = [onefold(dot(x, k2), mask) * SCALE for x, k2 in zip(dsc, k)]
    dk = [t_dot(x, q2) for x, q2 in zip(dsc, qs)]
    dv = [t_dot(x.astype(bf), d2) for x, d2 in zip(p, ds)]
    return list(zip(dq, dk, dv))


def call(body, name, out_shape, in_specs, out_specs, grid, args, scratch=(), flops=0):
    return pl.pallas_call(
        body,
        name=name,
        out_shape=out_shape,
        grid=grid,
        in_specs=in_specs,
        out_specs=out_specs,
        scratch_shapes=scratch,
        compiler_params=pltpu.CompilerParams(vmem_limit_bytes=58 * 1024 * 1024),
        cost_estimate=pl.CostEstimate(flops=flops, bytes_accessed=1 << 20, transcendentals=0),
    )(*args)


def whole(shape):
    zeros = (0,) * len(shape)
    return pl.BlockSpec(shape, lambda *_: zeros, pipeline_mode=pl.Buffered(1))


def per_page(shape, axis):
    def place(p):
        return tuple(p if k == axis else 0 for k in range(len(shape)))

    return pl.BlockSpec(shape, place)


def sds(shape, dtype):
    return jax.ShapeDtypeStruct(shape, dtype)


def window_fwd(x_ref, bias_ref, gw_ref, w_ref, mix_ref, att_ref, v1_ref):
    rows = x_ref.shape[0]
    x = x_ref[...].astype(f32)
    xn = (normalise(x)[0] * gw_ref[...]).astype(bf)
    for u in range(3):
        mix_ref[u] = dot(xn, w_ref[u]).astype(bf)

    def window(w, carry):
        at = pl.ds(pl.multiple_of(w * PATCH, 16), PATCH)
        bias = bias_ref[w]
        bias = jnp.concatenate([bias, bias], axis=0)
        for group in groups_of_pairs(PATCH, PATCH):
            cs = [lanes(p) for p in group]
            outs = pairs_forward(*([mix_ref[u, at, c] for c in cs] for u in range(3)), bias)
            for c, (out, _, _) in zip(cs, outs):
                att_ref[at, c] = out.astype(bf)
        return carry

    lax.fori_loop(0, rows // PATCH, window, 0)
    v1_ref[...] = x_ref[...].astype(f32) + dot(att_ref[...], w_ref[3])


def normed_units(x_ref, g_ref, w_ref, out_ref):
    xn = (normalise(x_ref[...])[0] * g_ref[...]).astype(bf)
    for u in range(3):
        out_ref[u] = dot(xn, w_ref[u]).astype(bf)


def read_fwd(rq_ref, k_ref, v_ref, o_ref, lse_ref):
    slots = rq_ref.shape[1]
    lane = lax.broadcasted_iota(jnp.int32, (slots, 128), 1)
    acc = jnp.zeros((slots, 128), f32)
    for group in groups_of_pairs(slots, k_ref.shape[1]):
        cs = [lanes(p) for p in group]
        outs = pairs_forward(*([ref[0, :, c] for c in cs] for ref in (rq_ref, k_ref, v_ref)), None)
        for p, c, (out, m, l) in zip(group, cs, outs):
            o_ref[0, :, c] = out
            lse = m + jnp.log(l)
            acc = jnp.where(lane == 2 * p, lse[:slots], acc)
            acc = jnp.where(lane == 2 * p + 1, lse[slots:], acc)
    lse_ref[0] = acc


def write_fwd(v1_ref, wq_ref, wk_ref, wv_ref, bias_ref, wo_ref, wr_ref, v2_ref):
    for group in groups_of_pairs(wq_ref.shape[1], wk_ref.shape[1]):
        cs = [lanes(p) for p in group]
        outs = pairs_forward(*([ref[0, :, c] for c in cs] for ref in (wq_ref, wk_ref, wv_ref)), bias_ref[0])
        for c, (out, _, _) in zip(cs, outs):
            wr_ref[:, c] = out.astype(bf)
    v2_ref[...] = v1_ref[...] + dot(wr_ref[...], wo_ref[0])


def mlp_both(steps, last, rows_of_core, core_ref, x_ref, g_ref, up_ref, down_ref, cot_ref, *refs):
    if last:
        y_in_ref, dxn_in_ref, out_ref, dx_ref, dg_ref = refs[:5]
        refs = refs[5:]
        xn_ref, y_ref, dxn_ref = refs[-3:]
        outs = refs[:-3]
    else:
        y_ref, dxn_ref = refs[:2]
        xn_ref = refs[-1]
        outs = refs[2:-1]
    half = len(outs) // 2
    j = pl.program_id(0)

    @pl.when(j == 0)
    def _():
        xn_ref[...] = (normalise(x_ref[...])[0] * g_ref[...]).astype(bf)

    xn = xn_ref[...]
    cot = cot_ref[...]
    up = up_ref[0]
    down = down_ref[...]
    act, slope = gelu_both(dot(xn, up))
    act = act.astype(bf)
    y = dot(act, down)
    dpre = (dot_t(cot, down) * slope).astype(bf)
    dxn = dot_t(dpre, up)
    emit_unit(core_ref, t_dot(xn, dpre), outs[:half], 0)
    d_down = t_dot(act, cot)
    if half == 1:
        outs[1][...] = d_down.astype(bf)
    else:
        span = 2 * rows_of_core
        for i in range(d_down.shape[0] // span):
            emit(core_ref, d_down[i * span : (i + 1) * span], outs[2], outs[3], (i, 0))

    @pl.when(j == 0)
    def _():
        y_ref[...] = y_in_ref[...] + y if last else y
        dxn_ref[...] = dxn_in_ref[...] + dxn if last else dxn

    @pl.when(j > 0)
    def _():
        y_ref[...] += y
        dxn_ref[...] += dxn

    if last:

        @pl.when(j == steps - 1)
        def _():
            x = x_ref[...]
            out_ref[...] = (x + y_ref[...]).astype(bf)
            hat, inv = normalise(x)
            dx, dg = norm_back(dxn_ref[...], hat, inv, g_ref[...])
            dx_ref[...] = cot_ref[...].astype(f32) + dx
            dg_ref[...] = dg


def write_bwd(core_ref, dv2_ref, wr_ref, wq_ref, wk_ref, wv_ref, bias_ref, wo_ref, dwq_ref, dwk_ref, dwv_ref, *refs):
    outs, acc_ref = refs[:-1], refs[-1]
    page = pl.program_id(0)
    d = dv2_ref[...].astype(bf)
    dwr = dot_t(d, wo_ref[0]).astype(bf)
    part = t_dot(wr_ref[...], d)

    @pl.when(page == 0)
    def _():
        acc_ref[...] = part

    @pl.when(page > 0)
    def _():
        acc_ref[...] += part

    @pl.when(page == pl.num_programs(0) - 1)
    def _():
        emit_unit(core_ref, acc_ref[...], outs, 0)

    for group in groups_of_pairs(wq_ref.shape[1], wk_ref.shape[1]):
        cs = [lanes(p) for p in group]
        parts = ([ref[0, :, c] for c in cs] for ref in (wq_ref, wk_ref, wv_ref))
        grads = pairs_backward(*parts, [dwr[:, c] for c in cs], [wr_ref[:, c] for c in cs], bias_ref[0])
        for c, (dq, dk, dv) in zip(cs, grads):
            dwq_ref[:, c] = dq.astype(bf)
            dwk_ref[0, :, c] = dk.astype(bf)
            dwv_ref[0, :, c] = dv.astype(bf)


def read_bwd(rq_ref, k_ref, v_ref, d_ref, r_ref, lse_ref, dq_ref, dk_ref, dv_ref):
    slots = rq_ref.shape[1]
    lse = lse_ref[0].astype(f32)

    def of_head(h):
        at = h // GHEADS * 3 * GHEADS + h % GHEADS
        hi, mid, lo = (lse[:, at + k * GHEADS : at + k * GHEADS + 1] for k in range(3))
        return (hi + mid) + lo

    for group in groups_of_pairs(slots, k_ref.shape[1]):
        cs = [lanes(p) for p in group]
        both = [jnp.concatenate([of_head(2 * p), of_head(2 * p + 1)], axis=0) for p in group]
        parts = ([ref[0, :, c] for c in cs] for ref in (rq_ref, k_ref, v_ref, d_ref, r_ref))
        for c, (dq, dk, dv) in zip(cs, pairs_backward(*parts, None, both)):
            dq_ref[0, :, c] = dq.astype(bf)
            dk_ref[:, c] = dk.astype(bf)
            dv_ref[:, c] = dv.astype(bf)


def emit(core_ref, rows, keep_ref, give_ref, at):
    half = rows.shape[0] // 2
    first, second = rows[:half], rows[half:]
    here = core_ref[0] == 0
    keep_ref[at] = jnp.where(here, first, second).astype(bf)
    give_ref[at] = jnp.where(here, second, first).astype(bf)


def emit_unit(core_ref, unit, outs, u):
    if len(outs) == 1:
        outs[0][u] = unit.astype(bf)
        return
    nq, nz = outs[0].shape[:2]
    span = unit.shape[0] // (nq * nz)
    for z in range(nz):
        for q in range(nq):
            i = z * nq + q
            emit(core_ref, unit[i * span : (i + 1) * span], outs[0], outs[1], (q, z, u))


def page_bwd(core_ref, v1_ref, dv2_ref, dk_ref, dv_ref, dwq_ref, gp_ref, wp_ref, dv1_ref, dg_ref, *refs):
    outs, acc_ref, gacc_ref = refs[:-2], refs[-2], refs[-1]
    page = pl.program_id(0)
    hat, inv = normalise(v1_ref[...])
    pn = (hat * gp_ref[...]).astype(bf)
    grads = (dk_ref, dv_ref, dwq_ref)
    dpn = dot_t(dk_ref[...], wp_ref[0]) + dot_t(dv_ref[...], wp_ref[1]) + dot_t(dwq_ref[...], wp_ref[2])
    dx, dg = norm_back(dpn, hat, inv, gp_ref[...])
    dv1_ref[...] = dv2_ref[...] + dx

    @pl.when(page == 0)
    def _():
        gacc_ref[...] = dg
        for u in range(3):
            acc_ref[u] = t_dot(pn, grads[u][...])

    @pl.when(page > 0)
    def _():
        gacc_ref[...] += dg
        for u in range(3):
            acc_ref[u] += t_dot(pn, grads[u][...])

    @pl.when(page == pl.num_programs(0) - 1)
    def _():
        dg_ref[...] = gacc_ref[...]
        for u in range(3):
            emit_unit(core_ref, acc_ref[u], outs, u)


def window_bwd(dv1_ref, mix_ref, att_ref, bias_ref, w_ref, *refs):
    dmix_ref, datt_ref = refs[-2:]
    rows = att_ref.shape[0]
    datt_ref[...] = dot_t(dv1_ref[...].astype(bf), w_ref[3]).astype(bf)

    def window(w, carry):
        at = pl.ds(pl.multiple_of(w * PATCH, 16), PATCH)
        bias = bias_ref[w]
        bias = jnp.concatenate([bias, bias], axis=0)
        for group in groups_of_pairs(PATCH, PATCH):
            cs = [lanes(p) for p in group]
            parts = ([mix_ref[u, at, c] for c in cs] for u in range(3))
            grads = pairs_backward(*parts, [datt_ref[at, c] for c in cs], [att_ref[at, c] for c in cs], bias)
            for c, grad in zip(cs, grads):
                for u in range(3):
                    dmix_ref[u, at, c] = grad[u].astype(bf)
        return carry

    lax.fori_loop(0, rows // PATCH, window, 0)


def window_grads(core_ref, dv1_ref, x_ref, dmix_ref, att_ref, gw_ref, *refs):
    outs, acc_ref = refs[:-1], refs[-1]
    page = pl.program_id(0)
    xn = (normalise(x_ref[...].astype(f32))[0] * gw_ref[...]).astype(bf)
    d1b = dv1_ref[...].astype(bf)

    @pl.when(page == 0)
    def _():
        for u in range(3):
            acc_ref[u] = t_dot(xn, dmix_ref[u])
        acc_ref[3] = t_dot(att_ref[...], d1b)

    @pl.when(page > 0)
    def _():
        for u in range(3):
            acc_ref[u] += t_dot(xn, dmix_ref[u])
        acc_ref[3] += t_dot(att_ref[...], d1b)

    @pl.when(page == pl.num_programs(0) - 1)
    def _():
        for u in range(4):
            emit_unit(core_ref, acc_ref[u], outs, u)


def window_end(dv1_ref, x_ref, dmix_ref, gw_ref, w_ref, grad_ref, dg_ref, gacc_ref):
    page = pl.program_id(0)
    hat, inv = normalise(x_ref[...].astype(f32))
    dxn = dot_t(dmix_ref[0], w_ref[0]) + dot_t(dmix_ref[1], w_ref[1]) + dot_t(dmix_ref[2], w_ref[2])
    dx, dg = norm_back(dxn.astype(bf).astype(f32), hat, inv, gw_ref[...])
    grad_ref[...] = (dv1_ref[...] + dx).astype(bf)

    @pl.when(page == 0)
    def _():
        gacc_ref[...] = dg

    @pl.when(page > 0)
    def _():
        gacc_ref[...] += dg

    dg_ref[...] = gacc_ref[...]


def slots_fwd(x_ref, g_ref, w_ref, bias_ref, mix_ref, att_ref, s1_ref):
    x = x_ref[...].astype(f32)
    xn = (normalise(x)[0] * g_ref[...]).astype(bf)
    for u in range(3):
        mix_ref[u] = dot(xn, w_ref[u]).astype(bf)
    for group in groups_of_pairs(x.shape[0], x.shape[0]):
        cs = [lanes(p) for p in group]
        outs = pairs_forward(*([mix_ref[u, :, c] for c in cs] for u in range(3)), bias_ref[...])
        for c, (out, _, _) in zip(cs, outs):
            att_ref[:, c] = out.astype(bf)
    s1_ref[...] = x + dot(att_ref[...], w_ref[3])


def own_columns(x, chip, span, step):
    total = x.shape[1]
    count = total // step * span
    row = lax.broadcasted_iota(jnp.int32, (total, count), 0)
    col = lax.broadcasted_iota(jnp.int32, (total, count), 1)
    at = lax.div(col, span) * step + chip * span + lax.rem(col, span)
    return dot(x, jnp.where(row == at, 1.0, 0.0).astype(bf)).astype(bf)


def emit_chip(core_ref, unit, outs, u, r):
    if len(outs) == 1:
        outs[0][u] = unit.astype(bf)
        return
    for z in range(unit.shape[0] // (2 * r)):
        emit(core_ref, unit[z * 2 * r : (z + 1) * 2 * r], outs[0], outs[1], (z, u))


def query_mlp(
    span,
    step,
    chip_ref,
    core_ref,
    s1_ref,
    read_ref,
    wo_ref,
    g_ref,
    up_ref,
    down_ref,
    cot_ref,
    out_ref,
    ds2_ref,
    message_ref,
    dg_ref,
    *outs,
):
    chip = chip_ref[0]
    reads = [read_ref[k] for k in range(GROUPS)]
    reading = jnp.concatenate([x[:, :GCOLS] for x in reads], axis=-1)
    sums = [x[:, GCOLS:] for x in reads] + [jnp.zeros((reading.shape[0], 128 - 3 * HEADS), bf)]
    message_ref[:, D : 2 * D] = reading
    message_ref[:, 2 * D :] = jnp.concatenate(sums, axis=-1)
    split = 2 if len(outs) == 2 and len(outs[0].shape) == 4 else 1
    s2 = s1_ref[...] + dot(reading, wo_ref[0])
    hat, inv = normalise(s2)
    xn = (hat * g_ref[...]).astype(bf)
    x_own = own_columns(xn, chip, span, step)
    cot = cot_ref[...]
    y, dxn = s2, None
    for k in range(4):
        up, down = up_ref[k], down_ref[k * D : (k + 1) * D]
        act, slope = gelu_both(dot(xn, up))
        act = act.astype(bf)
        y = y + dot(act, down)
        dpre = (dot_t(cot, down) * slope).astype(bf)
        part = dot_t(dpre, up)
        dxn = part if dxn is None else dxn + part
        emit_chip(core_ref, t_dot(x_own, dpre), outs[:split], k, span // 2)
        act_own = own_columns(act, chip, 4 * span, 4 * step)
        rows = act_own.shape[1]
        d_down = t_dot(act_own, cot)
        if split == 1:
            outs[1][0, k * rows : (k + 1) * rows] = d_down.astype(bf)
        else:
            part = rows // 8
            for t in range(4):
                both = [d_down[(4 * c + t) * part : (4 * c + t + 1) * part] for c in range(2)]
                emit(core_ref, jnp.concatenate(both, axis=0), outs[0], outs[1], (k, 5 + t))
    out_ref[...] = y.astype(bf)
    dx, dg = norm_back(dxn, hat, inv, g_ref[...])
    ds2 = cot.astype(f32) + dx
    ds2_ref[...] = ds2
    dg_ref[...] = dg
    d2b = ds2.astype(bf)
    message_ref[:, :D] = dot_t(d2b, wo_ref[0]).astype(bf)
    emit_chip(core_ref, t_dot(own_columns(reading, chip, span, step), d2b), outs[:split], 4, span // 2)


def query_back(
    span,
    step,
    chip_ref,
    core_ref,
    x_ref,
    s1_ref,
    ds2_ref,
    d_ref,
    gr_ref,
    wr_ref,
    ws_ref,
    mix_ref,
    att_ref,
    bias_ref,
    gs_ref,
    out_ref,
    dgs_ref,
    dgr_ref,
    *refs,
):
    outs, dmix_ref = refs[:-1], refs[-1]
    chip = chip_ref[0]
    hat, inv = normalise(s1_ref[...])
    rn_own = own_columns((hat * gr_ref[...]).astype(bf), chip, span, step)
    drn = dot_t(d_ref[0], wr_ref[0]) + dot_t(d_ref[1], wr_ref[1]) + dot_t(d_ref[2], wr_ref[2])
    dx, dg = norm_back(drn, hat, inv, gr_ref[...])
    dgr_ref[...] = dg
    for u in range(3):
        emit_chip(core_ref, t_dot(rn_own, d_ref[u]), outs, 4 + u, span // 2)
    ds1 = ds2_ref[...] + dx
    d1b = ds1.astype(bf)
    datt = dot_t(d1b, ws_ref[3]).astype(bf)
    emit_chip(core_ref, t_dot(own_columns(att_ref[...], chip, span, step), d1b), outs, 3, span // 2)
    for group in groups_of_pairs(datt.shape[0], datt.shape[0]):
        cs = [lanes(p) for p in group]
        parts = ([mix_ref[u, :, c] for c in cs] for u in range(3))
        grads = pairs_backward(*parts, [datt[:, c] for c in cs], [att_ref[:, c] for c in cs], bias_ref[...])
        for c, grad in zip(cs, grads):
            for u in range(3):
                dmix_ref[u, :, c] = grad[u].astype(bf)
    hat, inv = normalise(x_ref[...].astype(f32))
    xn_own = own_columns((hat * gs_ref[...]).astype(bf), chip, span, step)
    dxn = dot_t(dmix_ref[0], ws_ref[0]) + dot_t(dmix_ref[1], ws_ref[1]) + dot_t(dmix_ref[2], ws_ref[2])
    dx, dg = norm_back(dxn, hat, inv, gs_ref[...])
    dgs_ref[...] = dg
    out_ref[...] = (ds1 + dx).astype(bf)
    for u in range(3):
        emit_chip(core_ref, t_dot(xn_own, dmix_ref[u]), outs, u, span // 2)


def gain_grad(gain_ref, *pairs):
    total = sum(jnp.sum(grad * weight.astype(f32), axis=-1, keepdims=True) for grad, weight in pairs)
    return total / gain_ref[...].astype(f32)


def own_sum(z, own_ref, passed, u):
    total = own_ref[z, u].astype(f32)
    for ref in passed:
        total = total + ref[u].astype(f32)
    return total


def finish_most(
    nz,
    z_ref,
    net_ref,
    early_ref,
    up_ref,
    qup_ref,
    slots_ref,
    reader_ref,
    writer_ref,
    gp_ref,
    gv_ref,
    gs_ref,
    gr_ref,
    gq_ref,
    page_ref,
    late_ref,
    *refs,
):
    page, late = refs[: nz - 1], refs[nz - 1 : 2 * nz - 2]
    outs = refs[2 * nz - 2 :]
    d_up, d_down, d_qup, d_ro, d_qdown, d_reader, d_writer, d_wo, d_sq, d_so, d_gp, d_gv, d_gs, d_gr, d_gq = outs
    z = z_ref[0]

    def units(ref, start, count):
        return jnp.concatenate([ref[start + k].astype(f32) for k in range(count)], axis=-1)

    up = units(net_ref, 0, 4)
    d_up[...] = up
    d_gv[...] = gain_grad(gv_ref, (up, up_ref[...]))
    qup = units(early_ref, 0, 4)
    d_qup[...] = qup
    d_gq[...] = gain_grad(gq_ref, (qup, qup_ref[...]))
    d_ro[...] = early_ref[4].astype(f32)
    for k in range(4):
        d_down[k] = net_ref[4 + k].astype(f32)
        d_qdown[k] = early_ref[5 + k].astype(f32)
    read_k, read_v, write_q, out = (own_sum(z, page_ref, page, u) for u in range(4))
    sq = jnp.concatenate([own_sum(z, late_ref, late, u) for u in range(3)], axis=-1)
    so, read_q, write_k, write_v = (own_sum(z, late_ref, late, u) for u in range(3, 7))
    d_wo[...] = out
    d_sq[...] = sq
    d_so[...] = so
    d_reader[...] = jnp.concatenate([read_q, read_k, read_v], axis=-1)
    d_writer[...] = jnp.concatenate([write_q, write_k, write_v], axis=-1)
    d_gs[...] = gain_grad(gs_ref, (sq, slots_ref[...]))
    reader, writer = reader_ref[...], writer_ref[...]
    d_gp[...] = gain_grad(gp_ref, (read_k, reader[:, D : 2 * D]), (read_v, reader[:, 2 * D :]), (write_q, writer[:, :D]))
    d_gr[...] = gain_grad(gr_ref, (read_q, reader[:, :D]), (write_k, writer[:, D : 2 * D]), (write_v, writer[:, 2 * D :]))


def finish_windows(z_ref, gain_ref, qkv_ref, own_ref, *refs):
    passed, (d_qkv, d_out, d_gain) = refs[:-3], refs[-3:]
    z = z_ref[0]
    qkv = jnp.concatenate([own_sum(z, own_ref, passed, u) for u in range(3)], axis=-1)
    d_qkv[...] = qkv
    d_out[...] = own_sum(z, own_ref, passed, 3)
    d_gain[...] = gain_grad(gain_ref, (qkv, qkv_ref[...]))


def simple(body, name, args, outs, scratch=()):
    arrays = [a[0] if isinstance(a, tuple) else a for a in args]
    specs = [
        a[1]
        if isinstance(a, tuple)
        else pl.BlockSpec(memory_space=pltpu.SMEM)
        if a.ndim == 1
        else whole(a.shape)
        for a in args
    ]
    return call(
        body,
        name,
        tuple(sds(*o) for o in outs),
        specs,
        tuple(whole(o[0]) for o in outs),
        (1,),
        arrays,
        scratch=scratch,
        flops=1 << 30,
    )


def pack_rows(place, arrays, gains):
    window, out, slots, rows_of_slots, reader, rows_of_reader, writer, rows_of_writer, up, down, qup, qdown = arrays
    r = window.shape[0]

    def units(w):
        return [w[:, k * D : (k + 1) * D] for k in range(w.shape[1] // D)]

    def groups(win, o, sl, so, rd, ro, wr, wo, u, d, qu, qd, g):
        rd, wr = units(rd), units(wr)
        return (
            units(win) + [o] + units(sl) + [so, g],
            rd[1:] + wr[:1] + rd[:1] + wr[1:] + [wo],
            units(u) + [d[k] for k in range(4)],
            units(qu) + [ro] + [qd[k] for k in range(4)],
        )

    down, qdown = down.reshape(4, r, D), qdown.reshape(4, r, D)
    arrays = (window, out, slots, rows_of_slots, reader, rows_of_reader, writer, rows_of_writer, up, down, qup, qdown)
    if r % 8:
        return [jnp.stack(group) for group in groups(*arrays, gains)]

    def body(*refs):
        for group, out_ref in zip(groups(*refs[:13]), refs[13:]):
            for k, w in enumerate(group):
                out_ref[k] = w[...]

    return simple(body, "pack_rows", arrays + (gains,), [((n, r, D), bf) for n in (9, 7, 8, 9)])


def net_terms(place, ups, downs):
    nq, nz, _, r, _ = ups[0][0].shape
    half = nz // 2
    table = jnp.stack([place.core, place.chip]).astype(jnp.int32)

    def body(table_ref, *refs):
        outs = refs[8:]
        z = pl.program_id(0)
        first = jnp.where(table_ref[0] == 0, 1, 2)
        masks = (3 - first, 3, first, 0)
        for mask, out_ref in zip(masks, outs):
            at = jnp.bitwise_xor(table_ref[1], mask)
            for k in range(2):
                a, b = refs[2 * k], refs[2 * k + 1]
                for u in range(2):
                    out_ref[0, 2 * k + u] = (a[at, 0, u].astype(f32) + b[at, 0, u].astype(f32)).astype(bf)
            for k in range(2):
                a, b = refs[4 + 2 * k], refs[5 + 2 * k]

                @pl.when(z // half == k)
                def _():
                    for u in range(4):
                        out_ref[0, 4 + u] = (a[at, 0, u].astype(f32) + b[at, 0, u].astype(f32)).astype(bf)

    def down_block(k):
        return pl.BlockSpec((nq, 1, 4, r, D), lambda z: (0, jnp.clip(z - k * half, 0, half - 1), 0, 0, 0))

    up_block = pl.BlockSpec((nq, 1, 2, r, D), lambda z: (0, z, 0, 0, 0))
    return call(
        body,
        "net_terms",
        (sds((nz, 8, r, D), bf),) * 4,
        [pl.BlockSpec(memory_space=pltpu.SMEM)] + [up_block] * 4 + [down_block(0)] * 2 + [down_block(1)] * 2,
        (pl.BlockSpec((1, 8, r, D), lambda z: (z, 0, 0, 0)),) * 4,
        (nz,),
        (table, *ups[0], *ups[1], *downs[0], *downs[1]),
    )


def place_units(place, pieces, plain, tall):
    nz, n, r = pieces[0][0].shape[:3]
    left = n - plain - 4 * tall
    table = jnp.stack([place.core, place.chip % 4, place.z]).astype(jnp.int32)

    def body(table_ref, *args):
        refs, outs, (s_ref, sem) = args[:8], args[8:-2], args[-2:]
        core, chip, z = table_ref[0], table_ref[1], table_ref[2]
        now = pl.program_id(0)

        def targets():
            for c in range(2):
                owner = jnp.bitwise_xor(core, c)
                for i in range(4):
                    mask = jnp.where(owner == 0, i, (0, 2, 1, 3)[i])
                    yield 4 * c + i, s_ref.at[owner, jnp.bitwise_xor(chip, mask)]

        @pl.when(now == 0)
        def _():
            for to in range(nz):
                for k, there in targets():
                    pltpu.make_async_copy(refs[k].at[jnp.bitwise_xor(z, to)], there.at[to], sem.at[k, to]).start()

        for k, there in targets():
            pltpu.make_async_copy(refs[k].at[0], there.at[now], sem.at[k, now]).wait()
        for q in range(4):
            for u in range(plain):
                rows = [s_ref[c, q, now, u].astype(f32) for c in range(2)]
                outs[0][u, q] = jnp.concatenate(rows, axis=0).astype(bf)
            if tall:
                rows = [s_ref[c, q, now, plain + k].astype(f32) for c in range(2) for k in range(4)]
                outs[1][q] = jnp.concatenate(rows, axis=0).astype(bf)
            if left:
                rows = [s_ref[c, q, now, plain].astype(f32)[:1] for c in range(2)]
                outs[-1][q] = jnp.concatenate(rows + [jnp.zeros((6, D), f32)], axis=0)

    shapes = [jax.ShapeDtypeStruct((plain, 4 * nz, 2 * r, D), bf)]
    blocks = [pl.BlockSpec((plain, 4, 2 * r, D), lambda i: (0, i, 0, 0))]
    if tall:
        shapes.append(jax.ShapeDtypeStruct((4 * nz, 8 * r, D), bf))
        blocks.append(pl.BlockSpec((4, 8 * r, D), lambda i: (i, 0, 0)))
    if left:
        shapes.append(jax.ShapeDtypeStruct((4 * nz, 8, D), f32))
        blocks.append(pl.BlockSpec((4, 8, D), lambda i: (i, 0, 0)))
    out = pl.pallas_call(
        body,
        name="place_units",
        grid=(nz,),
        out_shape=tuple(shapes),
        in_specs=[pl.BlockSpec(memory_space=pltpu.SMEM)] + [pl.BlockSpec(memory_space=pl.ANY)] * 8,
        out_specs=tuple(blocks),
        scratch_shapes=[pltpu.VMEM((2, 4, nz, n, r, D), bf), pltpu.SemaphoreType.DMA((8, nz))],
        compiler_params=pltpu.CompilerParams(vmem_limit_bytes=60 * 1024 * 1024),
        cost_estimate=pl.CostEstimate(flops=0, bytes_accessed=n * D * D * 4, transcendentals=0),
    )(table, *pieces[0], *pieces[1])
    out = list(out)
    out[0] = out[0].reshape(plain, D, D)
    if tall:
        out[1] = out[1].reshape(4 * D, D)
    return out


def pick(stack, index, axis=0):
    return lax.dynamic_index_in_dim(stack, index, axis, keepdims=False)


def ordered(first, mine, other):
    return jnp.stack([jnp.where(first, mine, other), jnp.where(first, other, mine)])


class Place:
    def __init__(self):
        self.nz = lax.axis_size("dp")
        self.nf = lax.axis_size("fsdp")
        self.nq = self.nf // 2
        self.z = lax.axis_index("dp")
        self.f = lax.axis_index("fsdp")
        self.core = self.f % 2
        self.even = self.core == 0
        self.chip = self.f // 2
        self.group = self.chip % GROUPS

    def sibling(self, x):
        return lax.ppermute(x, "fsdp", [(f, f ^ 1) for f in range(self.nf)])

    def hop(self, x, mask, odd_mask=None):
        odd_mask = mask if odd_mask is None else odd_mask
        route = [(f, f ^ ((odd_mask if f % 2 else mask) << 1)) for f in range(self.nf)]
        return lax.ppermute(x, "fsdp", route)

    def across(self, x, mask):
        return lax.ppermute(x, "dp", [(z, z ^ mask) for z in range(self.nz)])

    def send_line(self, x):
        return [self.across(x, m) for m in range(1, self.nz)]

    def send_terms(self, now):
        return [self.across(pick(now, self.z ^ m), m) for m in range(1, self.nz)]

    def gather_square(self, block, bit):
        a, b = 1 << bit, 2 << bit
        first = self.hop(block, a, b)
        second = self.hop(block, b, a)
        return [block, first, second, self.hop(first, b, a)]

    def first_hop(self, x):
        return self.hop(x, 1, 2)

    def second_hop(self, x):
        return self.hop(x, 2, 1)

    def arranged(self, pieces, bit, odd):
        here = (self.chip >> bit) % 4
        stack = jnp.stack(pieces)
        at = [0, 1, 2, 3]
        swapped = jnp.where(odd, jnp.array([0, 2, 1, 3]), jnp.array(at))
        return jnp.stack([pick(stack, swapped[here ^ k]) for k in at])

    def gather_plain(self, block):
        stack = jnp.stack([block] + self.send_line(block))
        now = jnp.stack([pick(stack, self.z ^ k) for k in range(self.nz)])
        levels = 0
        for bit in range(0, self.nq.bit_length() - 1, 2):
            now = self.arranged(self.gather_square(now, bit), bit, ~self.even)
            levels += 1
        now = ordered(self.even, now, self.sibling(now))
        n, r = block.shape[:2]
        now = now.reshape(2, self.nq, self.nz, n, r, D)
        return jnp.transpose(now, (3, 2, 1, 0, 4, 5))

    def chip_terms(self, pairs):
        def parts(i, kind=f32):
            blocks = []
            for pair in pairs:
                along = []
                for keep, other in pair if isinstance(pair[0], (tuple, list)) else [pair]:
                    shape = (4,) + (() if self.nq == 4 else (self.nq // 4,)) + keep.shape[1:]
                    block = pick(keep.reshape(shape), i).astype(f32) + pick(other.reshape(shape), i).astype(f32)
                    along.append((block if self.nq == 4 else jnp.swapaxes(block, 0, 1)).astype(kind))
                blocks.append(along[0] if len(along) == 1 else jnp.concatenate(along))
            return jnp.concatenate(blocks, axis=-3)

        return parts

    def halves(self, x, r):
        x = x.reshape((-1, self.nz, self.nq, 2, r, x.shape[-1]))

        def rows(which):
            return jnp.transpose(pick(x, which, 3), (2, 1, 0, 3, 4))

        return rows(self.core), rows(1 - self.core)

    def square_terms(self, parts):
        bit = (self.nq.bit_length() - 1) - 2
        here = (self.chip >> bit) % 4
        first = jnp.where(self.even, 1, 2)
        masks = (3 - first, jnp.full_like(first, 3), first, jnp.zeros_like(first))
        return [parts(here ^ mask, kind) for mask, kind in zip(masks, (bf, bf, f32, f32))]

    def outer_hop(self, which, x):
        bit = (self.nq.bit_length() - 1) - 2
        a, b = 1 << bit, 2 << bit
        return self.hop(x, a, b) if which == 0 else self.hop(x, b, a)

    def inner_square(self, now):
        if now.ndim > 4:
            first = jnp.where(self.even, 1, 2)
            here = self.chip % 4

            def at(mask):
                return pick(now, here ^ mask, 1).astype(f32)

            second = self.hop(at(3 - first).astype(bf), 2, 1)
            corner = self.hop(at(3).astype(bf), 2, 1)
            moved = self.hop((at(first) + corner.astype(f32)).astype(bf), 1, 2)
            now = (at(0) + moved.astype(f32) + second.astype(f32)).astype(bf)
        return now

    def own_terms(self, now):
        return pick(now, self.z).astype(f32)

    def group_hops(self, x):
        return [self.hop(x, mask) for mask in range(1, GROUPS)]

    def in_order(self, pieces):
        stack = jnp.stack(pieces)
        return jnp.stack([pick(stack, self.group ^ k) for k in range(GROUPS)])

    def to_groups(self, blocks):
        return [self.hop(pick(blocks, self.group ^ mask), mask) for mask in range(1, GROUPS)]

    def owned_rows(self, mine, axis=0):
        own = lax.dynamic_slice_in_dim(mine, self.f * Q_DEV, Q_DEV, axis)
        give = lax.dynamic_slice_in_dim(mine, (self.f ^ 1) * Q_DEV, Q_DEV, axis)
        return ordered(self.even, own, self.sibling(give))


def tie(*arrays):
    return lax.optimization_barrier(arrays)


def stage(*moves):
    operands = tie(*[operand for _, operand in moves])
    return tie(*[move(operand) for (move, _), operand in zip(moves, operands)])


def split_three(x):
    hi = lax.reduce_precision(x, 8, 7)
    mid = lax.reduce_precision(x - hi, 8, 7)
    return [hi.astype(bf), mid.astype(bf), (x - hi - mid).astype(bf)]


def join_three(x):
    a, b, c = jnp.split(x.astype(f32), 3, axis=-1)
    return (a + b) + c


def columns(weight):
    rows, width = weight.shape
    return [weight[:, k * D : (k + 1) * D] for k in range(width // D)]


def strip_bias(place, bands, height):
    half = WIN // 2
    rows = (place.f % bands) * height + jnp.arange(height, dtype=jnp.int32)
    cols = (place.f // bands) * WIN + jnp.arange(WIN, dtype=jnp.int32)

    def label(at, total):
        return (at >= total - WIN).astype(jnp.int32) + (at >= total - half).astype(jnp.int32)

    labels = label(rows, height * bands)[:, None] * 3 + label(cols, WIN * WCOLS)
    labels = labels.reshape(height // WIN, PATCH)
    return jnp.where(labels[:, :, None] == labels[:, None, :], 0.0, -1e30).astype(f32)


def roll_beside(x, place, bands):
    route = [((f + bands) % place.nf, f) for f in range(place.nf)]
    return lax.ppermute(x, "fsdp", route)


def roll_in(x, beside, place, bands):
    half = WIN // 2
    pages, height = x.shape[:2]
    if bands > 1:
        x = jnp.concatenate([x[:, :, half:], beside.reshape(pages, height, half, D)], axis=2)
        route = [(f // bands * bands + (f + 1) % bands, f) for f in range(place.nf)]
        below = lax.ppermute(x[:, :half], "fsdp", route)
        return jnp.concatenate([x[:, half:], below], axis=1).reshape(-1, D)

    def body(x_ref, b_ref, out_ref, tall_ref, side_ref):
        side_ref[...] = b_ref[...].astype(f32)
        for to in range(height):
            row = (to + half) % height
            tall_ref[to * WIN : to * WIN + half] = x_ref[0, row].astype(f32)[half:]
            tall_ref[to * WIN + half : (to + 1) * WIN] = side_ref[row * half : (row + 1) * half]
        out_ref[...] = tall_ref[...].astype(bf)

    return call(
        body,
        "roll_in",
        sds((pages * height * WIN, D), bf),
        [per_page((1, height, WIN, D), 0), per_page((height * half, D), 0)],
        per_page((height * WIN, D), 0),
        (pages,),
        (x, beside),
        scratch=(pltpu.VMEM((height * WIN, D), f32), pltpu.VMEM((height * half, D), f32)),
        flops=1 << 20,
    )


def last_columns(x):
    half = WIN // 2
    height = x.shape[0] // MICRO // WIN

    def body(x_ref, out_ref, tall_ref, side_ref):
        tall_ref[...] = x_ref[...].astype(f32)
        for row in range(height):
            side_ref[row * half : (row + 1) * half] = tall_ref[row * WIN + half : (row + 1) * WIN]
        out_ref[...] = side_ref[...].astype(bf)

    return call(
        body,
        "last_columns",
        sds((MICRO * height * half, D), bf),
        [per_page((height * WIN, D), 0)],
        per_page((height * half, D), 0),
        (MICRO,),
        (x,),
        (pltpu.VMEM((height * WIN, D), f32), pltpu.VMEM((height * half, D), f32)),
    )


def roll_out(x, beside, place, bands):
    half = WIN // 2
    height = x.shape[0] // MICRO // WIN
    shape = (MICRO, height, WIN, D)
    if bands > 1:
        x = jnp.concatenate([beside.reshape(MICRO, height, half, D), x.reshape(shape)[:, :, :half]], axis=2)
        rows = [(f, f // bands * bands + (f + 1) % bands) for f in range(place.nf)]
        above = lax.ppermute(x[:, -half:], "fsdp", rows)
        return jnp.concatenate([above, x[:, :-half]], axis=1)

    def body(x_ref, b_ref, out_ref, tall_ref, side_ref):
        tall_ref[...] = x_ref[...].astype(f32)
        side_ref[...] = b_ref[...].astype(f32)
        for row in range(height):
            parts = [side_ref[row * half : (row + 1) * half], tall_ref[row * WIN : row * WIN + half]]
            out_ref[0, (row + half) % height] = jnp.concatenate(parts, axis=0).astype(bf)

    return call(
        body,
        "roll_out",
        sds(shape, bf),
        [per_page((height * WIN, D), 0), per_page((height * half, D), 0)],
        per_page((1,) + shape[1:], 0),
        (MICRO,),
        (x, beside),
        (pltpu.VMEM((height * WIN, D), f32), pltpu.VMEM((height * half, D), f32)),
    )


def local(
    visual,
    query_slots,
    lengths,
    slot_order,
    norm_window,
    window_qkv,
    window_out,
    norm_slots,
    slots_qkv,
    slots_out,
    norm_reader,
    norm_page,
    reader_qkv,
    reader_out,
    writer_qkv,
    writer_out,
    norm_visual_mlp,
    visual_up,
    visual_down,
    norm_query_mlp,
    query_up,
    query_down,
    visual_cot,
    query_cot,
):
    place = Place()
    nz, nf, nq, core, even = place.nz, place.nf, place.nq, place.core, place.even
    extra = nq // GROUPS
    bands = nf // WCOLS
    height = visual.shape[1]
    page_rows = height * WIN
    rows = MICRO * page_rows
    slots = Q_DEV * nf
    r = window_out.shape[0]

    fast = r % 8 == 0 and nq == 4
    gains = jnp.stack([norm_window, norm_slots, norm_reader, norm_page, norm_visual_mlp, norm_query_mlp])
    gains = jnp.zeros((r, D), bf).at[0, : 6 * r].set(gains.reshape(6 * r))
    arrays = (
        window_qkv,
        window_out,
        slots_qkv,
        slots_out,
        reader_qkv,
        reader_out,
        writer_qkv,
        writer_out,
        visual_up,
        visual_down,
        query_up,
        query_down,
    )
    one, two, three, four = pack_rows(place, arrays, gains)

    def squares(x):
        return [place.first_hop(x), place.second_hop(x)]

    def siblings(x):
        return jax.tree.map(place.sibling, x)

    def assemble(block, pieces, others, plain, tall):
        if fast:
            return place_units(place, [pieces, others], plain, tall)
        units = place.gather_plain(block)
        out = [units[:plain].reshape(plain, D, D)]
        if tall:
            out.append(jnp.transpose(units[plain:], (1, 2, 3, 0, 4, 5)).reshape(4 * D, D))
        elif block.shape[0] > plain:
            rows_left = units[plain, ..., 0, :].reshape(nz * nq, 2, D).astype(f32)
            out.append(jnp.pad(rows_left, ((0, 0), (0, 6), (0, 0))))
        return out

    positions = (slot_order[:, :, None] * Q_DEV + jnp.arange(Q_DEV, dtype=jnp.int32)).reshape(MICRO, slots)
    live = jnp.where(positions < lengths[:, None], 0.0, -1e30).astype(f32).reshape(MICRO, 1, slots)
    own_live = pick(live, core)
    bias = strip_bias(place, bands, height)
    chip_id = place.chip.astype(jnp.int32).reshape(1)
    core_id = core.astype(jnp.int32).reshape(1)

    def spread(x, bit):
        return place.hop(x, 1 << bit)

    def spread_order(x, got, bit):
        upper = (place.chip >> bit) % 2 == 1
        return jnp.concatenate([jnp.where(upper, got, x), jnp.where(upper, x, got)], axis=1)

    def all_dp(block, got):
        return jnp.stack([block] + list(got))

    act_block = per_page((page_rows, D), 0)
    three_block = per_page((3, page_rows, D), 1)

    def part_of(size, index, full):
        return full, pl.BlockSpec((size, D, D), lambda *_: (index, 0, 0), pipeline_mode=pl.Buffered(1))

    def run_first(args):
        sib_c, x = args
        w_one, gain_all = assemble(one, [all_one, f_one, s_one, c_one], [sib_one, sib_f_one, sib_s_one, sib_c], 8, 0)
        gain_all = gain_all[:, :2, : 6 * r].reshape(nz * nq * 2, 6, r)
        gain_all = jnp.transpose(gain_all, (1, 0, 2)).reshape(6, 1, D)
        windows = call(
            window_fwd,
            "window_fwd",
            (sds((3, rows, D), bf), sds((rows, D), bf), sds((rows, D), f32)),
            [act_block, whole(bias.shape), whole((1, D)), part_of(4, 0, None)[1]],
            (three_block, act_block, act_block),
            (MICRO,),
            (x, bias, gain_all[0], w_one),
            flops=2 * rows * 4 * D * D,
        )
        return w_one, gain_all, windows

    roll = partial(roll_beside, place=place, bands=bands)
    ends = jnp.stack([query_slots, query_cot])
    got, beside_x, ends_two = stage(
        (place.send_line, one),
        (roll, visual[:, :, : WIN // 2].reshape(-1, D)),
        (place.sibling, pick(ends, 1 - core, 1)),
    )
    all_one = all_dp(one, got)
    ends = jnp.swapaxes(ordered(even, pick(ends, core, 1), ends_two), 0, 1).reshape(2, 2 * Q_DEV, D)
    got, (f_one, s_one) = stage((place.send_line, two), (squares, all_one))
    c_one, ends_two, sib_one, sib_f_one, sib_s_one, x = stage(
        (place.second_hop, f_one),
        (partial(spread, bit=0), ends),
        (place.sibling, all_one),
        (place.sibling, f_one),
        (place.sibling, s_one),
        (lambda args: roll_in(*args, place, bands), (visual, beside_x)),
    )
    ends = spread_order(ends, ends_two, 0)
    sib_c_one, ends_two, got = tie(place.sibling(c_one), spread(ends, 1), got)
    ends = spread_order(ends, ends_two, 1)
    for bit in range(2, nq.bit_length() - 1):
        ends = spread_order(ends, spread(ends, bit), bit)
    xs, xs_cot = ends[0], ends[1]
    all_two = all_dp(two, got)
    got, (f_two, s_two), first = stage(
        (place.send_line, three), (squares, all_two), (run_first, (sib_c_one, x))
    )
    all_three = all_dp(three, got)
    w_one, gain_all, (mix, att, v1) = first
    g_window, g_slots, g_reader, g_page, g_vmlp, g_qmlp = (gain_all[k] for k in range(6))

    def run_slots(args):
        return simple(
            slots_fwd,
            "slots_fwd",
            (args[0], g_slots, part_of(4, 1, args[1]), own_live),
            [((3, slots, D), bf), ((slots, D), bf), ((slots, D), f32)],
        )

    c_two, sib_two, sib_f_two, sib_s_two, (mix_q, att_q, s1) = stage(
        (place.second_hop, f_two),
        (place.sibling, all_two),
        (place.sibling, f_two),
        (place.sibling, s_two),
        (run_slots, (xs, w_one)),
    )
    sib_c_two, all_three = tie(place.sibling(c_two), all_three)
    def run_second(args):
        sib_c, v1, s1 = args
        (w_two,) = assemble(two, [all_two, f_two, s_two, c_two], [sib_two, sib_f_two, sib_s_two, sib_c], 7, 0)
        (rd_own,) = simple(
            normed_units, "slots_units", (s1, g_reader, part_of(3, 1, w_two)), [((3, slots, D), bf)]
        )
        pk = call(
            normed_units,
            "page_units",
            sds((3, rows, D), bf),
            [act_block, whole((1, D)), part_of(3, 0, None)[1]],
            three_block,
            (MICRO,),
            (v1, g_page, w_two),
            flops=2 * rows * 3 * D * D,
        )
        return w_two, rd_own, pk

    got, (f_three, s_three), (w_two, rd_own, pk) = stage(
        (place.send_line, four), (squares, all_three), (run_second, (sib_c_two, v1, s1))
    )
    rd_two = place.sibling(rd_own)
    rd_two, got = tie(rd_two, got)
    all_four = all_dp(four, got)
    rd = jnp.swapaxes(ordered(even, rd_own, rd_two), 0, 1)
    rq, wk, wv = rd[0], rd[1], rd[2]
    slot_block = per_page((1, slots, D), 0)
    stat_block = per_page((1, slots, 128), 0)

    def of_pk(u):
        return pl.BlockSpec((1, page_rows, D), lambda p: (u, p, 0))

    def merge(terms):
        width = terms[0].shape[-1] // (HEAD + 1) * HEAD
        lse = jnp.stack([t[..., width:] for t in terms])
        top = jnp.max(lse, axis=0)
        weights = jnp.exp(lse - top)
        total = jnp.sum(weights, axis=0)
        shares = weights / total
        out = sum(t[..., :width] * jnp.repeat(share, HEAD, axis=-1) for t, share in zip(terms, shares))
        return jnp.concatenate([out, top + jnp.log(total)], axis=-1)

    def run_read(args):
        return call(
            read_fwd,
            "read_fwd",
            (sds((MICRO, slots, D), f32), sds((MICRO, slots, 128), f32)),
            [slot_block, of_pk(0), of_pk(1)],
            (slot_block, stat_block),
            (MICRO,),
            args,
            flops=2 * rows * slots * D * 4,
        )

    c_three, sib_three, sib_f_three, sib_s_three, (o_part, lse_part) = stage(
        (place.second_hop, f_three),
        (place.sibling, all_three),
        (place.sibling, f_three),
        (place.sibling, s_three),
        (run_read, (rq, pk, pk)),
    )
    terms = jnp.concatenate([o_part, lse_part[..., :HEADS]], axis=-1)
    live_block = per_page((1, 1, slots), 0)

    def run_write(args):
        return call(
            write_fwd,
            "write_fwd",
            (sds((rows, D), bf), sds((rows, D), f32)),
            [act_block, of_pk(2), slot_block, slot_block, live_block, part_of(1, 6, None)[1]],
            (act_block, act_block),
            (MICRO,),
            args,
            flops=2 * rows * D * D,
        )

    terms_two, sib_c_three, beside_cot, (writing, v2) = stage(
        (place.sibling, pick(terms, 1 - core)),
        (place.sibling, c_three),
        (roll, visual_cot[:, :, : WIN // 2].reshape(-1, D)),
        (run_write, (v1, pk, wk, wv, live, w_two)),
    )
    terms = merge([pick(terms, core), terms_two])
    blocks = jnp.concatenate(
        [terms[:, :D].reshape(slots, GROUPS, GCOLS), terms[:, D:].reshape(slots, GROUPS, GHEADS)], axis=-1
    )
    blocks = jnp.swapaxes(blocks, 0, 1)
    got, cot, (w_up, w_down) = stage(
        (place.to_groups, blocks),
        (lambda args: roll_in(*args, place, bands), (visual_cot, beside_cot)),
        (
            lambda sib_c: assemble(
                three, [all_three, f_three, s_three, c_three], [sib_three, sib_f_three, sib_s_three, sib_c], 4, 1
            ),
            sib_c_three,
        ),
    )
    chunk = D
    steps = 2 * D // chunk
    per_unit = D // chunk

    def once(*shape):
        return pl.BlockSpec(shape, lambda j: (0,) * len(shape), pipeline_mode=pl.Buffered(1))

    smem = pl.BlockSpec(memory_space=pltpu.SMEM)
    if fast:
        up_shapes = [sds((nq, nz, 2, r, D), bf)] * 2
        up_outs = [pl.BlockSpec((nq, nz, 1, r, chunk), lambda j: (0, 0, j // per_unit, 0, j % per_unit))] * 2
        several = chunk // (8 * r)
        down_shapes = [sds((nq, nz // 2, 4 * r, D), bf)] * 2
        down_outs = [
            pl.BlockSpec((several, 1, 4 * r, D), lambda j: (j % (nq // several), j // (nq // several), 0, 0))
        ] * 2
    else:
        up_shapes = [sds((2, D, D), bf)]
        up_outs = [pl.BlockSpec((1, D, chunk), lambda j: (j // per_unit, 0, j % per_unit))]
        down_shapes = [sds((2 * D, D), bf)]
        down_outs = [pl.BlockSpec((chunk, D), lambda j: (j, 0))]

    def run_mlp(last, args):
        at = steps if last else 0
        up_in = pl.BlockSpec((1, D, chunk), lambda j: ((j + at) // per_unit, 0, (j + at) % per_unit))
        down_in = pl.BlockSpec((chunk, D), lambda j: (j + at, 0))
        wide = once(rows, D)
        scratch = (pltpu.VMEM((rows, D), bf),)
        if last:
            shapes = [sds((rows, D), bf), sds((rows, D), f32), sds((1, D), f32)]
            outs = [wide, wide, once(1, D)]
            scratch = scratch + (pltpu.VMEM((rows, D), f32), pltpu.VMEM((rows, D), f32))
        else:
            shapes = [sds((rows, D), f32), sds((rows, D), f32)]
            outs = [wide, wide]
        out = call(
            partial(mlp_both, steps, last, 4 * r),
            "mlp_both",
            tuple(shapes + up_shapes + down_shapes),
            [smem, wide, once(1, D), up_in, down_in, wide] + [wide, wide] * last,
            tuple(outs + up_outs + down_outs),
            (steps,),
            (core_id,) + args,
            scratch=scratch,
            flops=2 * rows * 12 * D * D,
        )
        count = len(outs)
        if fast:
            up = out[count : count + 2]
            down = [y.reshape(nq, nz // 2, 4, r, D) for y in out[count + 2 :]]
        else:
            up = place.halves(out[count], r)
            d = out[count + 1].reshape(nz // 2, nq, 2, 4, r, D)
            down = [jnp.swapaxes(pick(d, which, 2), 0, 1) for which in (core, 1 - core)]
        return tuple(out[:count]) + (list(up), list(down))

    def run_grads(body, name, shapes, specs, outs, args, units, scratch, flops):
        if fast:
            unit_shapes = [sds((nq, nz, units, r, D), bf)] * 2
        else:
            unit_shapes = [sds((units, D, D), bf)]
        unit_outs = [whole(y.shape) for y in unit_shapes]
        out = call(
            body,
            name,
            tuple(shapes + unit_shapes),
            [smem] + specs,
            tuple(outs + unit_outs),
            (MICRO,),
            (core_id,) + args,
            scratch=scratch,
            flops=flops,
        )
        count = len(outs)
        if fast:
            pair = list(out[count:])
        else:
            pair = list(place.halves(out[count], r))
        return tuple(out[:count]) + (pair,)

    reading = merge([pick(blocks, place.group)] + list(got))
    for bit in range(2, nq.bit_length() - 1):
        reading = merge([reading, place.hop(reading, 1 << bit)])
    message = jnp.concatenate([reading[:, :GCOLS].astype(bf)] + split_three(reading[:, GCOLS:]), axis=-1)
    reads, (f_four, s_four), (y, dxn, up_one, down_one) = stage(
        (place.group_hops, message),
        (squares, all_four),
        (partial(run_mlp, False), (v2, g_vmlp, w_up, w_down, cot)),
    )
    c_four, sib_four, sib_f_four, sib_s_four, (v3, dv2, dg_vmlp, up_two, down_two) = stage(
        (place.second_hop, f_four),
        (place.sibling, all_four),
        (place.sibling, f_four),
        (place.sibling, s_four),
        (partial(run_mlp, True), (v2, g_vmlp, w_up, w_down, cot, y, dxn)),
    )
    reads = place.in_order([message] + list(reads))

    def run_write_bwd(args):
        return run_grads(
            write_bwd,
            "write_bwd",
            [sds((rows, D), bf), sds((MICRO, slots, D), bf), sds((MICRO, slots, D), bf)],
            [act_block, act_block, of_pk(2), slot_block, slot_block, live_block, part_of(1, 6, None)[1]],
            [act_block, slot_block, slot_block],
            args,
            1,
            (pltpu.VMEM((D, D), f32),),
            4 * rows * D * D,
        )

    sib_c_four, *net_got, (dwq, dwk, dwv, pair_wo) = stage(
        (place.sibling, c_four),
        (place.sibling, up_one[1]),
        (place.sibling, up_two[1]),
        (place.sibling, down_one[1]),
        (place.sibling, down_two[1]),
        (run_write_bwd, (dv2, writing, pk, wk, wv, live, w_two)),
    )
    down_pairs = [(down_one[0], net_got[2]), (down_two[0], net_got[3])]
    up_pairs = [(up_one[0], net_got[0]), (up_two[0], net_got[1])]
    if fast:
        second, corner, first, own_net = net_terms(place, up_pairs, down_pairs)
    else:
        second, corner, first, own_net = place.square_terms(place.chip_terms(up_pairs + [down_pairs]))

    def run_query(args):
        units, w_down = assemble(
            four, [all_four, f_four, s_four, c_four], [sib_four, sib_f_four, sib_s_four, sib_c_four], 5, 1
        )
        s1, reads = args
        up_block = pl.BlockSpec((4, D, D), lambda *_: (0, 0, 0), pipeline_mode=pl.Buffered(1))
        return simple(
            partial(query_mlp, 2 * r, D // nz),
            "query_mlp",
            (chip_id, core_id, s1, reads, part_of(1, 4, units), g_qmlp, (units, up_block), w_down, xs_cot),
            [((slots, D), bf), ((slots, D), f32), ((slots, 2 * D + 128), bf), ((1, D), f32)]
            + (chip_shapes(9, r) if fast else chip_shapes(5, r) + chip_shapes(1, 4 * r)),
        )

    def chip_shapes(k, r):
        return [((nz, k, r, D), bf)] * 2 if fast else [((k, nz * 2 * r, D), bf)]

    def chip_pair(outs, r):
        if fast:
            return list(outs)
        x = outs[0].reshape(-1, nz, 2, r, D)
        return [jnp.swapaxes(pick(x, which, 2), 0, 1) for which in (core, 1 - core)]

    second, corner, (q_out, ds2, message, dg_qmlp, *d_early) = stage(
        (partial(place.outer_hop, 1), second.astype(bf)),
        (partial(place.outer_hop, 1), corner.astype(bf)),
        (run_query, (s1, reads)),
    )
    own_net = own_net.astype(f32) + second.astype(f32)
    first = (first.astype(f32) + corner.astype(f32)).astype(bf)

    if fast:
        keep_early, give_early = d_early
    else:
        pairs = zip(chip_pair(d_early[:1], r), chip_pair(d_early[1:], 4 * r))
        keep_early, give_early = (jnp.concatenate([a, b.reshape(nz, 4, r, D)], axis=1) for a, b in pairs)
    message_two, early_got = stage((place.sibling, message), (place.sibling, give_early))
    message = ordered(even, message, message_two)
    early = (keep_early.astype(f32) + early_got.astype(f32)).astype(bf)
    early_sum = lax.psum_scatter(early.reshape(nz, 9 * r, D), "dp", scatter_dimension=0).reshape(9, r, D)

    def run_read_bwd(args):
        grad_block = pl.BlockSpec((1, slots, D), lambda p: (p, 0, 0))
        read_block = pl.BlockSpec((1, slots, D), lambda p: (p, 0, 1))
        sums_block = pl.BlockSpec((1, slots, 128), lambda p: (p, 0, 2 * D // 128))
        return call(
            read_bwd,
            "read_bwd",
            (sds((MICRO, slots, D), bf), sds((rows, D), bf), sds((rows, D), bf)),
            [slot_block, of_pk(0), of_pk(1), grad_block, read_block, sums_block],
            (slot_block, act_block, act_block),
            (MICRO,),
            args,
            flops=2 * rows * slots * D * 10,
        )

    drq, dk, dv = run_read_bwd((rq, pk, pk, message, message, message))

    def run_page_bwd(args):
        return run_grads(
            page_bwd,
            "page_bwd",
            [sds((rows, D), f32), sds((1, D), f32)],
            [act_block, act_block, act_block, act_block, act_block, whole((1, D)), whole((3, D, D))],
            [act_block, whole((1, D))],
            args,
            3,
            (pltpu.VMEM((3, D, D), f32), pltpu.VMEM((1, D), f32)),
            2 * rows * 6 * D * D,
        )

    d_slots = jnp.stack([drq, dwk, dwv], axis=1)
    slots_two, first, (dv1, dg_page, pair_page) = stage(
        (place.sibling, pick(d_slots, 1 - core)),
        (partial(place.outer_hop, 0), first),
        (run_page_bwd, (v1, dv2, dk, dv, dwq, g_page, w_two)),
    )
    own_net = place.inner_square((own_net + first.astype(f32)).astype(bf))
    net_sum = lax.psum_scatter(own_net.reshape(nz, 8 * r, D), "dp", scatter_dimension=0).reshape(8, r, D)
    d_slots = (pick(d_slots, core).astype(f32) + slots_two.astype(f32)).astype(bf)
    d_slots = jnp.transpose(d_slots.reshape(3, slots, GROUPS, GCOLS), (2, 0, 1, 3))

    def run_window_bwd(page, args):
        here = pl.BlockSpec((page_rows, D), lambda i: (page, 0))
        three_here = pl.BlockSpec((3, page_rows, D), lambda i: (0, page, 0))
        return pl.pallas_call(
            window_bwd,
            name="window_bwd",
            out_shape=sds((3, rows, D), bf),
            grid=(1,),
            in_specs=[here, three_here, here, whole(bias.shape), part_of(4, 0, None)[1]]
            + [pl.BlockSpec(memory_space=pl.ANY)] * page,
            out_specs=three_here,
            scratch_shapes=(pltpu.VMEM((page_rows, D), bf),),
            input_output_aliases={5: 0} if page else {},
            compiler_params=pltpu.CompilerParams(vmem_limit_bytes=58 * 1024 * 1024),
            cost_estimate=pl.CostEstimate(flops=rows * 2 * D * D, bytes_accessed=1 << 20, transcendentals=0),
        )(*args)

    page_got, got, dmix = stage(
        (siblings, [pair_page[1], pair_wo[1]]),
        (place.to_groups, d_slots),
        (partial(run_window_bwd, 0), (dv1, mix, att, bias, w_one)),
    )
    d_rd = sum(x.astype(f32) for x in [pick(d_slots, place.group)] + list(got)).astype(bf)
    for bit in range(2, nq.bit_length() - 1):
        d_rd = (d_rd.astype(f32) + place.hop(d_rd, 1 << bit).astype(f32)).astype(bf)
    second, corner, first, own_page = place.square_terms(
        place.chip_terms([(pair_page[0], page_got[0]), (pair_wo[0], page_got[1])])
    )
    rds, second, corner, dmix = stage(
        (place.group_hops, d_rd),
        (partial(place.outer_hop, 1), second.astype(bf)),
        (partial(place.outer_hop, 1), corner.astype(bf)),
        (partial(run_window_bwd, 1), (dv1, mix, att, bias, w_one, dmix)),
    )
    own_page = own_page + second.astype(f32)
    first = (first.astype(f32) + corner.astype(f32)).astype(bf)
    d_rd = jnp.transpose(place.in_order([d_rd] + list(rds)), (1, 2, 0, 3)).reshape(3, slots, D)

    def run_query_back(args):
        return simple(
            partial(query_back, 2 * r, D // nz),
            "query_back",
            (*args[:7], part_of(3, 1, args[7]), part_of(4, 1, args[8]), *args[9:]),
            [((slots, D), bf), ((1, D), f32), ((1, D), f32)] + chip_shapes(7, r),
            scratch=(pltpu.VMEM((3, slots, D), bf),),
        )

    def run_window_grads(args):
        return run_grads(
            window_grads,
            "window_grads",
            [],
            [act_block, act_block, three_block, act_block, whole((1, D))],
            [],
            args,
            4,
            (pltpu.VMEM((4, D, D), f32),),
            2 * rows * 4 * D * D,
        )

    def right(x):
        return lax.ppermute(x, "fsdp", [(f, (f + bands) % nf) for f in range(nf)])

    first, query_out, (x_grad, dg_slots, dg_reader, *d_late), side_out = stage(
        (partial(place.outer_hop, 0), first),
        (place.owned_rows, q_out),
        (
            run_query_back,
            (chip_id, core_id, xs, s1, ds2, d_rd, g_reader, w_two, w_one, mix_q, att_q, own_live, g_slots),
        ),
        (last_columns, v3),
    )
    own_page = place.inner_square((own_page + first.astype(f32)).astype(bf))
    keep_late, give_late = chip_pair(d_late, r)
    late_got, page_passed, side_out, (pair_window,) = stage(
        (place.sibling, give_late),
        (place.send_terms, own_page),
        (right, side_out),
        (run_window_grads, (dv1, x, dmix, att, g_window)),
    )
    pair_window, net_sum, early_sum = tie(pair_window, net_sum, early_sum)
    late = (keep_late.astype(f32) + late_got.astype(f32)).astype(bf)
    (window_got,) = stage((place.sibling, pair_window[1]))
    second, corner, first, own_window = place.square_terms(place.chip_terms([(pair_window[0], window_got)]))

    def run_window_end(args):
        return call(
            window_end,
            "window_end",
            (sds((rows, D), bf), sds((1, D), f32)),
            [act_block, act_block, three_block, whole((1, D)), part_of(4, 0, None)[1]],
            (act_block, whole((1, D))),
            (MICRO,),
            args,
            scratch=(pltpu.VMEM((1, D), f32),),
            flops=2 * rows * 3 * D * D,
        )

    def run_ends(args):
        v3, side_out, *rest = args
        v_grad, dg_window = run_window_end(rest)
        return v_grad, last_columns(v_grad), roll_out(v3, side_out, place, bands)

    second, corner, late_passed, (v_grad, side_grad, visual_out) = stage(
        (partial(place.outer_hop, 1), second.astype(bf)),
        (partial(place.outer_hop, 1), corner.astype(bf)),
        (place.send_terms, late),
        (run_ends, (v3, side_out, dv1, x, dmix, g_window, w_one)),
    )
    own_window = own_window + second.astype(f32)
    first = (first.astype(f32) + corner.astype(f32)).astype(bf)
    first, query_grad = stage((partial(place.outer_hop, 0), first), (place.owned_rows, x_grad))
    own_window = place.inner_square((own_window + first.astype(f32)).astype(bf))
    z_id = place.z.astype(jnp.int32).reshape(1)

    def column(gain):
        return gain.reshape(r, 1)

    def run_finish(args):
        net_sum, early_sum, own_page, page_passed, late, late_passed = args
        rows_of = [((r, 4 * D), f32), ((4, r, D), f32), ((r, 4 * D), f32), ((r, D), f32), ((4, r, D), f32)]
        rows_of += [((r, 3 * D), f32)] * 2 + [((r, D), f32), ((r, 3 * D), f32), ((r, D), f32)] + [((r, 1), f32)] * 5
        return simple(
            partial(finish_most, nz),
            "finish_most",
            (
                z_id,
                net_sum,
                early_sum,
                visual_up,
                query_up,
                slots_qkv,
                reader_qkv,
                writer_qkv,
                column(norm_page),
                column(norm_visual_mlp),
                column(norm_slots),
                column(norm_reader),
                column(norm_query_mlp),
                own_page,
                late,
                *page_passed,
                *late_passed,
            ),
            rows_of,
        )

    window_passed, side_grad, most = stage(
        (place.send_terms, own_window),
        (right, side_grad),
        (run_finish, (net_sum, early_sum, own_page, page_passed, late, late_passed)),
    )
    visual_grad = roll_out(v_grad, side_grad, place, bands)
    grad_win, grad_win_out, grad_gw = simple(
        finish_windows,
        "finish_windows",
        (z_id, column(norm_window), window_qkv, own_window, *window_passed),
        [((r, 3 * D), f32), ((r, D), f32), ((r, 1), f32)],
    )
    grad_up, grad_down, grad_qup, grad_ro, grad_qdown, grad_reader, grad_writer, grad_wo, grad_sq, grad_so = most[:10]
    grad_gp, grad_gv, grad_gs, grad_gr, grad_gq = most[10:]

    def gain(x):
        return x.reshape(r)

    return (
        visual_out,
        query_out,
        visual_grad,
        query_grad,
        gain(grad_gw),
        grad_win,
        grad_win_out,
        gain(grad_gs),
        grad_sq,
        grad_so,
        gain(grad_gr),
        gain(grad_gp),
        grad_reader,
        grad_ro,
        grad_writer,
        grad_wo,
        gain(grad_gv),
        grad_up,
        grad_down.reshape(4 * r, D),
        gain(grad_gq),
        grad_qup,
        grad_qdown.reshape(4 * r, D),
    )


def solution(mesh):
    page = P("dp", "fsdp", None, None)
    slot = P("dp", "fsdp", None)
    gain = P(("dp", "fsdp"))
    matrix = P(("dp", "fsdp"), None)
    weights = (
        gain,
        matrix,
        matrix,
        gain,
        matrix,
        matrix,
        gain,
        gain,
        matrix,
        matrix,
        matrix,
        matrix,
        gain,
        matrix,
        matrix,
        gain,
        matrix,
        matrix,
    )
    return jax.shard_map(
        local,
        mesh=mesh,
        in_specs=(page, slot, P("dp"), P("dp", None)) + weights + (page, slot),
        out_specs=(page, slot, page, slot) + weights,
        check_vma=False,
    )
```

```python
from functools import partial

import jax
import jax.numpy as jnp
from jax import lax
from jax.experimental import pallas as pl
from jax.experimental.pallas import tpu as pltpu
from jax.sharding import PartitionSpec as P

D = 768
HEADS = 12
HEAD = 64
WIN = 12
WCOLS = 8
Q_DEV = 16
MICRO = 2
PATCH = WIN * WIN
PAIRS = HEADS // 2
GROUPS = 4
GHEADS = HEADS // GROUPS
GCOLS = GHEADS * HEAD
SCALE = HEAD ** (-0.5)

bf = jnp.bfloat16
f32 = jnp.float32


def dot(a, b):
    return lax.dot_general(a, b, (((1,), (0,)), ((), ())), preferred_element_type=f32)


def dot_t(a, b):
    return lax.dot_general(a, b, (((1,), (1,)), ((), ())), preferred_element_type=f32)


def t_dot(a, b):
    return lax.dot_general(a, b, (((0,), (0,)), ((), ())), preferred_element_type=f32)


def normalise(x):
    centred = x - jnp.mean(x, axis=-1, keepdims=True)
    inv = lax.rsqrt(jnp.mean(centred * centred, axis=-1, keepdims=True) + 1e-05)
    return centred * inv, inv


def norm_back(grad, hat, inv, gain):
    scaled = grad * gain
    mean_one = jnp.mean(scaled, axis=-1, keepdims=True)
    mean_two = jnp.mean(scaled * hat, axis=-1, keepdims=True)
    return inv * (scaled - mean_one - hat * mean_two), jnp.sum(grad * hat, axis=0, keepdims=True)


def gelu_both(u):
    k = 0.7978845608028654
    t = jnp.tanh(k * (u + 0.044715 * u * u * u))
    slope = 0.5 * (1.0 + t) + 0.5 * u * (1.0 - t * t) * k * (1.0 + 3 * 0.044715 * u * u)
    return 0.5 * u * (1.0 + t), slope


def low_lanes(rows):
    return lax.broadcasted_iota(jnp.int32, (rows, 2 * HEAD), 1) < HEAD


def twofold(pair, mask):
    zero = jnp.zeros_like(pair)
    return jnp.concatenate([jnp.where(mask, pair, zero), jnp.where(mask, zero, pair)], axis=0)


def onefold(stacked, mask):
    rows = stacked.shape[0] // 2
    return jnp.where(mask, stacked[:rows], stacked[rows:])


def groups_of_pairs(q_rows, k_rows):
    together = max(1, min(PAIRS, 700000 // (2 * q_rows * k_rows)))
    return [range(p, min(p + together, PAIRS)) for p in range(0, PAIRS, together)]


def lanes(p):
    return slice(p * 2 * HEAD, (p + 1) * 2 * HEAD)


def scaled(q2, mask):
    return twofold(q2 * jnp.asarray(SCALE, bf), mask)


def pairs_forward(q, k, v, bias):
    mask = low_lanes(q[0].shape[0])
    s = [dot_t(scaled(q2, mask), k2) for q2, k2 in zip(q, k)]
    if bias is not None:
        s = [x + bias for x in s]
    m = [jnp.max(x, axis=-1, keepdims=True) for x in s]
    e = [jnp.exp(x - top) for x, top in zip(s, m)]
    l = [jnp.sum(x, axis=-1, keepdims=True) for x in e]
    out = [dot(x.astype(bf), v2) for x, v2 in zip(e, v)]
    return [(onefold(x / total, mask), top, total) for x, top, total in zip(out, m, l)]


def pairs_backward(q, k, v, d, a, bias, lse=None):
    mask = low_lanes(q[0].shape[0])
    qs = [scaled(q2, mask) for q2 in q]
    ds = [twofold(d2, mask) for d2 in d]
    s = [dot_t(q2, k2) for q2, k2 in zip(qs, k)]
    dp = [dot_t(d2, v2) for d2, v2 in zip(ds, v)]
    corr = [
        jnp.sum(d2.astype(f32) * twofold(a2, mask).astype(f32), axis=-1, keepdims=True) for d2, a2 in zip(ds, a)
    ]
    if bias is not None:
        s = [x + bias for x in s]
    if lse is None:
        e = [jnp.exp(x - jnp.max(x, axis=-1, keepdims=True)) for x in s]
        p = [x * (1.0 / jnp.sum(x, axis=-1, keepdims=True)) for x in e]
    else:
        p = [jnp.exp(x - y) for x, y in zip(s, lse)]
    dsc = [(x * (y - c)).astype(bf) for x, y, c in zip(p, dp, corr)]
    dq = [onefold(dot(x, k2), mask) * SCALE for x, k2 in zip(dsc, k)]
    dk = [t_dot(x, q2) for x, q2 in zip(dsc, qs)]
    dv = [t_dot(x.astype(bf), d2) for x, d2 in zip(p, ds)]
    return list(zip(dq, dk, dv))


def call(body, name, out_shape, in_specs, out_specs, grid, args, scratch=(), flops=0):
    return pl.pallas_call(
        body,
        name=name,
        out_shape=out_shape,
        grid=grid,
        in_specs=in_specs,
        out_specs=out_specs,
        scratch_shapes=scratch,
        compiler_params=pltpu.CompilerParams(vmem_limit_bytes=58 * 1024 * 1024),
        cost_estimate=pl.CostEstimate(flops=flops, bytes_accessed=1 << 20, transcendentals=0),
    )(*args)


def whole(shape):
    zeros = (0,) * len(shape)
    return pl.BlockSpec(shape, lambda *_: zeros, pipeline_mode=pl.Buffered(1))


def per_page(shape, axis):
    def place(p):
        return tuple(p if k == axis else 0 for k in range(len(shape)))

    return pl.BlockSpec(shape, place)


def sds(shape, dtype):
    return jax.ShapeDtypeStruct(shape, dtype)


def window_fwd(x_ref, bias_ref, gw_ref, w_ref, mix_ref, att_ref, v1_ref):
    rows = x_ref.shape[0]
    x = x_ref[...].astype(f32)
    xn = (normalise(x)[0] * gw_ref[...]).astype(bf)
    for u in range(3):
        mix_ref[u] = dot(xn, w_ref[u]).astype(bf)

    def window(w, carry):
        at = pl.ds(pl.multiple_of(w * PATCH, 16), PATCH)
        bias = bias_ref[w]
        bias = jnp.concatenate([bias, bias], axis=0)
        for group in groups_of_pairs(PATCH, PATCH):
            cs = [lanes(p) for p in group]
            outs = pairs_forward(*([mix_ref[u, at, c] for c in cs] for u in range(3)), bias)
            for c, (out, _, _) in zip(cs, outs):
                att_ref[at, c] = out.astype(bf)
        return carry

    lax.fori_loop(0, rows // PATCH, window, 0)
    v1_ref[...] = x_ref[...].astype(f32) + dot(att_ref[...], w_ref[3])


def normed_units(x_ref, g_ref, w_ref, out_ref):
    xn = (normalise(x_ref[...])[0] * g_ref[...]).astype(bf)
    for u in range(3):
        out_ref[u] = dot(xn, w_ref[u]).astype(bf)


def read_fwd(rq_ref, k_ref, v_ref, o_ref, lse_ref):
    slots = rq_ref.shape[1]
    lane = lax.broadcasted_iota(jnp.int32, (slots, 128), 1)
    acc = jnp.zeros((slots, 128), f32)
    for group in groups_of_pairs(slots, k_ref.shape[1]):
        cs = [lanes(p) for p in group]
        outs = pairs_forward(*([ref[0, :, c] for c in cs] for ref in (rq_ref, k_ref, v_ref)), None)
        for p, c, (out, m, l) in zip(group, cs, outs):
            o_ref[0, :, c] = out
            lse = m + jnp.log(l)
            acc = jnp.where(lane == 2 * p, lse[:slots], acc)
            acc = jnp.where(lane == 2 * p + 1, lse[slots:], acc)
    lse_ref[0] = acc


def write_fwd(v1_ref, wq_ref, wk_ref, wv_ref, bias_ref, wo_ref, wr_ref, v2_ref):
    for group in groups_of_pairs(wq_ref.shape[1], wk_ref.shape[1]):
        cs = [lanes(p) for p in group]
        outs = pairs_forward(*([ref[0, :, c] for c in cs] for ref in (wq_ref, wk_ref, wv_ref)), bias_ref[0])
        for c, (out, _, _) in zip(cs, outs):
            wr_ref[:, c] = out.astype(bf)
    v2_ref[...] = v1_ref[...] + dot(wr_ref[...], wo_ref[0])


def mlp_both(steps, last, rows_of_core, core_ref, x_ref, g_ref, up_ref, down_ref, cot_ref, *refs):
    if last:
        y_in_ref, dxn_in_ref, out_ref, dx_ref, dg_ref = refs[:5]
        refs = refs[5:]
        xn_ref, y_ref, dxn_ref = refs[-3:]
        outs = refs[:-3]
    else:
        y_ref, dxn_ref = refs[:2]
        xn_ref = refs[-1]
        outs = refs[2:-1]
    half = len(outs) // 2
    j = pl.program_id(0)

    @pl.when(j == 0)
    def _():
        xn_ref[...] = (normalise(x_ref[...])[0] * g_ref[...]).astype(bf)

    xn = xn_ref[...]
    cot = cot_ref[...]
    up = up_ref[0]
    down = down_ref[...]
    act, slope = gelu_both(dot(xn, up))
    act = act.astype(bf)
    y = dot(act, down)
    dpre = (dot_t(cot, down) * slope).astype(bf)
    dxn = dot_t(dpre, up)
    emit_unit(core_ref, t_dot(xn, dpre), outs[:half], 0)
    d_down = t_dot(act, cot)
    if half == 1:
        outs[1][...] = d_down.astype(bf)
    else:
        span = 2 * rows_of_core
        for i in range(d_down.shape[0] // span):
            emit(core_ref, d_down[i * span : (i + 1) * span], outs[2], outs[3], (i, 0))

    @pl.when(j == 0)
    def _():
        y_ref[...] = y_in_ref[...] + y if last else y
        dxn_ref[...] = dxn_in_ref[...] + dxn if last else dxn

    @pl.when(j > 0)
    def _():
        y_ref[...] += y
        dxn_ref[...] += dxn

    if last:

        @pl.when(j == steps - 1)
        def _():
            x = x_ref[...]
            out_ref[...] = (x + y_ref[...]).astype(bf)
            hat, inv = normalise(x)
            dx, dg = norm_back(dxn_ref[...], hat, inv, g_ref[...])
            dx_ref[...] = cot_ref[...].astype(f32) + dx
            dg_ref[...] = dg


def write_bwd(core_ref, dv2_ref, wr_ref, wq_ref, wk_ref, wv_ref, bias_ref, wo_ref, dwq_ref, dwk_ref, dwv_ref, *refs):
    outs, acc_ref = refs[:-1], refs[-1]
    page = pl.program_id(0)
    d = dv2_ref[...].astype(bf)
    dwr = dot_t(d, wo_ref[0]).astype(bf)
    part = t_dot(wr_ref[...], d)

    @pl.when(page == 0)
    def _():
        acc_ref[...] = part

    @pl.when(page > 0)
    def _():
        acc_ref[...] += part

    @pl.when(page == pl.num_programs(0) - 1)
    def _():
        emit_unit(core_ref, acc_ref[...], outs, 0)

    for group in groups_of_pairs(wq_ref.shape[1], wk_ref.shape[1]):
        cs = [lanes(p) for p in group]
        parts = ([ref[0, :, c] for c in cs] for ref in (wq_ref, wk_ref, wv_ref))
        grads = pairs_backward(*parts, [dwr[:, c] for c in cs], [wr_ref[:, c] for c in cs], bias_ref[0])
        for c, (dq, dk, dv) in zip(cs, grads):
            dwq_ref[:, c] = dq.astype(bf)
            dwk_ref[0, :, c] = dk.astype(bf)
            dwv_ref[0, :, c] = dv.astype(bf)


def read_bwd(rq_ref, k_ref, v_ref, d_ref, r_ref, lse_ref, dq_ref, dk_ref, dv_ref):
    slots = rq_ref.shape[1]
    lse = lse_ref[0].astype(f32)

    def of_head(h):
        at = h // GHEADS * 3 * GHEADS + h % GHEADS
        hi, mid, lo = (lse[:, at + k * GHEADS : at + k * GHEADS + 1] for k in range(3))
        return (hi + mid) + lo

    for group in groups_of_pairs(slots, k_ref.shape[1]):
        cs = [lanes(p) for p in group]
        both = [jnp.concatenate([of_head(2 * p), of_head(2 * p + 1)], axis=0) for p in group]
        parts = ([ref[0, :, c] for c in cs] for ref in (rq_ref, k_ref, v_ref, d_ref, r_ref))
        for c, (dq, dk, dv) in zip(cs, pairs_backward(*parts, None, both)):
            dq_ref[0, :, c] = dq.astype(bf)
            dk_ref[:, c] = dk.astype(bf)
            dv_ref[:, c] = dv.astype(bf)


def emit(core_ref, rows, keep_ref, give_ref, at):
    half = rows.shape[0] // 2
    first, second = rows[:half], rows[half:]
    here = core_ref[0] == 0
    keep_ref[at] = jnp.where(here, first, second).astype(bf)
    give_ref[at] = jnp.where(here, second, first).astype(bf)


def emit_unit(core_ref, unit, outs, u):
    if len(outs) == 1:
        outs[0][u] = unit.astype(bf)
        return
    nq, nz = outs[0].shape[:2]
    span = unit.shape[0] // (nq * nz)
    for z in range(nz):
        for q in range(nq):
            i = z * nq + q
            emit(core_ref, unit[i * span : (i + 1) * span], outs[0], outs[1], (q, z, u))


def page_bwd(core_ref, v1_ref, dv2_ref, dk_ref, dv_ref, dwq_ref, gp_ref, wp_ref, dv1_ref, dg_ref, *refs):
    outs, acc_ref, gacc_ref = refs[:-2], refs[-2], refs[-1]
    page = pl.program_id(0)
    hat, inv = normalise(v1_ref[...])
    pn = (hat * gp_ref[...]).astype(bf)
    grads = (dk_ref, dv_ref, dwq_ref)
    dpn = dot_t(dk_ref[...], wp_ref[0]) + dot_t(dv_ref[...], wp_ref[1]) + dot_t(dwq_ref[...], wp_ref[2])
    dx, dg = norm_back(dpn, hat, inv, gp_ref[...])
    dv1_ref[...] = dv2_ref[...] + dx

    @pl.when(page == 0)
    def _():
        gacc_ref[...] = dg
        for u in range(3):
            acc_ref[u] = t_dot(pn, grads[u][...])

    @pl.when(page > 0)
    def _():
        gacc_ref[...] += dg
        for u in range(3):
            acc_ref[u] += t_dot(pn, grads[u][...])

    @pl.when(page == pl.num_programs(0) - 1)
    def _():
        dg_ref[...] = gacc_ref[...]
        for u in range(3):
            emit_unit(core_ref, acc_ref[u], outs, u)


def window_bwd(dv1_ref, mix_ref, att_ref, bias_ref, w_ref, *refs):
    dmix_ref, datt_ref = refs[-2:]
    rows = att_ref.shape[0]
    datt_ref[...] = dot_t(dv1_ref[...].astype(bf), w_ref[3]).astype(bf)

    def window(w, carry):
        at = pl.ds(pl.multiple_of(w * PATCH, 16), PATCH)
        bias = bias_ref[w]
        bias = jnp.concatenate([bias, bias], axis=0)
        for group in groups_of_pairs(PATCH, PATCH):
            cs = [lanes(p) for p in group]
            parts = ([mix_ref[u, at, c] for c in cs] for u in range(3))
            grads = pairs_backward(*parts, [datt_ref[at, c] for c in cs], [att_ref[at, c] for c in cs], bias)
            for c, grad in zip(cs, grads):
                for u in range(3):
                    dmix_ref[u, at, c] = grad[u].astype(bf)
        return carry

    lax.fori_loop(0, rows // PATCH, window, 0)


def window_grads(core_ref, dv1_ref, x_ref, dmix_ref, att_ref, gw_ref, *refs):
    outs, acc_ref = refs[:-1], refs[-1]
    page = pl.program_id(0)
    xn = (normalise(x_ref[...].astype(f32))[0] * gw_ref[...]).astype(bf)
    d1b = dv1_ref[...].astype(bf)

    @pl.when(page == 0)
    def _():
        for u in range(3):
            acc_ref[u] = t_dot(xn, dmix_ref[u])
        acc_ref[3] = t_dot(att_ref[...], d1b)

    @pl.when(page > 0)
    def _():
        for u in range(3):
            acc_ref[u] += t_dot(xn, dmix_ref[u])
        acc_ref[3] += t_dot(att_ref[...], d1b)

    @pl.when(page == pl.num_programs(0) - 1)
    def _():
        for u in range(4):
            emit_unit(core_ref, acc_ref[u], outs, u)


def window_end(dv1_ref, x_ref, dmix_ref, gw_ref, w_ref, grad_ref, dg_ref, gacc_ref):
    page = pl.program_id(0)
    hat, inv = normalise(x_ref[...].astype(f32))
    dxn = dot_t(dmix_ref[0], w_ref[0]) + dot_t(dmix_ref[1], w_ref[1]) + dot_t(dmix_ref[2], w_ref[2])
    dx, dg = norm_back(dxn.astype(bf).astype(f32), hat, inv, gw_ref[...])
    grad_ref[...] = (dv1_ref[...] + dx).astype(bf)

    @pl.when(page == 0)
    def _():
        gacc_ref[...] = dg

    @pl.when(page > 0)
    def _():
        gacc_ref[...] += dg

    dg_ref[...] = gacc_ref[...]


def slots_fwd(x_ref, g_ref, w_ref, bias_ref, mix_ref, att_ref, s1_ref):
    x = x_ref[...].astype(f32)
    xn = (normalise(x)[0] * g_ref[...]).astype(bf)
    for u in range(3):
        mix_ref[u] = dot(xn, w_ref[u]).astype(bf)
    for group in groups_of_pairs(x.shape[0], x.shape[0]):
        cs = [lanes(p) for p in group]
        outs = pairs_forward(*([mix_ref[u, :, c] for c in cs] for u in range(3)), bias_ref[...])
        for c, (out, _, _) in zip(cs, outs):
            att_ref[:, c] = out.astype(bf)
    s1_ref[...] = x + dot(att_ref[...], w_ref[3])


def own_columns(x, chip, span, step):
    total = x.shape[1]
    count = total // step * span
    row = lax.broadcasted_iota(jnp.int32, (total, count), 0)
    col = lax.broadcasted_iota(jnp.int32, (total, count), 1)
    at = lax.div(col, span) * step + chip * span + lax.rem(col, span)
    return dot(x, jnp.where(row == at, 1.0, 0.0).astype(bf)).astype(bf)


def emit_chip(core_ref, unit, outs, u, r):
    if len(outs) == 1:
        outs[0][u] = unit.astype(bf)
        return
    for z in range(unit.shape[0] // (2 * r)):
        emit(core_ref, unit[z * 2 * r : (z + 1) * 2 * r], outs[0], outs[1], (z, u))


def query_mlp(
    span,
    step,
    chip_ref,
    core_ref,
    s1_ref,
    read_ref,
    wo_ref,
    g_ref,
    up_ref,
    down_ref,
    cot_ref,
    out_ref,
    ds2_ref,
    message_ref,
    dg_ref,
    *outs,
):
    chip = chip_ref[0]
    reads = [read_ref[k] for k in range(GROUPS)]
    reading = jnp.concatenate([x[:, :GCOLS] for x in reads], axis=-1)
    sums = [x[:, GCOLS:] for x in reads] + [jnp.zeros((reading.shape[0], 128 - 3 * HEADS), bf)]
    message_ref[:, D : 2 * D] = reading
    message_ref[:, 2 * D :] = jnp.concatenate(sums, axis=-1)
    split = 2 if len(outs) == 2 and len(outs[0].shape) == 4 else 1
    s2 = s1_ref[...] + dot(reading, wo_ref[0])
    hat, inv = normalise(s2)
    xn = (hat * g_ref[...]).astype(bf)
    x_own = own_columns(xn, chip, span, step)
    cot = cot_ref[...]
    y, dxn = s2, None
    for k in range(4):
        up, down = up_ref[k], down_ref[k * D : (k + 1) * D]
        act, slope = gelu_both(dot(xn, up))
        act = act.astype(bf)
        y = y + dot(act, down)
        dpre = (dot_t(cot, down) * slope).astype(bf)
        part = dot_t(dpre, up)
        dxn = part if dxn is None else dxn + part
        emit_chip(core_ref, t_dot(x_own, dpre), outs[:split], k, span // 2)
        act_own = own_columns(act, chip, 4 * span, 4 * step)
        rows = act_own.shape[1]
        d_down = t_dot(act_own, cot)
        if split == 1:
            outs[1][0, k * rows : (k + 1) * rows] = d_down.astype(bf)
        else:
            part = rows // 8
            for t in range(4):
                both = [d_down[(4 * c + t) * part : (4 * c + t + 1) * part] for c in range(2)]
                emit(core_ref, jnp.concatenate(both, axis=0), outs[0], outs[1], (k, 5 + t))
    out_ref[...] = y.astype(bf)
    dx, dg = norm_back(dxn, hat, inv, g_ref[...])
    ds2 = cot.astype(f32) + dx
    ds2_ref[...] = ds2
    dg_ref[...] = dg
    d2b = ds2.astype(bf)
    message_ref[:, :D] = dot_t(d2b, wo_ref[0]).astype(bf)
    emit_chip(core_ref, t_dot(own_columns(reading, chip, span, step), d2b), outs[:split], 4, span // 2)


def query_back(
    span,
    step,
    chip_ref,
    core_ref,
    x_ref,
    s1_ref,
    ds2_ref,
    d_ref,
    gr_ref,
    wr_ref,
    ws_ref,
    mix_ref,
    att_ref,
    bias_ref,
    gs_ref,
    out_ref,
    dgs_ref,
    dgr_ref,
    *refs,
):
    outs, dmix_ref = refs[:-1], refs[-1]
    chip = chip_ref[0]
    hat, inv = normalise(s1_ref[...])
    rn_own = own_columns((hat * gr_ref[...]).astype(bf), chip, span, step)
    drn = dot_t(d_ref[0], wr_ref[0]) + dot_t(d_ref[1], wr_ref[1]) + dot_t(d_ref[2], wr_ref[2])
    dx, dg = norm_back(drn, hat, inv, gr_ref[...])
    dgr_ref[...] = dg
    for u in range(3):
        emit_chip(core_ref, t_dot(rn_own, d_ref[u]), outs, 4 + u, span // 2)
    ds1 = ds2_ref[...] + dx
    d1b = ds1.astype(bf)
    datt = dot_t(d1b, ws_ref[3]).astype(bf)
    emit_chip(core_ref, t_dot(own_columns(att_ref[...], chip, span, step), d1b), outs, 3, span // 2)
    for group in groups_of_pairs(datt.shape[0], datt.shape[0]):
        cs = [lanes(p) for p in group]
        parts = ([mix_ref[u, :, c] for c in cs] for u in range(3))
        grads = pairs_backward(*parts, [datt[:, c] for c in cs], [att_ref[:, c] for c in cs], bias_ref[...])
        for c, grad in zip(cs, grads):
            for u in range(3):
                dmix_ref[u, :, c] = grad[u].astype(bf)
    hat, inv = normalise(x_ref[...].astype(f32))
    xn_own = own_columns((hat * gs_ref[...]).astype(bf), chip, span, step)
    dxn = dot_t(dmix_ref[0], ws_ref[0]) + dot_t(dmix_ref[1], ws_ref[1]) + dot_t(dmix_ref[2], ws_ref[2])
    dx, dg = norm_back(dxn, hat, inv, gs_ref[...])
    dgs_ref[...] = dg
    out_ref[...] = (ds1 + dx).astype(bf)
    for u in range(3):
        emit_chip(core_ref, t_dot(xn_own, dmix_ref[u]), outs, u, span // 2)


def gain_grad(gain_ref, *pairs):
    total = sum(jnp.sum(grad * weight.astype(f32), axis=-1, keepdims=True) for grad, weight in pairs)
    return total / gain_ref[...].astype(f32)


def own_sum(z, own_ref, passed, u):
    total = own_ref[z, u].astype(f32)
    for ref in passed:
        total = total + ref[u].astype(f32)
    return total


def finish_most(
    nz,
    z_ref,
    net_ref,
    early_ref,
    up_ref,
    qup_ref,
    slots_ref,
    reader_ref,
    writer_ref,
    gp_ref,
    gv_ref,
    gs_ref,
    gr_ref,
    gq_ref,
    page_ref,
    late_ref,
    *refs,
):
    page, late = refs[: nz - 1], refs[nz - 1 : 2 * nz - 2]
    outs = refs[2 * nz - 2 :]
    d_up, d_down, d_qup, d_ro, d_qdown, d_reader, d_writer, d_wo, d_sq, d_so, d_gp, d_gv, d_gs, d_gr, d_gq = outs
    z = z_ref[0]

    def units(ref, start, count):
        return jnp.concatenate([ref[start + k].astype(f32) for k in range(count)], axis=-1)

    up = units(net_ref, 0, 4)
    d_up[...] = up
    d_gv[...] = gain_grad(gv_ref, (up, up_ref[...]))
    qup = units(early_ref, 0, 4)
    d_qup[...] = qup
    d_gq[...] = gain_grad(gq_ref, (qup, qup_ref[...]))
    d_ro[...] = early_ref[4].astype(f32)
    for k in range(4):
        d_down[k] = net_ref[4 + k].astype(f32)
        d_qdown[k] = early_ref[5 + k].astype(f32)
    read_k, read_v, write_q, out = (own_sum(z, page_ref, page, u) for u in range(4))
    sq = jnp.concatenate([own_sum(z, late_ref, late, u) for u in range(3)], axis=-1)
    so, read_q, write_k, write_v = (own_sum(z, late_ref, late, u) for u in range(3, 7))
    d_wo[...] = out
    d_sq[...] = sq
    d_so[...] = so
    d_reader[...] = jnp.concatenate([read_q, read_k, read_v], axis=-1)
    d_writer[...] = jnp.concatenate([write_q, write_k, write_v], axis=-1)
    d_gs[...] = gain_grad(gs_ref, (sq, slots_ref[...]))
    reader, writer = reader_ref[...], writer_ref[...]
    d_gp[...] = gain_grad(gp_ref, (read_k, reader[:, D : 2 * D]), (read_v, reader[:, 2 * D :]), (write_q, writer[:, :D]))
    d_gr[...] = gain_grad(gr_ref, (read_q, reader[:, :D]), (write_k, writer[:, D : 2 * D]), (write_v, writer[:, 2 * D :]))


def finish_windows(z_ref, gain_ref, qkv_ref, own_ref, *refs):
    passed, (d_qkv, d_out, d_gain) = refs[:-3], refs[-3:]
    z = z_ref[0]
    qkv = jnp.concatenate([own_sum(z, own_ref, passed, u) for u in range(3)], axis=-1)
    d_qkv[...] = qkv
    d_out[...] = own_sum(z, own_ref, passed, 3)
    d_gain[...] = gain_grad(gain_ref, (qkv, qkv_ref[...]))


def simple(body, name, args, outs, scratch=()):
    arrays = [a[0] if isinstance(a, tuple) else a for a in args]
    specs = [
        a[1]
        if isinstance(a, tuple)
        else pl.BlockSpec(memory_space=pltpu.SMEM)
        if a.ndim == 1
        else whole(a.shape)
        for a in args
    ]
    return call(
        body,
        name,
        tuple(sds(*o) for o in outs),
        specs,
        tuple(whole(o[0]) for o in outs),
        (1,),
        arrays,
        scratch=scratch,
        flops=1 << 30,
    )


def pack_rows(place, arrays, gains):
    window, out, slots, rows_of_slots, reader, rows_of_reader, writer, rows_of_writer, up, down, qup, qdown = arrays
    r = window.shape[0]

    def units(w):
        return [w[:, k * D : (k + 1) * D] for k in range(w.shape[1] // D)]

    def groups(win, o, sl, so, rd, ro, wr, wo, u, d, qu, qd, g):
        rd, wr = units(rd), units(wr)
        return (
            units(win) + [o] + units(sl) + [so, g],
            rd[1:] + wr[:1] + rd[:1] + wr[1:] + [wo],
            units(u) + [d[k] for k in range(4)],
            units(qu) + [ro] + [qd[k] for k in range(4)],
        )

    down, qdown = down.reshape(4, r, D), qdown.reshape(4, r, D)
    arrays = (window, out, slots, rows_of_slots, reader, rows_of_reader, writer, rows_of_writer, up, down, qup, qdown)
    if r % 8:
        return [jnp.stack(group) for group in groups(*arrays, gains)]

    def body(*refs):
        for group, out_ref in zip(groups(*refs[:13]), refs[13:]):
            for k, w in enumerate(group):
                out_ref[k] = w[...]

    return simple(body, "pack_rows", arrays + (gains,), [((n, r, D), bf) for n in (9, 7, 8, 9)])


def net_terms(place, ups, downs):
    nq, nz, _, r, _ = ups[0][0].shape
    half = nz // 2
    table = jnp.stack([place.core, place.chip]).astype(jnp.int32)

    def body(table_ref, *refs):
        outs = refs[8:]
        z = pl.program_id(0)
        first = jnp.where(table_ref[0] == 0, 1, 2)
        masks = (3 - first, 3, first, 0)
        for mask, out_ref in zip(masks, outs):
            at = jnp.bitwise_xor(table_ref[1], mask)
            for k in range(2):
                a, b = refs[2 * k], refs[2 * k + 1]
                for u in range(2):
                    out_ref[0, 2 * k + u] = (a[at, 0, u].astype(f32) + b[at, 0, u].astype(f32)).astype(bf)
            for k in range(2):
                a, b = refs[4 + 2 * k], refs[5 + 2 * k]

                @pl.when(z // half == k)
                def _():
                    for u in range(4):
                        out_ref[0, 4 + u] = (a[at, 0, u].astype(f32) + b[at, 0, u].astype(f32)).astype(bf)

    def down_block(k):
        return pl.BlockSpec((nq, 1, 4, r, D), lambda z: (0, jnp.clip(z - k * half, 0, half - 1), 0, 0, 0))

    up_block = pl.BlockSpec((nq, 1, 2, r, D), lambda z: (0, z, 0, 0, 0))
    return call(
        body,
        "net_terms",
        (sds((nz, 8, r, D), bf),) * 4,
        [pl.BlockSpec(memory_space=pltpu.SMEM)] + [up_block] * 4 + [down_block(0)] * 2 + [down_block(1)] * 2,
        (pl.BlockSpec((1, 8, r, D), lambda z: (z, 0, 0, 0)),) * 4,
        (nz,),
        (table, *ups[0], *ups[1], *downs[0], *downs[1]),
    )


def place_units(place, pieces, plain, tall):
    nz, n, r = pieces[0][0].shape[:3]
    left = n - plain - 4 * tall
    table = jnp.stack([place.core, place.chip % 4, place.z]).astype(jnp.int32)

    def body(table_ref, *args):
        refs, outs, (s_ref, sem) = args[:8], args[8:-2], args[-2:]
        core, chip, z = table_ref[0], table_ref[1], table_ref[2]
        now = pl.program_id(0)

        def targets():
            for c in range(2):
                owner = jnp.bitwise_xor(core, c)
                for i in range(4):
                    mask = jnp.where(owner == 0, i, (0, 2, 1, 3)[i])
                    yield 4 * c + i, s_ref.at[owner, jnp.bitwise_xor(chip, mask)]

        @pl.when(now == 0)
        def _():
            for to in range(nz):
                for k, there in targets():
                    pltpu.make_async_copy(refs[k].at[jnp.bitwise_xor(z, to)], there.at[to], sem.at[k, to]).start()

        for k, there in targets():
            pltpu.make_async_copy(refs[k].at[0], there.at[now], sem.at[k, now]).wait()
        for q in range(4):
            for u in range(plain):
                rows = [s_ref[c, q, now, u].astype(f32) for c in range(2)]
                outs[0][u, q] = jnp.concatenate(rows, axis=0).astype(bf)
            if tall:
                rows = [s_ref[c, q, now, plain + k].astype(f32) for c in range(2) for k in range(4)]
                outs[1][q] = jnp.concatenate(rows, axis=0).astype(bf)
            if left:
                rows = [s_ref[c, q, now, plain].astype(f32)[:1] for c in range(2)]
                outs[-1][q] = jnp.concatenate(rows + [jnp.zeros((6, D), f32)], axis=0)

    shapes = [jax.ShapeDtypeStruct((plain, 4 * nz, 2 * r, D), bf)]
    blocks = [pl.BlockSpec((plain, 4, 2 * r, D), lambda i: (0, i, 0, 0))]
    if tall:
        shapes.append(jax.ShapeDtypeStruct((4 * nz, 8 * r, D), bf))
        blocks.append(pl.BlockSpec((4, 8 * r, D), lambda i: (i, 0, 0)))
    if left:
        shapes.append(jax.ShapeDtypeStruct((4 * nz, 8, D), f32))
        blocks.append(pl.BlockSpec((4, 8, D), lambda i: (i, 0, 0)))
    out = pl.pallas_call(
        body,
        name="place_units",
        grid=(nz,),
        out_shape=tuple(shapes),
        in_specs=[pl.BlockSpec(memory_space=pltpu.SMEM)] + [pl.BlockSpec(memory_space=pl.ANY)] * 8,
        out_specs=tuple(blocks),
        scratch_shapes=[pltpu.VMEM((2, 4, nz, n, r, D), bf), pltpu.SemaphoreType.DMA((8, nz))],
        compiler_params=pltpu.CompilerParams(vmem_limit_bytes=60 * 1024 * 1024),
        cost_estimate=pl.CostEstimate(flops=0, bytes_accessed=n * D * D * 4, transcendentals=0),
    )(table, *pieces[0], *pieces[1])
    out = list(out)
    out[0] = out[0].reshape(plain, D, D)
    if tall:
        out[1] = out[1].reshape(4 * D, D)
    return out


def pick(stack, index, axis=0):
    return lax.dynamic_index_in_dim(stack, index, axis, keepdims=False)


def ordered(first, mine, other):
    return jnp.stack([jnp.where(first, mine, other), jnp.where(first, other, mine)])


class Place:
    def __init__(self):
        self.nz = lax.axis_size("dp")
        self.nf = lax.axis_size("fsdp")
        self.nq = self.nf // 2
        self.z = lax.axis_index("dp")
        self.f = lax.axis_index("fsdp")
        self.core = self.f % 2
        self.even = self.core == 0
        self.chip = self.f // 2
        self.group = self.chip % GROUPS

    def sibling(self, x):
        return lax.ppermute(x, "fsdp", [(f, f ^ 1) for f in range(self.nf)])

    def hop(self, x, mask, odd_mask=None):
        odd_mask = mask if odd_mask is None else odd_mask
        route = [(f, f ^ ((odd_mask if f % 2 else mask) << 1)) for f in range(self.nf)]
        return lax.ppermute(x, "fsdp", route)

    def across(self, x, mask):
        return lax.ppermute(x, "dp", [(z, z ^ mask) for z in range(self.nz)])

    def send_line(self, x):
        return [self.across(x, m) for m in range(1, self.nz)]

    def send_terms(self, now):
        return [self.across(pick(now, self.z ^ m), m) for m in range(1, self.nz)]

    def gather_square(self, block, bit):
        a, b = 1 << bit, 2 << bit
        first = self.hop(block, a, b)
        second = self.hop(block, b, a)
        return [block, first, second, self.hop(first, b, a)]

    def first_hop(self, x):
        return self.hop(x, 1, 2)

    def second_hop(self, x):
        return self.hop(x, 2, 1)

    def arranged(self, pieces, bit, odd):
        here = (self.chip >> bit) % 4
        stack = jnp.stack(pieces)
        at = [0, 1, 2, 3]
        swapped = jnp.where(odd, jnp.array([0, 2, 1, 3]), jnp.array(at))
        return jnp.stack([pick(stack, swapped[here ^ k]) for k in at])

    def gather_plain(self, block):
        stack = jnp.stack([block] + self.send_line(block))
        now = jnp.stack([pick(stack, self.z ^ k) for k in range(self.nz)])
        levels = 0
        for bit in range(0, self.nq.bit_length() - 1, 2):
            now = self.arranged(self.gather_square(now, bit), bit, ~self.even)
            levels += 1
        now = ordered(self.even, now, self.sibling(now))
        n, r = block.shape[:2]
        now = now.reshape(2, self.nq, self.nz, n, r, D)
        return jnp.transpose(now, (3, 2, 1, 0, 4, 5))

    def chip_terms(self, pairs):
        def parts(i, kind=f32):
            blocks = []
            for pair in pairs:
                along = []
                for keep, other in pair if isinstance(pair[0], (tuple, list)) else [pair]:
                    shape = (4,) + (() if self.nq == 4 else (self.nq // 4,)) + keep.shape[1:]
                    block = pick(keep.reshape(shape), i).astype(f32) + pick(other.reshape(shape), i).astype(f32)
                    along.append((block if self.nq == 4 else jnp.swapaxes(block, 0, 1)).astype(kind))
                blocks.append(along[0] if len(along) == 1 else jnp.concatenate(along))
            return jnp.concatenate(blocks, axis=-3)

        return parts

    def halves(self, x, r):
        x = x.reshape((-1, self.nz, self.nq, 2, r, x.shape[-1]))

        def rows(which):
            return jnp.transpose(pick(x, which, 3), (2, 1, 0, 3, 4))

        return rows(self.core), rows(1 - self.core)

    def square_terms(self, parts):
        bit = (self.nq.bit_length() - 1) - 2
        here = (self.chip >> bit) % 4
        first = jnp.where(self.even, 1, 2)
        masks = (3 - first, jnp.full_like(first, 3), first, jnp.zeros_like(first))
        return [parts(here ^ mask, kind) for mask, kind in zip(masks, (bf, bf, f32, f32))]

    def outer_hop(self, which, x):
        bit = (self.nq.bit_length() - 1) - 2
        a, b = 1 << bit, 2 << bit
        return self.hop(x, a, b) if which == 0 else self.hop(x, b, a)

    def inner_square(self, now):
        if now.ndim > 4:
            first = jnp.where(self.even, 1, 2)
            here = self.chip % 4

            def at(mask):
                return pick(now, here ^ mask, 1).astype(f32)

            second = self.hop(at(3 - first).astype(bf), 2, 1)
            corner = self.hop(at(3).astype(bf), 2, 1)
            moved = self.hop((at(first) + corner.astype(f32)).astype(bf), 1, 2)
            now = (at(0) + moved.astype(f32) + second.astype(f32)).astype(bf)
        return now

    def own_terms(self, now):
        return pick(now, self.z).astype(f32)

    def group_hops(self, x):
        return [self.hop(x, mask) for mask in range(1, GROUPS)]

    def in_order(self, pieces):
        stack = jnp.stack(pieces)
        return jnp.stack([pick(stack, self.group ^ k) for k in range(GROUPS)])

    def to_groups(self, blocks):
        return [self.hop(pick(blocks, self.group ^ mask), mask) for mask in range(1, GROUPS)]

    def owned_rows(self, mine, axis=0):
        own = lax.dynamic_slice_in_dim(mine, self.f * Q_DEV, Q_DEV, axis)
        give = lax.dynamic_slice_in_dim(mine, (self.f ^ 1) * Q_DEV, Q_DEV, axis)
        return ordered(self.even, own, self.sibling(give))


def tie(*arrays):
    return lax.optimization_barrier(arrays)


def stage(*moves):
    operands = tie(*[operand for _, operand in moves])
    return tie(*[move(operand) for (move, _), operand in zip(moves, operands)])


def split_three(x):
    hi = lax.reduce_precision(x, 8, 7)
    mid = lax.reduce_precision(x - hi, 8, 7)
    return [hi.astype(bf), mid.astype(bf), (x - hi - mid).astype(bf)]


def join_three(x):
    a, b, c = jnp.split(x.astype(f32), 3, axis=-1)
    return (a + b) + c


def columns(weight):
    rows, width = weight.shape
    return [weight[:, k * D : (k + 1) * D] for k in range(width // D)]


def strip_bias(place, bands, height):
    half = WIN // 2
    rows = (place.f % bands) * height + jnp.arange(height, dtype=jnp.int32)
    cols = (place.f // bands) * WIN + jnp.arange(WIN, dtype=jnp.int32)

    def label(at, total):
        return (at >= total - WIN).astype(jnp.int32) + (at >= total - half).astype(jnp.int32)

    labels = label(rows, height * bands)[:, None] * 3 + label(cols, WIN * WCOLS)
    labels = labels.reshape(height // WIN, PATCH)
    return jnp.where(labels[:, :, None] == labels[:, None, :], 0.0, -1e30).astype(f32)


def roll_beside(x, place, bands):
    route = [((f + bands) % place.nf, f) for f in range(place.nf)]
    return lax.ppermute(x, "fsdp", route)


def roll_in(x, beside, place, bands):
    half = WIN // 2
    pages, height = x.shape[:2]
    if bands > 1:
        x = jnp.concatenate([x[:, :, half:], beside.reshape(pages, height, half, D)], axis=2)
        route = [(f // bands * bands + (f + 1) % bands, f) for f in range(place.nf)]
        below = lax.ppermute(x[:, :half], "fsdp", route)
        return jnp.concatenate([x[:, half:], below], axis=1).reshape(-1, D)

    def body(x_ref, b_ref, out_ref, tall_ref, side_ref):
        side_ref[...] = b_ref[...].astype(f32)
        for to in range(height):
            row = (to + half) % height
            tall_ref[to * WIN : to * WIN + half] = x_ref[0, row].astype(f32)[half:]
            tall_ref[to * WIN + half : (to + 1) * WIN] = side_ref[row * half : (row + 1) * half]
        out_ref[...] = tall_ref[...].astype(bf)

    return call(
        body,
        "roll_in",
        sds((pages * height * WIN, D), bf),
        [per_page((1, height, WIN, D), 0), per_page((height * half, D), 0)],
        per_page((height * WIN, D), 0),
        (pages,),
        (x, beside),
        scratch=(pltpu.VMEM((height * WIN, D), f32), pltpu.VMEM((height * half, D), f32)),
        flops=1 << 20,
    )


def last_columns(x):
    half = WIN // 2
    height = x.shape[0] // MICRO // WIN

    def body(x_ref, out_ref, tall_ref, side_ref):
        tall_ref[...] = x_ref[...].astype(f32)
        for row in range(height):
            side_ref[row * half : (row + 1) * half] = tall_ref[row * WIN + half : (row + 1) * WIN]
        out_ref[...] = side_ref[...].astype(bf)

    return call(
        body,
        "last_columns",
        sds((MICRO * height * half, D), bf),
        [per_page((height * WIN, D), 0)],
        per_page((height * half, D), 0),
        (MICRO,),
        (x,),
        (pltpu.VMEM((height * WIN, D), f32), pltpu.VMEM((height * half, D), f32)),
    )


def roll_out(x, beside, place, bands):
    half = WIN // 2
    height = x.shape[0] // MICRO // WIN
    shape = (MICRO, height, WIN, D)
    if bands > 1:
        x = jnp.concatenate([beside.reshape(MICRO, height, half, D), x.reshape(shape)[:, :, :half]], axis=2)
        rows = [(f, f // bands * bands + (f + 1) % bands) for f in range(place.nf)]
        above = lax.ppermute(x[:, -half:], "fsdp", rows)
        return jnp.concatenate([above, x[:, :-half]], axis=1)

    def body(x_ref, b_ref, out_ref, tall_ref, side_ref):
        tall_ref[...] = x_ref[...].astype(f32)
        side_ref[...] = b_ref[...].astype(f32)
        for row in range(height):
            parts = [side_ref[row * half : (row + 1) * half], tall_ref[row * WIN : row * WIN + half]]
            out_ref[0, (row + half) % height] = jnp.concatenate(parts, axis=0).astype(bf)

    return call(
        body,
        "roll_out",
        sds(shape, bf),
        [per_page((height * WIN, D), 0), per_page((height * half, D), 0)],
        per_page((1,) + shape[1:], 0),
        (MICRO,),
        (x, beside),
        (pltpu.VMEM((height * WIN, D), f32), pltpu.VMEM((height * half, D), f32)),
    )


def local(
    visual,
    query_slots,
    lengths,
    slot_order,
    norm_window,
    window_qkv,
    window_out,
    norm_slots,
    slots_qkv,
    slots_out,
    norm_reader,
    norm_page,
    reader_qkv,
    reader_out,
    writer_qkv,
    writer_out,
    norm_visual_mlp,
    visual_up,
    visual_down,
    norm_query_mlp,
    query_up,
    query_down,
    visual_cot,
    query_cot,
):
    place = Place()
    nz, nf, nq, core, even = place.nz, place.nf, place.nq, place.core, place.even
    extra = nq // GROUPS
    bands = nf // WCOLS
    height = visual.shape[1]
    page_rows = height * WIN
    rows = MICRO * page_rows
    slots = Q_DEV * nf
    r = window_out.shape[0]

    fast = r % 8 == 0 and nq == 4
    gains = jnp.stack([norm_window, norm_slots, norm_reader, norm_page, norm_visual_mlp, norm_query_mlp])
    gains = jnp.zeros((r, D), bf).at[0, : 6 * r].set(gains.reshape(6 * r))
    arrays = (
        window_qkv,
        window_out,
        slots_qkv,
        slots_out,
        reader_qkv,
        reader_out,
        writer_qkv,
        writer_out,
        visual_up,
        visual_down,
        query_up,
        query_down,
    )
    one, two, three, four = pack_rows(place, arrays, gains)

    def squares(x):
        return [place.first_hop(x), place.second_hop(x)]

    def siblings(x):
        return jax.tree.map(place.sibling, x)

    def assemble(block, pieces, others, plain, tall):
        if fast:
            return place_units(place, [pieces, others], plain, tall)
        units = place.gather_plain(block)
        out = [units[:plain].reshape(plain, D, D)]
        if tall:
            out.append(jnp.transpose(units[plain:], (1, 2, 3, 0, 4, 5)).reshape(4 * D, D))
        elif block.shape[0] > plain:
            rows_left = units[plain, ..., 0, :].reshape(nz * nq, 2, D).astype(f32)
            out.append(jnp.pad(rows_left, ((0, 0), (0, 6), (0, 0))))
        return out

    positions = (slot_order[:, :, None] * Q_DEV + jnp.arange(Q_DEV, dtype=jnp.int32)).reshape(MICRO, slots)
    live = jnp.where(positions < lengths[:, None], 0.0, -1e30).astype(f32).reshape(MICRO, 1, slots)
    own_live = pick(live, core)
    bias = strip_bias(place, bands, height)
    chip_id = place.chip.astype(jnp.int32).reshape(1)
    core_id = core.astype(jnp.int32).reshape(1)

    def spread(x, bit):
        return place.hop(x, 1 << bit)

    def spread_order(x, got, bit):
        upper = (place.chip >> bit) % 2 == 1
        return jnp.concatenate([jnp.where(upper, got, x), jnp.where(upper, x, got)], axis=1)

    def all_dp(block, got):
        return jnp.stack([block] + list(got))

    act_block = per_page((page_rows, D), 0)
    three_block = per_page((3, page_rows, D), 1)

    def part_of(size, index, full):
        return full, pl.BlockSpec((size, D, D), lambda *_: (index, 0, 0), pipeline_mode=pl.Buffered(1))

    def run_first(args):
        sib_c, x = args
        w_one, gain_all = assemble(one, [all_one, f_one, s_one, c_one], [sib_one, sib_f_one, sib_s_one, sib_c], 8, 0)
        gain_all = gain_all[:, :2, : 6 * r].reshape(nz * nq * 2, 6, r)
        gain_all = jnp.transpose(gain_all, (1, 0, 2)).reshape(6, 1, D)
        windows = call(
            window_fwd,
            "window_fwd",
            (sds((3, rows, D), bf), sds((rows, D), bf), sds((rows, D), f32)),
            [act_block, whole(bias.shape), whole((1, D)), part_of(4, 0, None)[1]],
            (three_block, act_block, act_block),
            (MICRO,),
            (x, bias, gain_all[0], w_one),
            flops=2 * rows * 4 * D * D,
        )
        return w_one, gain_all, windows

    roll = partial(roll_beside, place=place, bands=bands)
    ends = jnp.stack([query_slots, query_cot])
    got, beside_x, ends_two = stage(
        (place.send_line, one),
        (roll, visual[:, :, : WIN // 2].reshape(-1, D)),
        (place.sibling, pick(ends, 1 - core, 1)),
    )
    all_one = all_dp(one, got)
    ends = jnp.swapaxes(ordered(even, pick(ends, core, 1), ends_two), 0, 1).reshape(2, 2 * Q_DEV, D)
    got, (f_one, s_one) = stage((place.send_line, two), (squares, all_one))
    c_one, ends_two, sib_one, sib_f_one, sib_s_one, x = stage(
        (place.second_hop, f_one),
        (partial(spread, bit=0), ends),
        (place.sibling, all_one),
        (place.sibling, f_one),
        (place.sibling, s_one),
        (lambda args: roll_in(*args, place, bands), (visual, beside_x)),
    )
    ends = spread_order(ends, ends_two, 0)
    sib_c_one, got = tie(place.sibling(c_one), got)
    ends_two = spread(ends, 1)
    ends = spread_order(ends, ends_two, 1)
    for bit in range(2, nq.bit_length() - 1):
        ends = spread_order(ends, spread(ends, bit), bit)
    xs, xs_cot = ends[0], ends[1]
    all_two = all_dp(two, got)
    got, (f_two, s_two), first = stage(
        (place.send_line, three), (squares, all_two), (run_first, (sib_c_one, x))
    )
    all_three = all_dp(three, got)
    w_one, gain_all, (mix, att, v1) = first
    g_window, g_slots, g_reader, g_page, g_vmlp, g_qmlp = (gain_all[k] for k in range(6))

    def run_slots(args):
        return simple(
            slots_fwd,
            "slots_fwd",
            (args[0], g_slots, part_of(4, 1, args[1]), own_live),
            [((3, slots, D), bf), ((slots, D), bf), ((slots, D), f32)],
        )

    c_two, sib_two, sib_f_two, sib_s_two, (mix_q, att_q, s1) = stage(
        (place.second_hop, f_two),
        (place.sibling, all_two),
        (place.sibling, f_two),
        (place.sibling, s_two),
        (run_slots, (xs, w_one)),
    )
    sib_c_two, all_three = tie(place.sibling(c_two), all_three)
    def run_second(args):
        sib_c, v1, s1 = args
        (w_two,) = assemble(two, [all_two, f_two, s_two, c_two], [sib_two, sib_f_two, sib_s_two, sib_c], 7, 0)
        (rd_own,) = simple(
            normed_units, "slots_units", (s1, g_reader, part_of(3, 1, w_two)), [((3, slots, D), bf)]
        )
        pk = call(
            normed_units,
            "page_units",
            sds((3, rows, D), bf),
            [act_block, whole((1, D)), part_of(3, 0, None)[1]],
            three_block,
            (MICRO,),
            (v1, g_page, w_two),
            flops=2 * rows * 3 * D * D,
        )
        return w_two, rd_own, pk

    got, (f_three, s_three), (w_two, rd_own, pk) = stage(
        (place.send_line, four), (squares, all_three), (run_second, (sib_c_two, v1, s1))
    )
    rd_two = place.sibling(rd_own)
    rd_two, got = tie(rd_two, got)
    all_four = all_dp(four, got)
    rd = jnp.swapaxes(ordered(even, rd_own, rd_two), 0, 1)
    rq, wk, wv = rd[0], rd[1], rd[2]
    slot_block = per_page((1, slots, D), 0)
    stat_block = per_page((1, slots, 128), 0)

    def of_pk(u):
        return pl.BlockSpec((1, page_rows, D), lambda p: (u, p, 0))

    def merge(terms):
        width = terms[0].shape[-1] // (HEAD + 1) * HEAD
        lse = jnp.stack([t[..., width:] for t in terms])
        top = jnp.max(lse, axis=0)
        weights = jnp.exp(lse - top)
        total = jnp.sum(weights, axis=0)
        shares = weights / total
        out = sum(t[..., :width] * jnp.repeat(share, HEAD, axis=-1) for t, share in zip(terms, shares))
        return jnp.concatenate([out, top + jnp.log(total)], axis=-1)

    def run_read(args):
        return call(
            read_fwd,
            "read_fwd",
            (sds((MICRO, slots, D), f32), sds((MICRO, slots, 128), f32)),
            [slot_block, of_pk(0), of_pk(1)],
            (slot_block, stat_block),
            (MICRO,),
            args,
            flops=2 * rows * slots * D * 4,
        )

    c_three, sib_three, sib_f_three, sib_s_three, (o_part, lse_part) = stage(
        (place.second_hop, f_three),
        (place.sibling, all_three),
        (place.sibling, f_three),
        (place.sibling, s_three),
        (run_read, (rq, pk, pk)),
    )
    terms = jnp.concatenate([o_part, lse_part[..., :HEADS]], axis=-1)
    live_block = per_page((1, 1, slots), 0)

    def run_write(args):
        return call(
            write_fwd,
            "write_fwd",
            (sds((rows, D), bf), sds((rows, D), f32)),
            [act_block, of_pk(2), slot_block, slot_block, live_block, part_of(1, 6, None)[1]],
            (act_block, act_block),
            (MICRO,),
            args,
            flops=2 * rows * D * D,
        )

    terms_two, sib_c_three, beside_cot, (writing, v2) = stage(
        (place.sibling, pick(terms, 1 - core)),
        (place.sibling, c_three),
        (roll, visual_cot[:, :, : WIN // 2].reshape(-1, D)),
        (run_write, (v1, pk, wk, wv, live, w_two)),
    )
    terms = merge([pick(terms, core), terms_two])
    blocks = jnp.concatenate(
        [terms[:, :D].reshape(slots, GROUPS, GCOLS), terms[:, D:].reshape(slots, GROUPS, GHEADS)], axis=-1
    )
    blocks = jnp.swapaxes(blocks, 0, 1)
    got, cot, (w_up, w_down) = stage(
        (place.to_groups, blocks),
        (lambda args: roll_in(*args, place, bands), (visual_cot, beside_cot)),
        (
            lambda sib_c: assemble(
                three, [all_three, f_three, s_three, c_three], [sib_three, sib_f_three, sib_s_three, sib_c], 4, 1
            ),
            sib_c_three,
        ),
    )
    chunk = D
    steps = 2 * D // chunk
    per_unit = D // chunk

    def once(*shape):
        return pl.BlockSpec(shape, lambda j: (0,) * len(shape), pipeline_mode=pl.Buffered(1))

    smem = pl.BlockSpec(memory_space=pltpu.SMEM)
    if fast:
        up_shapes = [sds((nq, nz, 2, r, D), bf)] * 2
        up_outs = [pl.BlockSpec((nq, nz, 1, r, chunk), lambda j: (0, 0, j // per_unit, 0, j % per_unit))] * 2
        several = chunk // (8 * r)
        down_shapes = [sds((nq, nz // 2, 4 * r, D), bf)] * 2
        down_outs = [
            pl.BlockSpec((several, 1, 4 * r, D), lambda j: (j % (nq // several), j // (nq // several), 0, 0))
        ] * 2
    else:
        up_shapes = [sds((2, D, D), bf)]
        up_outs = [pl.BlockSpec((1, D, chunk), lambda j: (j // per_unit, 0, j % per_unit))]
        down_shapes = [sds((2 * D, D), bf)]
        down_outs = [pl.BlockSpec((chunk, D), lambda j: (j, 0))]

    def run_mlp(last, args):
        at = steps if last else 0
        up_in = pl.BlockSpec((1, D, chunk), lambda j: ((j + at) // per_unit, 0, (j + at) % per_unit))
        down_in = pl.BlockSpec((chunk, D), lambda j: (j + at, 0))
        wide = once(rows, D)
        scratch = (pltpu.VMEM((rows, D), bf),)
        if last:
            shapes = [sds((rows, D), bf), sds((rows, D), f32), sds((1, D), f32)]
            outs = [wide, wide, once(1, D)]
            scratch = scratch + (pltpu.VMEM((rows, D), f32), pltpu.VMEM((rows, D), f32))
        else:
            shapes = [sds((rows, D), f32), sds((rows, D), f32)]
            outs = [wide, wide]
        out = call(
            partial(mlp_both, steps, last, 4 * r),
            "mlp_both",
            tuple(shapes + up_shapes + down_shapes),
            [smem, wide, once(1, D), up_in, down_in, wide] + [wide, wide] * last,
            tuple(outs + up_outs + down_outs),
            (steps,),
            (core_id,) + args,
            scratch=scratch,
            flops=2 * rows * 12 * D * D,
        )
        count = len(outs)
        if fast:
            up = out[count : count + 2]
            down = [y.reshape(nq, nz // 2, 4, r, D) for y in out[count + 2 :]]
        else:
            up = place.halves(out[count], r)
            d = out[count + 1].reshape(nz // 2, nq, 2, 4, r, D)
            down = [jnp.swapaxes(pick(d, which, 2), 0, 1) for which in (core, 1 - core)]
        return tuple(out[:count]) + (list(up), list(down))

    def run_grads(body, name, shapes, specs, outs, args, units, scratch, flops):
        if fast:
            unit_shapes = [sds((nq, nz, units, r, D), bf)] * 2
        else:
            unit_shapes = [sds((units, D, D), bf)]
        unit_outs = [whole(y.shape) for y in unit_shapes]
        out = call(
            body,
            name,
            tuple(shapes + unit_shapes),
            [smem] + specs,
            tuple(outs + unit_outs),
            (MICRO,),
            (core_id,) + args,
            scratch=scratch,
            flops=flops,
        )
        count = len(outs)
        if fast:
            pair = list(out[count:])
        else:
            pair = list(place.halves(out[count], r))
        return tuple(out[:count]) + (pair,)

    reading = merge([pick(blocks, place.group)] + list(got))
    for bit in range(2, nq.bit_length() - 1):
        reading = merge([reading, place.hop(reading, 1 << bit)])
    message = jnp.concatenate([reading[:, :GCOLS].astype(bf)] + split_three(reading[:, GCOLS:]), axis=-1)
    reads, f_four, sib_four, (y, dxn, up_one, down_one) = stage(
        (place.group_hops, message),
        (place.first_hop, all_four),
        (place.sibling, all_four),
        (partial(run_mlp, False), (v2, g_vmlp, w_up, w_down, cot)),
    )
    c_four, s_four, sib_f_four, up_one_got, down_one_got, (v3, dv2, dg_vmlp, up_two, down_two) = stage(
        (place.second_hop, f_four),
        (place.second_hop, all_four),
        (place.sibling, f_four),
        (place.sibling, up_one[1]),
        (place.sibling, down_one[1]),
        (partial(run_mlp, True), (v2, g_vmlp, w_up, w_down, cot, y, dxn)),
    )
    reads = place.in_order([message] + list(reads))

    def run_write_bwd(args):
        return run_grads(
            write_bwd,
            "write_bwd",
            [sds((rows, D), bf), sds((MICRO, slots, D), bf), sds((MICRO, slots, D), bf)],
            [act_block, act_block, of_pk(2), slot_block, slot_block, live_block, part_of(1, 6, None)[1]],
            [act_block, slot_block, slot_block],
            args,
            1,
            (pltpu.VMEM((D, D), f32),),
            4 * rows * D * D,
        )

    sib_c_four, sib_s_four, up_two_got, down_two_got, (dwq, dwk, dwv, pair_wo) = stage(
        (place.sibling, c_four),
        (place.sibling, s_four),
        (place.sibling, up_two[1]),
        (place.sibling, down_two[1]),
        (run_write_bwd, (dv2, writing, pk, wk, wv, live, w_two)),
    )
    down_pairs = [(down_one[0], down_one_got), (down_two[0], down_two_got)]
    up_pairs = [(up_one[0], up_one_got), (up_two[0], up_two_got)]
    if fast:
        second, corner, first, own_net = net_terms(place, up_pairs, down_pairs)
    else:
        second, corner, first, own_net = place.square_terms(place.chip_terms(up_pairs + [down_pairs]))

    def run_query(args):
        units, w_down = assemble(
            four, [all_four, f_four, s_four, c_four], [sib_four, sib_f_four, sib_s_four, sib_c_four], 5, 1
        )
        s1, reads = args
        up_block = pl.BlockSpec((4, D, D), lambda *_: (0, 0, 0), pipeline_mode=pl.Buffered(1))
        return simple(
            partial(query_mlp, 2 * r, D // nz),
            "query_mlp",
            (chip_id, core_id, s1, reads, part_of(1, 4, units), g_qmlp, (units, up_block), w_down, xs_cot),
            [((slots, D), bf), ((slots, D), f32), ((slots, 2 * D + 128), bf), ((1, D), f32)]
            + (chip_shapes(9, r) if fast else chip_shapes(5, r) + chip_shapes(1, 4 * r)),
        )

    def chip_shapes(k, r):
        return [((nz, k, r, D), bf)] * 2 if fast else [((k, nz * 2 * r, D), bf)]

    def chip_pair(outs, r):
        if fast:
            return list(outs)
        x = outs[0].reshape(-1, nz, 2, r, D)
        return [jnp.swapaxes(pick(x, which, 2), 0, 1) for which in (core, 1 - core)]

    second, corner, (q_out, ds2, message, dg_qmlp, *d_early) = stage(
        (partial(place.outer_hop, 1), second.astype(bf)),
        (partial(place.outer_hop, 1), corner.astype(bf)),
        (run_query, (s1, reads)),
    )
    own_net = own_net.astype(f32) + second.astype(f32)
    first = (first.astype(f32) + corner.astype(f32)).astype(bf)

    if fast:
        keep_early, give_early = d_early
    else:
        pairs = zip(chip_pair(d_early[:1], r), chip_pair(d_early[1:], 4 * r))
        keep_early, give_early = (jnp.concatenate([a, b.reshape(nz, 4, r, D)], axis=1) for a, b in pairs)
    message_two, early_got = stage((place.sibling, message), (place.sibling, give_early))
    message = ordered(even, message, message_two)
    early = (keep_early.astype(f32) + early_got.astype(f32)).astype(bf)
    early_sum = lax.psum_scatter(early.reshape(nz, 9 * r, D), "dp", scatter_dimension=0).reshape(9, r, D)

    def run_read_bwd(args):
        grad_block = pl.BlockSpec((1, slots, D), lambda p: (p, 0, 0))
        read_block = pl.BlockSpec((1, slots, D), lambda p: (p, 0, 1))
        sums_block = pl.BlockSpec((1, slots, 128), lambda p: (p, 0, 2 * D // 128))
        return call(
            read_bwd,
            "read_bwd",
            (sds((MICRO, slots, D), bf), sds((rows, D), bf), sds((rows, D), bf)),
            [slot_block, of_pk(0), of_pk(1), grad_block, read_block, sums_block],
            (slot_block, act_block, act_block),
            (MICRO,),
            args,
            flops=2 * rows * slots * D * 10,
        )

    drq, dk, dv = run_read_bwd((rq, pk, pk, message, message, message))

    def run_page_bwd(args):
        return run_grads(
            page_bwd,
            "page_bwd",
            [sds((rows, D), f32), sds((1, D), f32)],
            [act_block, act_block, act_block, act_block, act_block, whole((1, D)), whole((3, D, D))],
            [act_block, whole((1, D))],
            args,
            3,
            (pltpu.VMEM((3, D, D), f32), pltpu.VMEM((1, D), f32)),
            2 * rows * 6 * D * D,
        )

    d_slots = jnp.stack([drq, dwk, dwv], axis=1)
    slots_two, first, (dv1, dg_page, pair_page) = stage(
        (place.sibling, pick(d_slots, 1 - core)),
        (partial(place.outer_hop, 0), first),
        (run_page_bwd, (v1, dv2, dk, dv, dwq, g_page, w_two)),
    )
    own_net = place.inner_square((own_net + first.astype(f32)).astype(bf))
    net_sum = lax.psum_scatter(own_net.reshape(nz, 8 * r, D), "dp", scatter_dimension=0).reshape(8, r, D)
    d_slots = (pick(d_slots, core).astype(f32) + slots_two.astype(f32)).astype(bf)
    d_slots = jnp.transpose(d_slots.reshape(3, slots, GROUPS, GCOLS), (2, 0, 1, 3))

    def run_window_bwd(page, args):
        here = pl.BlockSpec((page_rows, D), lambda i: (page, 0))
        three_here = pl.BlockSpec((3, page_rows, D), lambda i: (0, page, 0))
        return pl.pallas_call(
            window_bwd,
            name="window_bwd",
            out_shape=sds((3, rows, D), bf),
            grid=(1,),
            in_specs=[here, three_here, here, whole(bias.shape), part_of(4, 0, None)[1]]
            + [pl.BlockSpec(memory_space=pl.ANY)] * page,
            out_specs=three_here,
            scratch_shapes=(pltpu.VMEM((page_rows, D), bf),),
            input_output_aliases={5: 0} if page else {},
            compiler_params=pltpu.CompilerParams(vmem_limit_bytes=58 * 1024 * 1024),
            cost_estimate=pl.CostEstimate(flops=rows * 2 * D * D, bytes_accessed=1 << 20, transcendentals=0),
        )(*args)

    page_got, got, dmix = stage(
        (siblings, [pair_page[1], pair_wo[1]]),
        (place.to_groups, d_slots),
        (partial(run_window_bwd, 0), (dv1, mix, att, bias, w_one)),
    )
    d_rd = sum(x.astype(f32) for x in [pick(d_slots, place.group)] + list(got)).astype(bf)
    for bit in range(2, nq.bit_length() - 1):
        d_rd = (d_rd.astype(f32) + place.hop(d_rd, 1 << bit).astype(f32)).astype(bf)
    second, corner, first, own_page = place.square_terms(
        place.chip_terms([(pair_page[0], page_got[0]), (pair_wo[0], page_got[1])])
    )
    rds, second, corner, dmix = stage(
        (place.group_hops, d_rd),
        (partial(place.outer_hop, 1), second.astype(bf)),
        (partial(place.outer_hop, 1), corner.astype(bf)),
        (partial(run_window_bwd, 1), (dv1, mix, att, bias, w_one, dmix)),
    )
    own_page = own_page + second.astype(f32)
    first = (first.astype(f32) + corner.astype(f32)).astype(bf)
    d_rd = jnp.transpose(place.in_order([d_rd] + list(rds)), (1, 2, 0, 3)).reshape(3, slots, D)

    def run_query_back(args):
        return simple(
            partial(query_back, 2 * r, D // nz),
            "query_back",
            (*args[:7], part_of(3, 1, args[7]), part_of(4, 1, args[8]), *args[9:]),
            [((slots, D), bf), ((1, D), f32), ((1, D), f32)] + chip_shapes(7, r),
            scratch=(pltpu.VMEM((3, slots, D), bf),),
        )

    def run_window_grads(args):
        return run_grads(
            window_grads,
            "window_grads",
            [],
            [act_block, act_block, three_block, act_block, whole((1, D))],
            [],
            args,
            4,
            (pltpu.VMEM((4, D, D), f32),),
            2 * rows * 4 * D * D,
        )

    def right(x):
        return lax.ppermute(x, "fsdp", [(f, (f + bands) % nf) for f in range(nf)])

    first, query_out, (x_grad, dg_slots, dg_reader, *d_late), side_out = stage(
        (partial(place.outer_hop, 0), first),
        (place.owned_rows, q_out),
        (
            run_query_back,
            (chip_id, core_id, xs, s1, ds2, d_rd, g_reader, w_two, w_one, mix_q, att_q, own_live, g_slots),
        ),
        (last_columns, v3),
    )
    own_page = place.inner_square((own_page + first.astype(f32)).astype(bf))
    keep_late, give_late = chip_pair(d_late, r)
    late_got, page_passed, side_out, (pair_window,) = stage(
        (place.sibling, give_late),
        (place.send_terms, own_page),
        (right, side_out),
        (run_window_grads, (dv1, x, dmix, att, g_window)),
    )
    pair_window, net_sum, early_sum = tie(pair_window, net_sum, early_sum)
    late = (keep_late.astype(f32) + late_got.astype(f32)).astype(bf)
    (window_got,) = stage((place.sibling, pair_window[1]))
    second, corner, first, own_window = place.square_terms(place.chip_terms([(pair_window[0], window_got)]))

    def run_window_end(args):
        return call(
            window_end,
            "window_end",
            (sds((rows, D), bf), sds((1, D), f32)),
            [act_block, act_block, three_block, whole((1, D)), part_of(4, 0, None)[1]],
            (act_block, whole((1, D))),
            (MICRO,),
            args,
            scratch=(pltpu.VMEM((1, D), f32),),
            flops=2 * rows * 3 * D * D,
        )

    def run_ends(args):
        v3, side_out, *rest = args
        v_grad, dg_window = run_window_end(rest)
        return v_grad, last_columns(v_grad), roll_out(v3, side_out, place, bands)

    second, corner, late_passed, (v_grad, side_grad, visual_out) = stage(
        (partial(place.outer_hop, 1), second.astype(bf)),
        (partial(place.outer_hop, 1), corner.astype(bf)),
        (place.send_terms, late),
        (run_ends, (v3, side_out, dv1, x, dmix, g_window, w_one)),
    )
    own_window = own_window + second.astype(f32)
    first = (first.astype(f32) + corner.astype(f32)).astype(bf)
    first, query_grad = stage((partial(place.outer_hop, 0), first), (place.owned_rows, x_grad))
    own_window = place.inner_square((own_window + first.astype(f32)).astype(bf))
    z_id = place.z.astype(jnp.int32).reshape(1)

    def column(gain):
        return gain.reshape(r, 1)

    def run_finish(args):
        net_sum, early_sum, own_page, page_passed, late, late_passed = args
        rows_of = [((r, 4 * D), f32), ((4, r, D), f32), ((r, 4 * D), f32), ((r, D), f32), ((4, r, D), f32)]
        rows_of += [((r, 3 * D), f32)] * 2 + [((r, D), f32), ((r, 3 * D), f32), ((r, D), f32)] + [((r, 1), f32)] * 5
        return simple(
            partial(finish_most, nz),
            "finish_most",
            (
                z_id,
                net_sum,
                early_sum,
                visual_up,
                query_up,
                slots_qkv,
                reader_qkv,
                writer_qkv,
                column(norm_page),
                column(norm_visual_mlp),
                column(norm_slots),
                column(norm_reader),
                column(norm_query_mlp),
                own_page,
                late,
                *page_passed,
                *late_passed,
            ),
            rows_of,
        )

    window_passed, side_grad, most = stage(
        (place.send_terms, own_window),
        (right, side_grad),
        (run_finish, (net_sum, early_sum, own_page, page_passed, late, late_passed)),
    )
    visual_grad = roll_out(v_grad, side_grad, place, bands)
    grad_win, grad_win_out, grad_gw = simple(
        finish_windows,
        "finish_windows",
        (z_id, column(norm_window), window_qkv, own_window, *window_passed),
        [((r, 3 * D), f32), ((r, D), f32), ((r, 1), f32)],
    )
    grad_up, grad_down, grad_qup, grad_ro, grad_qdown, grad_reader, grad_writer, grad_wo, grad_sq, grad_so = most[:10]
    grad_gp, grad_gv, grad_gs, grad_gr, grad_gq = most[10:]

    def gain(x):
        return x.reshape(r)

    return (
        visual_out,
        query_out,
        visual_grad,
        query_grad,
        gain(grad_gw),
        grad_win,
        grad_win_out,
        gain(grad_gs),
        grad_sq,
        grad_so,
        gain(grad_gr),
        gain(grad_gp),
        grad_reader,
        grad_ro,
        grad_writer,
        grad_wo,
        gain(grad_gv),
        grad_up,
        grad_down.reshape(4 * r, D),
        gain(grad_gq),
        grad_qup,
        grad_qdown.reshape(4 * r, D),
    )


def solution(mesh):
    page = P("dp", "fsdp", None, None)
    slot = P("dp", "fsdp", None)
    gain = P(("dp", "fsdp"))
    matrix = P(("dp", "fsdp"), None)
    weights = (
        gain,
        matrix,
        matrix,
        gain,
        matrix,
        matrix,
        gain,
        gain,
        matrix,
        matrix,
        matrix,
        matrix,
        gain,
        matrix,
        matrix,
        gain,
        matrix,
        matrix,
    )
    return jax.shard_map(
        local,
        mesh=mesh,
        in_specs=(page, slot, P("dp"), P("dp", None)) + weights + (page, slot),
        out_specs=(page, slot, page, slot) + weights,
        check_vma=False,
    )
```
